32 devices in a mesh: dp: 8 (over z, y), tensor: 4 (over x, core).
Axes of the slice: x: 2, y: 2, z: 4, core: 2. Of those that a mesh axis runs over, the one named last changes fastest.
Arguments:
- hidden_in: bfloat16 [16384, 768], P(('dp', 'tensor')), may hold values from -6 to 6
- qkv_weight: float32 [3, 768, 768], P(None, 'dp', 'tensor'), may hold values from -0.21875 to 0.21875
- out_weight: float32 [768, 768], P('tensor', 'dp'), may hold values from -2.5 to 2.5
- up_weight: float32 [768, 3072], P('dp', 'tensor'), may hold values from -0.21875 to 0.21875
- up_bias: float32 [24, 128], P('tensor', 'dp'), may hold values from -3 to 3
- down_weight: float32 [3072, 768], P('tensor', 'dp'), may hold values from -0.109375 to 0.109375
- norm_params: float32 [4, 768], P(None, 'dp'), may hold values from -1 to 1.6, as said below
- cotangent: bfloat16 [16384, 768], P(('dp', 'tensor')), may hold values from -6 to 6
- head_swap: int32 [12], replicated, may hold values from 0 to 1
- slot_kind: int32 [16], P('dp'), may hold values from 0 to 1
Outputs:
- mixed: bfloat16 [16384, 768], P(('dp', 'tensor'))
- input_grad: float32 [16384, 768], P(('dp', 'tensor'))
- qkv_grad: float32 [3, 768, 768], P(None, 'dp', 'tensor')
- out_grad: float32 [768, 768], P('tensor', 'dp')
- up_grad: float32 [768, 3072], P('dp', 'tensor')
- up_bias_grad: float32 [24, 128], P('tensor', 'dp')
- down_grad: float32 [3072, 768], P('tensor', 'dp')
- norm_grad: float32 [4, 768], P('tensor', 'dp')
The draws below stay inside these ranges and needn't reach their ends.
Inputs may be any that keep to these rules, and one draw needn't show every extreme that they name: `head_swap`: 0 keeps every query block on its own key block; 1 swaps the two blocks of a sequence. `slot_kind`: 1 marks a slot with one sequence of 1024 tokens, 0 a slot with two of 512. `norm_params`: rows 0 and 2 are gains near 1, rows 1 and 3 biases.
All inputs are finite; a program needn't handle non-finite values.
Results may differ from the reference program's by a relative error of at most 0.018.
Values may be sent and summed in bfloat16 or wider, within the bound.
A program may use at most 128 MiB of HBM per device.

```python
import math
from functools import partial
import jax
import jax.numpy as jnp
from jax import lax

D = 768
H = 12
HD = 64
FF = 3072
LONG_LEN = 1024
TOKENS = 16384


def draw_norm_params(key, part):
    key = jax.random.fold_in(key, 5)
    base = jnp.clip(jax.random.normal(key, (4, D), jnp.float32), -3.0, 3.0)
    spread = jnp.array([0.15, 0.3, 0.15, 0.3], jnp.float32)[:, None]
    offset = jnp.array([1.0, 0.0, 1.0, 0.0], jnp.float32)[:, None]
    return offset + spread * base


def set_ends(result, own_key, low, high):
    extent = result.shape
    place = [jax.random.randint(jax.random.fold_in(own_key, axis), (), 0, extent[axis]) for axis in range(len(extent))]
    result = result.at[tuple(place)].set(low)
    longest = extent.index(max(extent))
    place[longest] = (place[longest] + 1) % extent[longest]
    return result.at[tuple(place)].set(high)


def block_scale(rng, shape, pieces, smallest, top_value):
    gain = 1.0
    for position, blocks in pieces:
        heights = jax.random.uniform(jax.random.fold_in(jax.random.fold_in(rng, 6), position), (blocks,), jnp.float32, smallest / len(pieces), top_value / len(pieces))
        gain = gain * jnp.repeat(jnp.exp(heights), shape[position] // blocks).reshape((-1,) + (1,) * (len(shape) - 1 - position))
    return gain


def bell_draw(key, dims, deviation, bound, shards=(), kind=jnp.bfloat16):
    loudness = block_scale(key, dims, shards, -0.22, 0.18) if shards else 1.0
    values = jax.random.normal(key, dims, jnp.float32) * deviation * loudness
    return jnp.minimum(jnp.maximum(values, -bound), bound).astype(kind)


def setup_inputs(seed: int = 0) -> dict:
    arg_keys = jax.random.split(jax.random.key(seed), 11)
    hidden_in = bell_draw(arg_keys[0], (TOKENS, D), 1.0, 6.0, ((0, 32),))
    qkv_weight = bell_draw(arg_keys[1], (3, D, D), D ** -0.5, 0.21875, ((1, 8), (2, 4)), jnp.float32)
    out_weight = bell_draw(arg_keys[2], (D, D), (max(D // 128, 1)) ** -0.5, 2.5, ((0, 4), (1, 8)), jnp.float32)
    up_weight = bell_draw(arg_keys[3], (D, FF), D ** -0.5, 0.21875, ((0, 8), (1, 4)), jnp.float32)
    up_bias = bell_draw(arg_keys[4], (FF // 128, 128), 0.5, 3.0, ((0, 4), (1, 8)), jnp.float32)
    down_weight = bell_draw(arg_keys[5], (FF, D), FF ** -0.5, 0.109375, ((0, 4), (1, 8)), jnp.float32)
    norm_params = draw_norm_params(jax.random.fold_in(arg_keys[10], 71), 0)
    cotangent = bell_draw(arg_keys[7], (TOKENS, D), 1.0, 6.0, ((0, 32),))
    head_swap = set_ends(jax.random.randint(arg_keys[8], (H,), 0, 2), jax.random.fold_in(arg_keys[8], 1), 0, 1).astype(jnp.int32)
    slot_kind = set_ends(jax.random.randint(arg_keys[9], (TOKENS // LONG_LEN,), 0, 2), jax.random.fold_in(arg_keys[9], 1), 0, 1).astype(jnp.int32)
    return {"hidden_in": hidden_in, "qkv_weight": qkv_weight, "out_weight": out_weight, "up_weight": up_weight, "up_bias": up_bias, "down_weight": down_weight, "norm_params": norm_params, "cotangent": cotangent, "head_swap": head_swap, "slot_kind": slot_kind}


EPSILON = 1e-05
NEGATIVE = -1e+30

@jax.custom_vjp
def low(v):
    return lax.optimization_barrier(v.astype(jnp.bfloat16)).astype(jnp.float32)

@jax.custom_vjp
def low_back(v):
    return v

def low_keep(v):
    return (low(v), None)

def low_pass(kept, grad):
    return (grad,)

def back_keep(v):
    return (v, None)

def back_low(kept, grad):
    return (low(grad),)
low.defvjp(low_keep, low_pass)
low_back.defvjp(back_keep, back_low)

def layer_norm(residual, scales, offset):
    center = residual - lax.optimization_barrier(jnp.mean(residual, axis=-1, keepdims=True))
    spread = lax.optimization_barrier(jnp.mean(center * center, axis=-1, keepdims=True))
    return center * lax.rsqrt(spread + EPSILON) * scales + offset

def attend(inputs, head_swap):
    queries, keys_in, values_in, slot_type = inputs
    half_len = LONG_LEN // 2
    quarter = half_len // 2
    shape_four = (2, half_len, H, HD)
    query_half = queries.reshape(shape_four)
    key_half = keys_in.reshape(shape_four)
    value_half = values_in.reshape(shape_four)
    flipped = (head_swap * slot_type == 1)[None, None, :, None]
    key_pick = jnp.where(flipped, key_half[::-1], key_half)
    value_pick = jnp.where(flipped, value_half[::-1], value_half)
    scores = jnp.einsum('jqhd,jkhd->jhqk', query_half, key_pick, precision=lax.Precision.HIGHEST)
    scores = low_back(scores * (1.0 / math.sqrt(HD)))
    blocks = jnp.arange(half_len, dtype=jnp.int32) // quarter
    matching = jnp.bitwise_xor(blocks[None, :, None], head_swap[:, None, None]) == blocks[None, None, :]
    allowed = jnp.logical_or(slot_type == 1, matching)[None]
    scores = jnp.where(allowed, scores, NEGATIVE)
    largest = lax.optimization_barrier(jnp.max(scores, axis=-1, keepdims=True))
    powers = jnp.exp(scores - largest)
    attention = low(powers / lax.optimization_barrier(jnp.sum(powers, axis=-1, keepdims=True)))
    context = jnp.einsum('jhqk,jkhd->jqhd', attention, value_pick, precision=lax.Precision.HIGHEST)
    return context.reshape(LONG_LEN, H * HD)

def reference(hidden_in, qkv_weight, out_weight, up_weight, up_bias, down_weight, norm_params, cotangent, head_swap, slot_kind):
    slot_count = TOKENS // LONG_LEN

    def forward(hidden, wqkv, wout, wup, bup, wdown, norms):
        norms_low = low(norms)
        proj = jnp.einsum('td,cde->cte', hidden, low(wqkv), precision=lax.Precision.HIGHEST)
        proj = low_back(low(proj))
        split_shape = (slot_count, LONG_LEN, H, HD)
        context = lax.map(jax.checkpoint(partial(attend, head_swap=head_swap)), (proj[0].reshape(split_shape), proj[1].reshape(split_shape), proj[2].reshape(split_shape), slot_kind))
        context = low_back(low(context.reshape(TOKENS, D)))
        attn_out = low_back(jnp.dot(context, low(wout), precision=lax.Precision.HIGHEST))
        normed1 = layer_norm(hidden + attn_out, norms_low[0], norms_low[1])
        ffn_in = low(normed1)
        pre = low_back(jnp.dot(ffn_in, low(wup), precision=lax.Precision.HIGHEST) + low(bup).reshape(FF))
        act = low(jax.nn.gelu(pre, approximate=False))
        ffn_out = low_back(jnp.dot(act, low(wdown), precision=lax.Precision.HIGHEST))
        return layer_norm(normed1 + ffn_out, norms_low[2], norms_low[3])
    hidden = hidden_in.astype(jnp.float32)
    mixed, pull_back = jax.vjp(forward, hidden, qkv_weight, out_weight, up_weight, up_bias, down_weight, norm_params)
    grads = pull_back(cotangent.astype(jnp.float32))
    return (mixed.astype(jnp.bfloat16), grads[0], grads[1], grads[2], grads[3], grads[4], grads[5], grads[6])
```

```python
from functools import partial
import math

import jax
import jax.numpy as jnp
from jax import lax
from jax.experimental import pallas as pl
from jax.experimental.pallas import tpu as pltpu
from jax.sharding import PartitionSpec as P

LONG_LEN = 1024
EPSILON = 1e-05
NEGATIVE = -1e30

BF = jnp.bfloat16
F32 = jnp.float32
NN = (((1,), (0,)), ((), ()))
NT = (((1,), (1,)), ((), ()))
TN = (((0,), (0,)), ((), ()))
PIECES = 6
SLOTS = 3
ROWS = 512
D = 768
HALF = 384


def dot(a, b, dims):
    return lax.dot_general(a, b, dims, preferred_element_type=F32)


def layer_kernel(
    hid, attn_in, up_in, down_in, misc_in, cot, swap, kind,
    mixed, igrad, g_attn, g_up, g_down, g_misc,
    W, AX, QKV, KVO, AT, CTX, XH, RS1, FI, ACT, GP, ACC, GF, DKVR,
    M, NB, V, VR, FX,
    SQ, SR, PB, RA, RB, RA2, RB2, RZ,
    zs, zr, xs, xr, ys, yr, hs, hr, ds_, dr, ms, mr, es, er,
    qs, qr, as_, ar, bs, br, a2s, a2r, b2s, b2r, rzs, rzr, vs, vr,
    c_sib, c_a, c_b, c_a2, c_b2, c_z,
):
    d = lax.axis_index("dp")
    t = lax.axis_index("tensor")
    z, y = d // 2, lax.rem(d, 2)
    x, c = t // 2, lax.rem(t, 2)
    ox, oy, oc = 1 - x, 1 - y, 1 - c

    def zk(k):
        hi, lo = z // 2, lax.rem(z, 2)
        kh, kl = k // 2, k % 2
        h2 = hi if kh == 0 else 1 - hi
        l2 = lo if kl == 0 else 1 - lo
        return 2 * h2 + l2

    zz = [zk(k) for k in range(4)]
    sib = (d, 2 * x + oc)
    xn = (d, 2 * ox + c)
    yn = (2 * z + oy, t)
    zn = [(2 * zz[k] + y, t) for k in range(4)]

    def rc(src, dst, s, r, dev):
        return pltpu.make_async_remote_copy(
            src_ref=src, dst_ref=dst, send_sem=s, recv_sem=r,
            device_id=dev, device_id_type=pl.DeviceIdType.MESH,
        )

    bar = pltpu.get_barrier_semaphore()
    for dev in (sib, xn, yn, zn[1], zn[2], zn[3]):
        pl.semaphore_signal(bar, inc=1, device_id=dev, device_id_type=pl.DeviceIdType.MESH)
    pl.semaphore_wait(bar, 6)

    def where(p, xx, core):
        if p < 2:
            return 2 * core + p, pl.multiple_of(xx * HALF, 128)
        if p < 4:
            return 4 + 2 * xx + core, (p - 2) * HALF
        return 8 + 2 * xx + core, (p - 4) * HALF

    def slab(p, xx, zi, yi, core=None):
        m, lane = where(p, xx, c if core is None else core)
        return W.at[m, zi, yi, :, :, pl.ds(lane, HALF)]

    def col(p, xx, yi, core=None):
        m, lane = where(p, xx, c if core is None else core)
        return W.at[m, :, yi, :, :, pl.ds(lane, HALF)]

    def hcol(p, xx, yi, half):
        m, lane = where(p, xx, c)
        return W.at[m, :, yi, half, :, pl.ds(lane, HALF)]

    def zcp(p, k, recv=False):
        s = slab(p, x, zz[k] if recv else z, y)
        return rc(s, s, zs.at[p, k - 1], zr.at[p, k - 1], zn[k])

    def xcp(p, k, recv=False):
        s = slab(p, ox if recv else x, zz[k], y)
        return rc(s, s, xs.at[p, k], xr.at[p, k], xn)

    def ycp(p, k, recv=False):
        s = slab(p, x, zz[k], oy if recv else y)
        return rc(s, s, ys.at[p, k], yr.at[p, k], yn)

    def acp(p, recv=False):
        s = hcol(p, ox, oy if recv else y, 0)
        return rc(s, s, hs.at[p, 0], hr.at[p, 0], yn)

    def bcp(p, recv=False):
        s = hcol(p, ox if recv else x, oy, 1)
        return rc(s, s, hs.at[p, 1], hr.at[p, 1], xn)

    groups = [(x, y), (ox, y), (x, oy), (ox, oy)]

    def dcp(p, g, recv=False):
        xx, yy = groups[g]
        s = col(p, xx, yy, oc if recv else c)
        return rc(s, s, ds_.at[p, g], dr.at[p, g], sib)

    def own(p):
        for k in (1, 2, 3):
            zcp(p, k).start()
        xcp(p, 0).start()
        ycp(p, 0).start()

    def zf(p):
        for k in (1, 2, 3):
            zcp(p, k, True).wait_recv()
            xcp(p, k).start()
            ycp(p, k).start()
        dcp(p, 0).start()

    def xf(p):
        for k in range(4):
            xcp(p, k, True).wait_recv()
        acp(p).start()
        dcp(p, 1).start()
        for k in range(4):
            ycp(p, k, True).wait_recv()
        bcp(p).start()
        dcp(p, 2).start()

    def fin(p):
        acp(p, True).wait_recv()
        bcp(p, True).wait_recv()
        dcp(p, 3).start()

    def ready(p):
        for g in range(4):
            dcp(p, g, True).wait_recv()

    def drain(p):
        for k in (1, 2, 3):
            zcp(p, k).wait_send()
        for k in range(4):
            xcp(p, k).wait_send()
            ycp(p, k).wait_send()
        acp(p).wait_send()
        bcp(p).wait_send()
        for g in range(4):
            dcp(p, g).wait_send()

    axc = rc(attn_in.at[pl.ds(2 * oc, 2)], AX, es.at[0], er.at[0], sib)
    axc.start()
    W[4 + t, z, y] = up_in[...].reshape(2, 48, D)
    W[8 + t, z, y] = down_in[...].reshape(2, 48, D)
    M[c, x, y, z] = misc_in[...]
    mz = [rc(M.at[c, x, y, z], M.at[c, x, y, z], ms.at[k - 1], mr.at[k - 1], zn[k]) for k in (1, 2, 3)]
    for cp in mz:
        cp.start()
    axc.wait_recv()
    own_lane = pl.ds(pl.multiple_of(x * HALF, 128), HALF)
    for i in range(2):
        W[2 * c + i, z, y, :, :, own_lane] = (attn_in[2 * c + i] + AX[i]).reshape(2, 48, HALF)
    for p in range(4):
        own(p)

    for cp in mz:
        cp.wait_recv()
    mx = rc(M.at[c, x, y], M.at[c, x, y], ms.at[3], mr.at[3], xn)
    mx.start()
    zf(0)
    zf(1)
    mx.wait_recv()
    my = rc(M.at[c, :, y], M.at[c, :, y], ms.at[4], mr.at[4], yn)
    my.start()
    own(4)
    own(5)
    zf(2)
    my.wait_recv()
    md = rc(M.at[c], M.at[c], ms.at[5], mr.at[5], sib)
    md.start()
    xf(0)
    xf(1)
    zf(3)
    md.wait_recv()

    si = lax.broadcasted_iota(jnp.int32, (128, D), 0)
    sj = lax.broadcasted_iota(jnp.int32, (128, D), 1)
    bpos = (si // 16) * 128 + si % 16
    norm_acc = jnp.zeros((32, D), F32)
    bias_acc = jnp.zeros((32, D), F32)
    for zi in range(4):
        for yi in range(2):
            dd = 2 * zi + yi
            stack = M[:, :, yi, zi].reshape(32, 128).astype(BF)
            e = jnp.where((si < 96) & (sj == si + dd * 96), 1.0, 0.0).astype(BF)
            f = jnp.where((si < 96) & (sj == bpos + dd * 16), 1.0, 0.0).astype(BF)
            norm_acc = norm_acc + dot(stack, e, NN)
            bias_acc = bias_acc + dot(stack, f, NN)
    NB[0] = norm_acc
    NB[1] = bias_acc

    fin(0)
    fin(1)
    xf(2)
    ready(0)
    ready(1)

    def mat(m):
        return W[m].reshape(D, D)

    for m in (1, 2, 0):
        QKV[m] = dot(hid[...], mat(m), NN).astype(BF)
        if m == 2:
            kvc = rc(QKV.at[pl.ds(1, 2)], KVO, es.at[1], er.at[1], sib)
            kvc.start()
    zf(4)
    fin(2)
    xf(3)
    kvc.wait_recv()

    kd = kind[x]
    lane = lax.broadcasted_iota(jnp.int32, (1, 128), 1)
    keylane = lax.broadcasted_iota(jnp.int32, (1, ROWS), 1)
    low_lane = lane < 64

    def flips(hp):
        fa = kd * swap[2 * hp]
        fb = kd * swap[2 * hp + 1]
        return jnp.where(low_lane, jnp.full((1, 128), fa, jnp.int32), jnp.full((1, 128), fb, jnp.int32)) == 1

    def pair_lanes(hp):
        return pl.ds(pl.multiple_of(hp * 128, 128), 128)

    def attn_fwd(hp):
        ls = pair_lanes(hp)
        fl = flips(hp)
        kk = jnp.where(fl, KVO[0, :, ls], QKV[1, :, ls])
        vv = jnp.where(fl, KVO[1, :, ls], QKV[2, :, ls])
        for rb in range(2):
            rows = slice(rb * 256, rb * 256 + 256)
            q = QKV[0, rows, ls] * jnp.asarray(0.125, BF)
            outs = []
            for e in range(2):
                sw = swap[2 * hp + e]
                qe = jnp.where(low_lane if e == 0 else ~low_lane, q, jnp.zeros_like(q))
                s = dot(qe, kk, NT)
                kb = jnp.where(keylane >= 256, 1, 0)
                same = jnp.where(kb == rb, 0, 1)
                seen = (same == jnp.full((1, ROWS), sw, jnp.int32)) | (jnp.full((1, ROWS), kd, jnp.int32) == 1)
                s = s + jnp.where(seen, 0.0, NEGATIVE)
                top = jnp.max(s, axis=1, keepdims=True)
                pw = jnp.exp(s - top)
                tot = jnp.sum(pw, axis=1, keepdims=True)
                a = (pw * (1.0 / tot)).astype(BF)
                AT[2 * hp + e, rows, :] = a
                outs.append(dot(a, vv, NN))
            CTX[rows, ls] = jnp.where(low_lane, outs[0], outs[1]).astype(BF)

    pl.loop(0, 2)(attn_fwd)
    zf(5)
    fin(3)
    pl.loop(2, 4)(attn_fwd)
    xf(4)
    pl.loop(4, 6)(attn_fwd)
    ready(2)
    ready(3)

    ACC[...] = dot(CTX[...], mat(3), NT)

    def ln_rows(i):
        return pl.ds(pl.multiple_of(i * 128, 128), 128)

    g1, b1 = NB[0, 0:1, :], NB[0, 1:2, :]
    g2, b2 = NB[0, 2:3, :], NB[0, 3:4, :]

    @pl.loop(0, 4)
    def _(i):
        rs = ln_rows(i)
        r = hid[rs, :].astype(F32) + ACC[rs, :]
        cen = r - jnp.mean(r, axis=1, keepdims=True)
        rstd = lax.rsqrt(jnp.mean(cen * cen, axis=1, keepdims=True) + EPSILON)
        xh = cen * rstd
        XH[rs, :] = xh
        RS1[rs, :] = rstd
        FI[rs, :] = (xh * g1 + b1).astype(BF)

    xf(5)
    fin(4)
    for tt in range(4):
        xx, cc = tt // 2, tt % 2
        row = (cc * 2 + xx) * 8 + 4
        pre = dot(FI[...], mat(4 + tt), NN) + NB[1, row : row + 1, :]
        cdf = 0.5 * (1.0 + lax.erf(pre * math.sqrt(0.5)))
        ACT[tt] = (pre * cdf).astype(BF)
        GP[tt] = (cdf + pre * (jnp.exp(-0.5 * pre * pre) * (1.0 / math.sqrt(2.0 * math.pi)))).astype(BF)

    fin(5)
    ready(4)

    def half_mat(m, h):
        return W[m, :, :, :, :, h * HALF : h * HALF + HALF].reshape(D, HALF)

    acc = dot(ACT[0, :, 0:HALF], half_mat(8, 0), NT)
    for tt in range(1, 4):
        acc = acc + dot(ACT[tt, :, 0:HALF], half_mat(8 + tt, 0), NT)
    ACC[...] = acc
    ready(5)
    acc = dot(ACT[0, :, HALF:D], half_mat(8, 1), NT)
    for tt in range(1, 4):
        acc = acc + dot(ACT[tt, :, HALF:D], half_mat(8 + tt, 1), NT)
    ACC[...] += acc

    V[...] = jnp.zeros_like(V)

    @pl.loop(0, 4)
    def _(i):
        rs = ln_rows(i)
        r = XH[rs, :] * g1 + b1 + ACC[rs, :]
        cen = r - jnp.mean(r, axis=1, keepdims=True)
        rstd = lax.rsqrt(jnp.mean(cen * cen, axis=1, keepdims=True) + EPSILON)
        n2 = cen * rstd
        mixed[rs, :] = (n2 * g2 + b2).astype(BF)
        co = cot[rs, :].astype(F32)
        e = co * g2
        gr = rstd * (e - jnp.mean(e, axis=1, keepdims=True) - n2 * jnp.mean(e * n2, axis=1, keepdims=True))
        ACC[rs, :] = gr
        GF[rs, :] = gr.astype(BF)
        V[2:3, :] += jnp.sum(co * n2, axis=0, keepdims=True)
        V[3:4, :] += jnp.sum(co, axis=0, keepdims=True)

    def b_sib(r):
        return rc(SQ.at[r % SLOTS], SR.at[r % SLOTS], qs.at[r], qr.at[r], sib)

    def b_a(r):
        q = r % SLOTS
        return rc(PB.at[q, ox, :, :, 0], RA.at[q], as_.at[r], ar.at[r], xn)

    def b_b(r):
        q = r % SLOTS
        return rc(PB.at[q, :, :, oy, 1], RB.at[q], bs.at[r], br.at[r], yn)

    def b_a2(r):
        q = r % SLOTS
        return rc(PB.at[q, x, :, oy, 0], RA2.at[q], a2s.at[r], a2r.at[r], yn)

    def b_b2(r):
        q = r % SLOTS
        return rc(PB.at[q, ox, :, y, 1], RB2.at[q], b2s.at[r], b2r.at[r], xn)

    def b_z(r, k):
        q = r % SLOTS
        return rc(PB.at[q, x, zz[k], y], RZ.at[q, k - 1], rzs.at[r, k - 1], rzr.at[r, k - 1], zn[k])

    def credit(sem, dev, r):
        if r + SLOTS < PIECES:
            pl.semaphore_signal(sem, inc=1, device_id=dev, device_id_type=pl.DeviceIdType.MESH)

    def need(sem, r):
        if r >= SLOTS:
            pl.semaphore_wait(sem, 1)

    def part(r, xx, core):
        if r < 4:
            src = ACT if r < 2 else GP
            lhs = GF if r < 2 else FI
            h = r % 2
            return dot(lhs[...], src[2 * xx + core, :, h * HALF : h * HALF + HALF], TN)
        raise ValueError

    def part_attn(m, xx):
        if m < 3:
            return dot(hid[...], ACT[m, :, xx * HALF : xx * HALF + HALF], TN)
        return dot(GF[...], CTX[:, xx * HALF : xx * HALF + HALF], TN)

    def gen_sib(r):
        q = r % SLOTS
        if r < 4:
            for xx in range(2):
                SQ[q, xx] = part(r, xx, oc).astype(BF).reshape(4, 2, 2, 48, HALF)
        else:
            for core in range(2):
                @pl.when(oc == core)
                def _():
                    for xx in range(2):
                        SQ[q, xx] = part_attn(2 * core + r - 4, xx).astype(BF).reshape(4, 2, 2, 48, HALF)
        need(c_sib, r)
        b_sib(r).start()

    def gen_own(r):
        q = r % SLOTS
        b_sib(r).wait_recv()
        if r < 4:
            for xx in range(2):
                v = part(r, xx, c).reshape(4, 2, 2, 48, HALF) + SR[q, xx].astype(F32)
                PB[q, xx] = v.astype(BF)
        else:
            for core in range(2):
                @pl.when(c == core)
                def _():
                    for xx in range(2):
                        v = part_attn(2 * core + r - 4, xx).reshape(4, 2, 2, 48, HALF) + SR[q, xx].astype(F32)
                        PB[q, xx] = v.astype(BF)
        credit(c_sib, sib, r)
        need(c_a, r)
        b_a(r).start()
        need(c_b, r)
        b_b(r).start()

    def add(dst, src):
        return (dst.astype(F32) + src.astype(F32)).astype(BF)

    def st1(r):
        q = r % SLOTS
        b_a(r).wait_recv()
        PB[q, x, :, :, 0] = add(PB[q, x, :, :, 0], RA[q])
        credit(c_a, xn, r)
        need(c_a2, r)
        b_a2(r).start()
        b_b(r).wait_recv()
        PB[q, :, :, y, 1] = add(PB[q, :, :, y, 1], RB[q])
        credit(c_b, yn, r)
        need(c_b2, r)
        b_b2(r).start()

    def st2(r):
        q = r % SLOTS
        b_a2(r).wait_recv()
        PB[q, x, :, y, 0] = add(PB[q, x, :, y, 0], RA2[q])
        credit(c_a2, yn, r)
        b_b2(r).wait_recv()
        PB[q, x, :, y, 1] = add(PB[q, x, :, y, 1], RB2[q])
        credit(c_b2, xn, r)
        for k in (1, 2, 3):
            need(c_z.at[k - 1], r)
            b_z(r, k).start()

    def st3(r):
        q = r % SLOTS
        tot = PB[q, x, z, y].astype(F32)
        for k in (1, 2, 3):
            b_z(r, k).wait_recv()
            tot = tot + RZ[q, k - 1].astype(F32)
            credit(c_z.at[k - 1], zn[k], r)
        tot = tot.reshape(96, HALF)
        h = r % 2
        if r < 2:
            g_down[:, h * HALF : h * HALF + HALF] = tot
        elif r < 4:
            g_up[:, h * HALF : h * HALF + HALF] = tot
        else:
            FX[c, h] = tot
        b_sib(r).wait_send()
        b_a(r).wait_send()
        b_b(r).wait_send()
        b_a2(r).wait_send()
        b_b2(r).wait_send()
        for k in (1, 2, 3):
            b_z(r, k).wait_send()

    gen_sib(0)
    gen_sib(1)
    gen_own(0)
    gen_own(1)

    for tt in range(4):
        ga = dot(GF[...], mat(8 + tt), NN)
        gp = (ga * GP[tt].astype(F32)).astype(BF)
        GP[tt] = gp
        V[4 + tt : 5 + tt, :] = jnp.sum(gp.astype(F32), axis=0, keepdims=True)
        if tt == 2:
            st1(0)

    gen_sib(2)
    gen_own(2)
    st1(1)
    st2(0)

    acc = dot(GP[0], mat(4), NT)
    for tt in range(1, 4):
        acc = acc + dot(GP[tt], mat(4 + tt), NT)
    ACC[...] += acc

    @pl.loop(0, 4)
    def _(i):
        rs = ln_rows(i)
        gn = ACC[rs, :]
        xh = XH[rs, :]
        e = gn * g1
        gr = RS1[rs, :] * (e - jnp.mean(e, axis=1, keepdims=True) - xh * jnp.mean(e * xh, axis=1, keepdims=True))
        igrad[rs, :] = gr
        GF[rs, :] = gr.astype(BF)
        V[0:1, :] += jnp.sum(gn * xh, axis=0, keepdims=True)
        V[1:2, :] += jnp.sum(gn, axis=0, keepdims=True)

    vc = [
        rc(V, VR.at[0], vs.at[0], vr.at[0], sib),
        rc(V, VR.at[1], vs.at[1], vr.at[1], xn),
        rc(V, VR.at[2], vs.at[2], vr.at[2], yn),
    ] + [rc(V, VR.at[2 + k], vs.at[2 + k], vr.at[2 + k], zn[k]) for k in (1, 2, 3)]

    def v_step(i):
        vc[i].wait()
        V[...] += VR[i]

    vc[0].start()
    st3(0)
    gen_sib(3)
    gen_own(3)
    st2(1)
    st1(2)
    v_step(0)
    vc[1].start()

    FI[...] = dot(GF[...], mat(3), NN).astype(BF)
    v_step(1)
    vc[2].start()

    def attn_bwd(hp):
        ls = pair_lanes(hp)
        fl = flips(hp)
        kk = jnp.where(fl, KVO[0, :, ls], QKV[1, :, ls])
        vv = jnp.where(fl, KVO[1, :, ls], QKV[2, :, ls])
        q = QKV[0, :, ls]
        do = FI[:, ls]
        dvs, dqs, dks = [], [], []
        for e in range(2):
            a = AT[2 * hp + e]
            dvs.append(dot(a, do, TN))
            de = jnp.where(low_lane if e == 0 else ~low_lane, do, jnp.zeros_like(do))
            dp = dot(de, vv, NT)
            af = a.astype(F32)
            w = af * dp
            gs = (w - af * jnp.sum(w, axis=1, keepdims=True)).astype(BF)
            dqs.append(dot(gs, kk, NN))
            dks.append(dot(gs, q, TN))
        ACT[0, :, ls] = (jnp.where(low_lane, dqs[0], dqs[1]) * 0.125).astype(BF)
        GP[0, :, ls] = (jnp.where(low_lane, dks[0], dks[1]) * 0.125).astype(BF)
        GP[1, :, ls] = jnp.where(low_lane, dvs[0], dvs[1]).astype(BF)

    pl.loop(0, 2)(attn_bwd)
    st2(2)
    st3(1)
    v_step(2)
    for k in (1, 2, 3):
        vc[2 + k].start()
    pl.loop(2, 4)(attn_bwd)
    st1(3)
    pl.loop(4, 6)(attn_bwd)
    dkvc = rc(GP.at[pl.ds(0, 2)], DKVR, es.at[2], er.at[2], sib)
    dkvc.start()
    for k in (1, 2, 3):
        vc[2 + k].wait()
    g_misc[...] = V[...] + VR[3] + VR[4] + VR[5]
    st3(2)
    st2(3)
    dkvc.wait()

    def pick(hp):
        ls = pair_lanes(hp)
        fl = flips(hp)
        ACT[1, :, ls] = jnp.where(fl, DKVR[0, :, ls], GP[0, :, ls])
        ACT[2, :, ls] = jnp.where(fl, DKVR[1, :, ls], GP[1, :, ls])

    pl.loop(0, 6)(pick)

    gen_sib(4)
    gen_own(4)
    st3(3)
    gen_sib(5)
    gen_own(5)
    acc = dot(ACT[0], mat(0), NT)
    for m in (1, 2):
        acc = acc + dot(ACT[m], mat(m), NT)
    igrad[...] += acc
    st1(4)
    st1(5)
    st2(4)
    st2(5)
    st3(4)
    st3(5)
    fx = rc(FX.at[c], FX.at[c], es.at[3], er.at[3], sib)
    fx.start()
    for p in range(PIECES):
        drain(p)
    for cp in mz:
        cp.wait_send()
    mx.wait_send()
    my.wait_send()
    md.wait_send()
    axc.wait_send()
    kvc.wait_send()
    fx.wait()
    g_attn[...] = FX[...].reshape(4, 96, HALF)


def scratch():
    vm = pltpu.VMEM
    dma = lambda *s: pltpu.SemaphoreType.DMA(s)
    n = PIECES
    return [
        vm((12, 4, 2, 2, 48, D), BF), vm((2, 96, HALF), BF), vm((3, ROWS, D), BF), vm((2, ROWS, D), BF),
        vm((12, ROWS, ROWS), BF), vm((ROWS, D), BF), vm((ROWS, D), F32), vm((ROWS, 1), F32), vm((ROWS, D), BF),
        vm((4, ROWS, D), BF), vm((4, ROWS, D), BF), vm((ROWS, D), F32), vm((ROWS, D), BF), vm((2, ROWS, D), BF),
        vm((2, 2, 2, 4, 8, 128), F32), vm((2, 32, D), F32), vm((8, D), F32), vm((6, 8, D), F32), vm((2, 2, 96, HALF), F32),
        vm((SLOTS, 2, 4, 2, 2, 48, HALF), BF), vm((SLOTS, 2, 4, 2, 2, 48, HALF), BF), vm((SLOTS, 2, 4, 2, 2, 48, HALF), BF),
        vm((SLOTS, 4, 2, 48, HALF), BF), vm((SLOTS, 2, 4, 48, HALF), BF), vm((SLOTS, 4, 48, HALF), BF),
        vm((SLOTS, 4, 48, HALF), BF), vm((SLOTS, 3, 2, 48, HALF), BF),
        dma(n, 3), dma(n, 3), dma(n, 4), dma(n, 4), dma(n, 4), dma(n, 4), dma(n, 2), dma(n, 2), dma(n, 4), dma(n, 4),
        dma(6), dma(6), dma(4), dma(4),
        dma(n), dma(n), dma(n), dma(n), dma(n), dma(n), dma(n), dma(n), dma(n), dma(n), dma(n, 3), dma(n, 3), dma(6), dma(6),
        pltpu.SemaphoreType.REGULAR, pltpu.SemaphoreType.REGULAR, pltpu.SemaphoreType.REGULAR,
        pltpu.SemaphoreType.REGULAR, pltpu.SemaphoreType.REGULAR, pltpu.SemaphoreType.REGULAR((3,)),
    ]


def whole_layer(
    hidden_in, qkv_weight, out_weight, up_weight, up_bias, down_weight, norm_params, cotangent, head_swap, slot_kind
):
    core = lax.rem(lax.axis_index("tensor"), 2)
    dp = lax.axis_index("dp")
    tensor = lax.axis_index("tensor")
    shard = jnp.concatenate([qkv_weight, out_weight.T[None]]).astype(BF)
    blank = jnp.zeros_like(shard)
    attn_in = jnp.where(core == 0, jnp.concatenate([shard, blank], 2), jnp.concatenate([blank, shard], 2))
    small = jnp.concatenate([norm_params, up_bias.reshape(1, 96), jnp.zeros((3, 96), F32)])
    small = jnp.pad(small, ((0, 0), (0, 32))).astype(BF).astype(F32)
    vmem = pl.BlockSpec(memory_space=pltpu.VMEM)
    smem = pl.BlockSpec(memory_space=pltpu.SMEM)
    sds = jax.ShapeDtypeStruct
    mixed, igrad, ga, gu, gd, gm = pl.pallas_call(
        layer_kernel,
        out_shape=(
            sds((ROWS, D), BF), sds((ROWS, D), F32), sds((4, 96, HALF), F32),
            sds((96, D), F32), sds((96, D), F32), sds((8, D), F32),
        ),
        in_specs=[vmem] * 6 + [smem] * 2,
        out_specs=(vmem,) * 6,
        scratch_shapes=scratch(),
        compiler_params=pltpu.CompilerParams(
            collective_id=0, has_side_effects=True, vmem_limit_bytes=63 * 2**20
        ),
        name="layer",
    )(
        hidden_in, attn_in, up_weight.astype(BF), down_weight.T.astype(BF), small, cotangent, head_swap, slot_kind
    )
    mine = lax.dynamic_slice_in_dim(ga, core * 192, 192, axis=2)
    bias = lax.dynamic_slice_in_dim(gm, 4 + tensor, 1, 0).reshape(6, 8, 16)
    bias = lax.dynamic_slice_in_dim(bias, dp, 1, 1).reshape(6, 16)
    norm = lax.dynamic_slice(gm, (tensor, dp * 96), (1, 96))
    return (mixed, igrad, mine[:3], mine[3].T, gu, bias, gd.T, norm)


def norm_rows(residual, scales, offset):
    center = residual - jnp.mean(residual, axis=-1, keepdims=True)
    spread = jnp.mean(center * center, axis=-1, keepdims=True)
    return center * lax.rsqrt(spread + EPSILON) * scales + offset


def smooth_gate(values):
    return jax.nn.gelu(values, approximate=False)


def arrange(queries, keys_in, values_in, slot_type, local_swaps):
    slot_len, head_count, head_size = queries.shape
    half_len = slot_len // 2
    quarter = half_len // 2
    shape_four = (2, half_len, head_count, head_size)
    query_half = queries.reshape(shape_four)
    key_half = keys_in.reshape(shape_four)
    value_half = values_in.reshape(shape_four)
    flipped = (local_swaps * slot_type == 1)[None, None, :, None]
    key_pick = jnp.where(flipped, key_half[::-1], key_half)
    value_pick = jnp.where(flipped, value_half[::-1], value_half)
    blocks = jnp.arange(half_len, dtype=jnp.int32) // quarter
    matching = (
        jnp.bitwise_xor(blocks[None, :, None], local_swaps[:, None, None]) == blocks[None, None, :]
    )
    allowed = jnp.logical_or(slot_type == 1, matching)
    return (query_half, key_pick, value_pick, allowed, flipped)


def masked_scores(query_half, key_pick, allowed):
    scale = 1.0 / math.sqrt(query_half.shape[-1])
    scores = (
        jnp.einsum("jqhd,jkhd->jhqk", query_half, key_pick, preferred_element_type=jnp.float32)
        * scale
    )
    return jnp.where(allowed[None], scores, NEGATIVE)


def slot_forward(inputs, local_swaps):
    queries, keys_in, values_in, slot_type = inputs
    query_half, key_pick, value_pick, allowed, flipped = arrange(
        queries, keys_in, values_in, slot_type, local_swaps
    )
    scores = masked_scores(query_half, key_pick, allowed)
    largest = jnp.max(scores, axis=-1, keepdims=True)
    powers = jnp.exp(scores - largest)
    totals = jnp.sum(powers, axis=-1, keepdims=True)
    attention = (powers / totals).astype(jnp.bfloat16)
    context = jnp.einsum(
        "jhqk,jkhd->jqhd", attention, value_pick, preferred_element_type=jnp.float32
    )
    return (context.astype(jnp.bfloat16).reshape(queries.shape[0], -1), largest + jnp.log(totals))


def slot_backward(inputs, local_swaps):
    queries, keys_in, values_in, slot_type, log_totals, grad_out = inputs
    slot_len, head_count, head_size = queries.shape
    scale = 1.0 / math.sqrt(head_size)
    query_half, key_pick, value_pick, allowed, flipped = arrange(
        queries, keys_in, values_in, slot_type, local_swaps
    )
    attention = jnp.exp(masked_scores(query_half, key_pick, allowed) - log_totals)
    grad_half = grad_out.reshape(query_half.shape)
    grad_vpick = jnp.einsum(
        "jhqk,jqhd->jkhd",
        attention.astype(jnp.bfloat16),
        grad_half,
        preferred_element_type=jnp.float32,
    ).astype(jnp.bfloat16)
    grad_attention = jnp.einsum(
        "jqhd,jkhd->jhqk", grad_half, value_pick, preferred_element_type=jnp.float32
    )
    row_dots = jnp.sum(attention * grad_attention, axis=-1, keepdims=True)
    grad_scores = (attention * (grad_attention - row_dots)).astype(jnp.bfloat16)
    grad_query = (
        jnp.einsum("jhqk,jkhd->jqhd", grad_scores, key_pick, preferred_element_type=jnp.float32)
        * scale
    ).astype(jnp.bfloat16)
    grad_kpick = (
        jnp.einsum("jhqk,jqhd->jkhd", grad_scores, query_half, preferred_element_type=jnp.float32)
        * scale
    ).astype(jnp.bfloat16)
    grad_key = jnp.where(flipped, grad_kpick[::-1], grad_kpick)
    grad_value = jnp.where(flipped, grad_vpick[::-1], grad_vpick)
    return (
        grad_query.reshape(slot_len, -1),
        grad_key.reshape(slot_len, -1),
        grad_value.reshape(slot_len, -1),
    )


def per_device(
    hidden_in,
    qkv_weight,
    out_weight,
    up_weight,
    up_bias,
    down_weight,
    norm_params,
    cotangent,
    head_swap,
    slot_kind,
):
    tensor_count = lax.axis_size("tensor")
    tensor_rank = lax.axis_index("tensor")
    heads_here = head_swap.shape[0] // tensor_count
    local_swaps = lax.dynamic_slice_in_dim(head_swap, tensor_rank * heads_here, heads_here)
    qkv_low = qkv_weight.astype(jnp.bfloat16)
    out_low = out_weight.astype(jnp.bfloat16)
    norm_low = norm_params.astype(jnp.bfloat16)
    up_low = up_weight.astype(jnp.bfloat16)
    bias_low = up_bias.astype(jnp.bfloat16)
    down_low = down_weight.astype(jnp.bfloat16)
    qkv_full, out_full, norm_full = (
        lax.all_gather(qkv_low, "dp", axis=1, tiled=True),
        lax.all_gather(out_low, "dp", axis=1, tiled=True),
        lax.all_gather(norm_low, "dp", axis=1, tiled=True),
    )
    norm_gain = norm_full.astype(jnp.float32)
    full_in = lax.all_gather(hidden_in, "tensor", axis=0, tiled=True)
    group_rows = full_in.shape[0]
    local_width = qkv_full.shape[2]
    head_size = local_width // heads_here
    slot_count = group_rows // LONG_LEN

    def by_slot(rows):
        return rows.reshape(slot_count, LONG_LEN, heads_here, head_size)

    projected = jnp.einsum(
        "td,cde->cte", full_in, qkv_full, preferred_element_type=jnp.float32
    ).astype(jnp.bfloat16)
    context, log_totals = lax.map(
        partial(slot_forward, local_swaps=local_swaps),
        (by_slot(projected[0]), by_slot(projected[1]), by_slot(projected[2]), slot_kind),
    )
    context = context.reshape(group_rows, local_width)
    rows = context
    attn_share = lax.psum_scatter(
        jnp.dot(rows, out_full, preferred_element_type=jnp.float32).astype(jnp.bfloat16),
        "tensor",
        scatter_dimension=0,
        tiled=True,
    ).astype(jnp.float32)
    resid_one = hidden_in.astype(jnp.float32) + attn_share
    normed_one, norm_one_back = jax.vjp(norm_rows, resid_one, norm_gain[0], norm_gain[1])
    up_full, bias_full, down_full = (
        lax.all_gather(up_low, "dp", axis=0, tiled=True),
        lax.all_gather(bias_low, "dp", axis=1, tiled=True),
        lax.all_gather(down_low, "dp", axis=1, tiled=True),
    )
    ffn_in = lax.all_gather(normed_one.astype(jnp.bfloat16), "tensor", axis=0, tiled=True)
    pre = jnp.dot(ffn_in, up_full, preferred_element_type=jnp.float32) + bias_full.reshape(
        -1
    ).astype(jnp.float32)
    act_value, gate_back = jax.vjp(smooth_gate, pre)
    act = act_value.astype(jnp.bfloat16)
    rows = act
    ffn_share = lax.psum_scatter(
        jnp.dot(rows, down_full, preferred_element_type=jnp.float32).astype(jnp.bfloat16),
        "tensor",
        scatter_dimension=0,
        tiled=True,
    ).astype(jnp.float32)
    normed_two, norm_two_back = jax.vjp(
        norm_rows, normed_one + ffn_share, norm_gain[2], norm_gain[3]
    )
    mixed = normed_two.astype(jnp.bfloat16)
    grad_resid_two, grad_gain_two, grad_bias_two = norm_two_back(cotangent.astype(jnp.float32))
    grad_ffn = lax.all_gather(grad_resid_two.astype(jnp.bfloat16), "tensor", axis=0, tiled=True)
    grad_down = jnp.einsum("tf,td->fd", act, grad_ffn, preferred_element_type=jnp.float32)
    grad_act = jnp.einsum("td,fd->tf", grad_ffn, down_full, preferred_element_type=jnp.float32)
    grad_pre = gate_back(grad_act)[0].astype(jnp.bfloat16)
    grad_up = jnp.einsum("td,tf->df", ffn_in, grad_pre, preferred_element_type=jnp.float32)
    grad_bias = jnp.sum(grad_pre.astype(jnp.float32), axis=0).reshape(bias_full.shape)
    rows = grad_pre
    grad_normed_one = grad_resid_two + lax.psum_scatter(
        jnp.einsum("tf,df->td", rows, up_full, preferred_element_type=jnp.float32).astype(
            jnp.bfloat16
        ),
        "tensor",
        scatter_dimension=0,
        tiled=True,
    ).astype(jnp.float32)
    grad_resid_one, grad_gain_one, grad_bias_one = norm_one_back(grad_normed_one)
    grad_attn = lax.all_gather(grad_resid_one.astype(jnp.bfloat16), "tensor", axis=0, tiled=True)
    grad_out = jnp.einsum("tw,td->wd", context, grad_attn, preferred_element_type=jnp.float32)
    grad_context = jnp.einsum(
        "td,wd->tw", grad_attn, out_full, preferred_element_type=jnp.float32
    ).astype(jnp.bfloat16)
    grad_query, grad_key, grad_value = lax.map(
        partial(slot_backward, local_swaps=local_swaps),
        (
            by_slot(projected[0]),
            by_slot(projected[1]),
            by_slot(projected[2]),
            slot_kind,
            log_totals,
            grad_context.reshape(slot_count, LONG_LEN, local_width),
        ),
    )
    grad_proj = jnp.stack([grad_query, grad_key, grad_value]).reshape(3, group_rows, local_width)
    grad_qkv = jnp.einsum("td,cte->cde", full_in, grad_proj, preferred_element_type=jnp.float32)
    grad_in_part = jnp.einsum(
        "cte,cde->td", grad_proj, qkv_full, preferred_element_type=jnp.float32
    )
    norm_part = jnp.stack([grad_gain_one, grad_bias_one, grad_gain_two, grad_bias_two])
    grad_in_share, norm_row = (
        lax.psum_scatter(
            grad_in_part.astype(jnp.bfloat16), "tensor", scatter_dimension=0, tiled=True
        ).astype(jnp.float32),
        lax.psum_scatter(
            norm_part.astype(jnp.bfloat16), "tensor", scatter_dimension=0, tiled=True
        ).astype(jnp.float32),
    )
    input_grad = grad_resid_one + grad_in_share
    qkv_grad, out_grad, up_grad, up_bias_grad, down_grad, norm_grad = (
        lax.psum_scatter(grad_qkv, "dp", scatter_dimension=1, tiled=True),
        lax.psum_scatter(grad_out, "dp", scatter_dimension=1, tiled=True),
        lax.psum_scatter(grad_up, "dp", scatter_dimension=0, tiled=True),
        lax.psum_scatter(grad_bias, "dp", scatter_dimension=1, tiled=True),
        lax.psum_scatter(grad_down, "dp", scatter_dimension=1, tiled=True),
        lax.psum_scatter(norm_row, "dp", scatter_dimension=1, tiled=True),
    )
    return (mixed, input_grad, qkv_grad, out_grad, up_grad, up_bias_grad, down_grad, norm_grad)


def solution(mesh):
    placed = (
        P(("dp", "tensor"), None),
        P(None, "dp", "tensor"),
        P("tensor", "dp"),
        P("dp", "tensor"),
        P("tensor", "dp"),
        P("tensor", "dp"),
        P(None, "dp"),
        P(("dp", "tensor"), None),
        P(),
        P("dp"),
    )
    planned = mesh.shape["dp"] == 8 and mesh.shape["tensor"] == 4
    return jax.shard_map(
        whole_layer if planned else per_device,
        mesh=mesh,
        in_specs=placed,
        out_specs=(
            P(("dp", "tensor"), None),
            P(("dp", "tensor"), None),
            P(None, "dp", "tensor"),
            P("tensor", "dp"),
            P("dp", "tensor"),
            P("tensor", "dp"),
            P("tensor", "dp"),
            P("tensor", "dp"),
        ),
        check_vma=False,
    )
```

```python
from functools import partial
import math

import jax
import jax.numpy as jnp
from jax import lax
from jax.experimental import pallas as pl
from jax.experimental.pallas import tpu as pltpu
from jax.sharding import PartitionSpec as P

LONG_LEN = 1024
EPSILON = 1e-05
NEGATIVE = -1e30

BF = jnp.bfloat16
F32 = jnp.float32
NN = (((1,), (0,)), ((), ()))
NT = (((1,), (1,)), ((), ()))
TN = (((0,), (0,)), ((), ()))
PIECES = 6
SLOTS = 3
ROWS = 512
D = 768
HALF = 384


def dot(a, b, dims):
    return lax.dot_general(a, b, dims, preferred_element_type=F32)


def layer_kernel(
    hid, qkv_w, out_w, up_w, up_b, down_w, norm_p, cot, swap, kind,
    mixed, igrad, g_attn, g_up, g_down, g_misc,
    W, SH, AX, QKV, KVO, AT, CTX, XH, RS1, FI, ACT, GP, ACC, GF, DKVR,
    M, NB, V, VR, FX,
    SQ, SR, PB, RA, RB, RA2, RB2, RO, RZ,
    zs, zr, xs, xr, ys, yr, hs, hr, ds_, dr, ms, mr, es, er,
    qs, qr, as_, ar, bs, br, a2s, a2r, b2s, b2r, rzs, rzr, vs, vr,
    c_sib, c_a, c_b, c_a2, c_b2,
):
    d = lax.axis_index("dp")
    t = lax.axis_index("tensor")
    z, y = d // 2, lax.rem(d, 2)
    x, c = t // 2, lax.rem(t, 2)
    ox, oy, oc = 1 - x, 1 - y, 1 - c

    def zk(k):
        hi, lo = z // 2, lax.rem(z, 2)
        kh, kl = k // 2, k % 2
        h2 = hi if kh == 0 else 1 - hi
        l2 = lo if kl == 0 else 1 - lo
        return 2 * h2 + l2

    zz = [zk(k) for k in range(4)]
    sib = (d, 2 * x + oc)
    xn = (d, 2 * ox + c)
    yn = (2 * z + oy, t)
    zn = [(2 * zz[k] + y, t) for k in range(4)]

    def rc(src, dst, s, r, dev):
        return pltpu.make_async_remote_copy(
            src_ref=src, dst_ref=dst, send_sem=s, recv_sem=r,
            device_id=dev, device_id_type=pl.DeviceIdType.MESH,
        )

    bar = pltpu.get_barrier_semaphore()
    for dev in (sib, xn, yn, zn[1], zn[2], zn[3]):
        pl.semaphore_signal(bar, inc=1, device_id=dev, device_id_type=pl.DeviceIdType.MESH)
    pl.semaphore_wait(bar, 6)

    def where(p, xx, core):
        if p < 2:
            return 2 * core + p, pl.multiple_of(xx * HALF, 128)
        if p < 4:
            return 4 + 2 * xx + core, (p - 2) * HALF
        return 8 + 2 * xx + core, (p - 4) * HALF

    def slab(p, xx, zi, yi, core=None):
        m, lane = where(p, xx, c if core is None else core)
        return W.at[m, zi, yi, :, :, pl.ds(lane, HALF)]

    def col(p, xx, yi, core=None):
        m, lane = where(p, xx, c if core is None else core)
        return W.at[m, :, yi, :, :, pl.ds(lane, HALF)]

    def hcol(p, xx, yi, half):
        m, lane = where(p, xx, c)
        return W.at[m, :, yi, half, :, pl.ds(lane, HALF)]

    def zcp(p, k, recv=False):
        s = slab(p, x, zz[k] if recv else z, y)
        return rc(s, s, zs.at[p, k - 1], zr.at[p, k - 1], zn[k])

    def xcp(p, k, recv=False):
        s = slab(p, ox if recv else x, zz[k], y)
        return rc(s, s, xs.at[p, k], xr.at[p, k], xn)

    def ycp(p, k, recv=False):
        s = slab(p, x, zz[k], oy if recv else y)
        return rc(s, s, ys.at[p, k], yr.at[p, k], yn)

    def acp(p, recv=False):
        s = hcol(p, ox, oy if recv else y, 0)
        return rc(s, s, hs.at[p, 0], hr.at[p, 0], yn)

    def bcp(p, recv=False):
        s = hcol(p, ox if recv else x, oy, 1)
        return rc(s, s, hs.at[p, 1], hr.at[p, 1], xn)

    groups = [(x, y), (ox, y), (x, oy), (ox, oy)]

    def dcp(p, g, recv=False):
        xx, yy = groups[g]
        s = col(p, xx, yy, oc if recv else c)
        return rc(s, s, ds_.at[p, g], dr.at[p, g], sib)

    def own(p):
        for k in (2, 3, 1):
            zcp(p, k).start()
        xcp(p, 0).start()
        ycp(p, 0).start()

    def zf(p):
        for k in (1, 2, 3):
            zcp(p, k, True).wait_recv()
            xcp(p, k).start()
            ycp(p, k).start()
        dcp(p, 0).start()

    def xf(p):
        for k in range(4):
            xcp(p, k, True).wait_recv()
        acp(p).start()
        dcp(p, 1).start()
        for k in range(4):
            ycp(p, k, True).wait_recv()
        bcp(p).start()
        dcp(p, 2).start()

    def fin(p):
        acp(p, True).wait_recv()
        bcp(p, True).wait_recv()
        dcp(p, 3).start()

    def ready(p):
        for g in range(4):
            dcp(p, g, True).wait_recv()

    def drain(p):
        for k in (1, 2, 3):
            zcp(p, k).wait_send()
        for k in range(4):
            xcp(p, k).wait_send()
            ycp(p, k).wait_send()
        acp(p).wait_send()
        bcp(p).wait_send()
        for g in range(4):
            dcp(p, g).wait_send()

    SH[0:3, :, 0:192] = qkv_w[...].astype(BF)
    SH[3, :, 0:192] = out_w[...].astype(BF).T
    axc = rc(SH.at[pl.ds(2 * oc, 2)], AX, es.at[0], er.at[0], sib)
    axc.start()
    M[c, x, y, z, 0, 0:4, 0:96] = norm_p[...].astype(BF).astype(F32)
    M[c, x, y, z, 1, 0:6, 0:16] = up_b[...].astype(BF).astype(F32)
    mz = [rc(M.at[c, x, y, z], M.at[c, x, y, z], ms.at[k - 1], mr.at[k - 1], zn[k]) for k in (1, 2, 3)]
    for cp in mz:
        cp.start()
    W[4 + t, z, y] = up_w[...].astype(BF).reshape(2, 48, D)
    W[8 + t, z, y] = down_w[...].astype(BF).reshape(2, 48, D)
    axc.wait_recv()
    own_lane = pl.ds(pl.multiple_of(x * HALF, 128), HALF)
    first = jnp.full((96, 192), c, jnp.int32) == 0
    for i in range(2):
        mine, theirs = SH[2 * c + i, :, 0:192], AX[i, :, 0:192]
        both = jnp.concatenate([jnp.where(first, mine, theirs), jnp.where(first, theirs, mine)], axis=1)
        W[2 * c + i, z, y, :, :, own_lane] = both.reshape(2, 48, HALF)
    for p in range(PIECES):
        own(p)

    for cp in mz:
        cp.wait_recv()
    mx = rc(M.at[c, x, y], M.at[c, x, y], ms.at[3], mr.at[3], xn)
    mx.start()
    zf(0)
    mx.wait_recv()
    my = rc(M.at[c, :, y], M.at[c, :, y], ms.at[4], mr.at[4], yn)
    my.start()
    zf(1)
    xf(0)
    my.wait_recv()
    md = rc(M.at[c], M.at[c], ms.at[5], mr.at[5], sib)
    md.start()
    xf(1)
    zf(2)
    fin(0)
    md.wait_recv()

    def picks(width, step, count):
        si = lax.broadcasted_iota(jnp.int32, (128, width), 0)
        sj = lax.broadcasted_iota(jnp.int32, (128, width), 1)
        return lambda dd: jnp.where((si < count) & (sj == si + dd * step), 1.0, 0.0).astype(BF)

    norm_pick, bias_pick = picks(D, 96, 96), picks(128, 16, 16)
    norm_acc = jnp.zeros((16, D), F32)
    bias_acc = jnp.zeros((32, 128), F32)
    for zi in range(4):
        for yi in range(2):
            dd = 2 * zi + yi
            norm_acc = norm_acc + dot(M[c, x, yi, zi].reshape(16, 128).astype(BF), norm_pick(dd), NN)
            bias_acc = bias_acc + dot(M[:, :, yi, zi, 1].reshape(32, 128).astype(BF), bias_pick(dd), NN)
    NB[0] = norm_acc[0:8]
    for tt in range(4):
        row = (tt % 2 * 2 + tt // 2) * 8
        for r in range(6):
            NB[1, tt : tt + 1, r * 128 : r * 128 + 128] = bias_acc[row + r : row + r + 1]

    fin(1)
    ready(0)
    zf(3)
    xf(2)
    ready(1)

    def mat(m):
        return W[m].reshape(D, D)

    for m in (1, 2, 0):
        QKV[m] = dot(hid[...], mat(m), NN).astype(BF)
        if m == 2:
            kvc = rc(QKV.at[pl.ds(1, 2)], KVO, es.at[1], er.at[1], sib)
            kvc.start()
    zf(4)
    fin(2)
    kvc.wait_recv()

    kd = kind[x]
    lane = lax.broadcasted_iota(jnp.int32, (1, 128), 1)
    keylane = lax.broadcasted_iota(jnp.int32, (1, ROWS), 1)
    low_lane = lane < 64

    def flips(hp):
        fa = kd * swap[2 * hp]
        fb = kd * swap[2 * hp + 1]
        return jnp.where(low_lane, jnp.full((1, 128), fa, jnp.int32), jnp.full((1, 128), fb, jnp.int32)) == 1

    def pair_lanes(hp):
        return pl.ds(pl.multiple_of(hp * 128, 128), 128)

    def attn_fwd(hp):
        ls = pair_lanes(hp)
        fl = flips(hp)
        kk = jnp.where(fl, KVO[0, :, ls], QKV[1, :, ls])
        vv = jnp.where(fl, KVO[1, :, ls], QKV[2, :, ls])
        for rb in range(2):
            rows = slice(rb * 256, rb * 256 + 256)
            q = QKV[0, rows, ls] * jnp.asarray(0.125, BF)
            outs = []
            for e in range(2):
                sw = swap[2 * hp + e]
                qe = jnp.where(low_lane if e == 0 else ~low_lane, q, jnp.zeros_like(q))
                s = dot(qe, kk, NT)
                kb = jnp.where(keylane >= 256, 1, 0)
                same = jnp.where(kb == rb, 0, 1)
                seen = (same == jnp.full((1, ROWS), sw, jnp.int32)) | (jnp.full((1, ROWS), kd, jnp.int32) == 1)
                s = s + jnp.where(seen, 0.0, NEGATIVE)
                top = jnp.max(s, axis=1, keepdims=True)
                pw = jnp.exp(s - top)
                tot = jnp.sum(pw, axis=1, keepdims=True)
                a = (pw * (1.0 / tot)).astype(BF)
                AT[2 * hp + e, rows, :] = a
                outs.append(dot(a, vv, NN))
            CTX[rows, ls] = jnp.where(low_lane, outs[0], outs[1]).astype(BF)

    pl.loop(0, 1)(attn_fwd)
    xf(3)
    pl.loop(1, 2)(attn_fwd)
    zf(5)
    pl.loop(2, 4)(attn_fwd)
    fin(3)
    xf(4)
    pl.loop(4, 6)(attn_fwd)
    ready(2)
    ready(3)

    ACC[...] = dot(CTX[...], mat(3), NT)

    def ln_rows(i):
        return pl.ds(pl.multiple_of(i * 128, 128), 128)

    g1, b1 = NB[0, 0:1, :], NB[0, 1:2, :]
    g2, b2 = NB[0, 2:3, :], NB[0, 3:4, :]

    @pl.loop(0, 4)
    def _(i):
        rs = ln_rows(i)
        r = hid[rs, :].astype(F32) + ACC[rs, :]
        cen = r - jnp.mean(r, axis=1, keepdims=True)
        rstd = lax.rsqrt(jnp.mean(cen * cen, axis=1, keepdims=True) + EPSILON)
        xh = cen * rstd
        XH[rs, :] = xh
        RS1[rs, :] = rstd
        FI[rs, :] = (xh * g1 + b1).astype(BF)

    xf(5)
    fin(4)
    for tt in range(4):
        pre = dot(FI[...], mat(4 + tt), NN) + NB[1, tt : tt + 1, :]
        cdf = 0.5 * (1.0 + lax.erf(pre * math.sqrt(0.5)))
        ACT[tt] = (pre * cdf).astype(BF)
        GP[tt] = (cdf + pre * (jnp.exp(-0.5 * pre * pre) * (1.0 / math.sqrt(2.0 * math.pi)))).astype(BF)

    fin(5)
    ready(4)

    def half_mat(m, h):
        return W[m, :, :, :, :, h * HALF : h * HALF + HALF].reshape(D, HALF)

    acc = dot(ACT[0, :, 0:HALF], half_mat(8, 0), NT)
    for tt in range(1, 4):
        acc = acc + dot(ACT[tt, :, 0:HALF], half_mat(8 + tt, 0), NT)
    ACC[...] = acc
    ready(5)
    acc = dot(ACT[0, :, HALF:D], half_mat(8, 1), NT)
    for tt in range(1, 4):
        acc = acc + dot(ACT[tt, :, HALF:D], half_mat(8 + tt, 1), NT)
    ACC[...] += acc

    V[...] = jnp.zeros_like(V)

    @pl.loop(0, 4)
    def _(i):
        rs = ln_rows(i)
        r = XH[rs, :] * g1 + b1 + ACC[rs, :]
        cen = r - jnp.mean(r, axis=1, keepdims=True)
        rstd = lax.rsqrt(jnp.mean(cen * cen, axis=1, keepdims=True) + EPSILON)
        n2 = cen * rstd
        mixed[rs, :] = (n2 * g2 + b2).astype(BF)
        co = cot[rs, :].astype(F32)
        e = co * g2
        gr = rstd * (e - jnp.mean(e, axis=1, keepdims=True) - n2 * jnp.mean(e * n2, axis=1, keepdims=True))
        ACC[rs, :] = gr
        GF[rs, :] = gr.astype(BF)
        V[2:3, :] += jnp.sum(co * n2, axis=0, keepdims=True)
        V[3:4, :] += jnp.sum(co, axis=0, keepdims=True)

    def sq(r, xx):
        if r < 2:
            return SQ.at[r, xx]
        return W.at[8 + 2 * (r // 2 - 1) + xx, :, :, :, :, pl.ds((r % 2) * HALF, HALF)]

    def pb(r, xx, *rest):
        if r < 4:
            return PB.at[(r, xx) + rest]
        rest = rest + (slice(None),) * (4 - len(rest))
        return W.at[(4 + xx,) + rest + (pl.ds((r % 2) * HALF, HALF),)]

    def pb_all(r, *rest):
        if r < 4:
            return PB.at[(r, slice(None)) + rest]
        rest = rest + (slice(None),) * (4 - len(rest))
        return W.at[(pl.ds(4, 2),) + rest + (pl.ds((r % 2) * HALF, HALF),)]

    def b_sib(r):
        q = r % SLOTS
        if r < 2:
            return rc(SQ.at[r], SR.at[q], qs.at[r], qr.at[r], sib)
        src = W.at[pl.ds(8 + 2 * (r // 2 - 1), 2), :, :, :, :, pl.ds((r % 2) * HALF, HALF)]
        return rc(src, SR.at[q], qs.at[r], qr.at[r], sib)

    ALL = slice(None)

    def b_a(r):
        return rc(pb(r, ox, ALL, ALL, 0), RA.at[r % SLOTS], as_.at[r], ar.at[r], xn)

    def b_b(r):
        return rc(pb_all(r, ALL, oy, 1), RB.at[r % SLOTS], bs.at[r], br.at[r], yn)

    def b_a2(r, k):
        dst = RO.at[r, 0] if k == 0 else RA2.at[r % SLOTS, k - 1]
        return rc(pb(r, x, zz[k], oy, 0), dst, a2s.at[r, k], a2r.at[r, k], yn)

    def b_b2(r, k):
        dst = RO.at[r, 1] if k == 0 else RB2.at[r % SLOTS, k - 1]
        return rc(pb(r, ox, zz[k], y, 1), dst, b2s.at[r, k], b2r.at[r, k], xn)

    def b_z(r, k):
        return rc(pb(r, x, zz[k], y), RZ.at[r, k - 1], rzs.at[r, k - 1], rzr.at[r, k - 1], zn[k])

    def credit(sem, dev, r):
        if r + SLOTS < PIECES:
            pl.semaphore_signal(sem, inc=1, device_id=dev, device_id_type=pl.DeviceIdType.MESH)

    def need(sem, r):
        if r >= SLOTS:
            pl.semaphore_wait(sem, 1)

    def part(r, xx, core):
        if r < 4:
            src = ACT if r < 2 else GP
            lhs = GF if r < 2 else FI
            h = r % 2
            return dot(lhs[...], src[2 * xx + core, :, h * HALF : h * HALF + HALF], TN)
        raise ValueError

    def part_attn(m, xx):
        if m < 3:
            return dot(hid[...], ACT[m, :, xx * HALF : xx * HALF + HALF], TN)
        return dot(GF[...], CTX[:, xx * HALF : xx * HALF + HALF], TN)

    def gen_sib(r):
        if r < 4:
            for xx in range(2):
                sq(r, xx)[...] = part(r, xx, oc).astype(BF).reshape(4, 2, 2, 48, HALF)
        else:
            for core in range(2):
                @pl.when(oc == core)
                def _():
                    for xx in range(2):
                        sq(r, xx)[...] = part_attn(2 * core + r - 4, xx).astype(BF).reshape(4, 2, 2, 48, HALF)
        need(c_sib, r)
        b_sib(r).start()

    def gen_own(r):
        q = r % SLOTS
        b_sib(r).wait_recv()
        if r < 4:
            for xx in range(2):
                v = part(r, xx, c).reshape(4, 2, 2, 48, HALF) + SR[q, xx].astype(F32)
                pb(r, xx)[...] = v.astype(BF)
        else:
            for core in range(2):
                @pl.when(c == core)
                def _():
                    for xx in range(2):
                        v = part_attn(2 * core + r - 4, xx).reshape(4, 2, 2, 48, HALF) + SR[q, xx].astype(F32)
                        pb(r, xx)[...] = v.astype(BF)
        credit(c_sib, sib, r)
        need(c_a, r)
        b_a(r).start()
        need(c_b, r)
        b_b(r).start()

    def add(dst, src):
        dst[...] = (dst[...].astype(F32) + src[...].astype(F32)).astype(BF)

    def st1(r):
        q = r % SLOTS
        b_a(r).wait_recv()
        add(pb(r, x, ALL, ALL, 0), RA.at[q])
        credit(c_a, xn, r)
        need(c_a2, r)
        for k in (2, 3, 1):
            b_a2(r, k).start()
        b_b(r).wait_recv()
        add(pb_all(r, ALL, y, 1), RB.at[q])
        credit(c_b, yn, r)
        need(c_b2, r)
        for k in (2, 3, 1):
            b_b2(r, k).start()

    def st2o(r):
        b_a2(r, 0).start()
        b_b2(r, 0).start()

    def st2(r):
        q = r % SLOTS
        for k in (2, 3, 1):
            b_a2(r, k).wait_recv()
            add(pb(r, x, zz[k], y, 0), RA2.at[q, k - 1])
            b_b2(r, k).wait_recv()
            add(pb(r, x, zz[k], y, 1), RB2.at[q, k - 1])
            b_z(r, k).start()
        credit(c_a2, yn, r)
        credit(c_b2, xn, r)

    def st3(r):
        tot = pb(r, x, z, y)[...].astype(F32)
        for k in (2, 3, 1):
            b_z(r, k).wait_recv()
            tot = tot + RZ[r, k - 1].astype(F32)
        b_a2(r, 0).wait_recv()
        b_b2(r, 0).wait_recv()
        tot = (tot + RO[r].astype(F32)).reshape(96, HALF)
        h = r % 2
        if r < 2:
            g_down[:, h * HALF : h * HALF + HALF] = tot
        elif r < 4:
            g_up[:, h * HALF : h * HALF + HALF] = tot
        else:
            FX[c, h] = tot

    def rs_drain(r):
        b_sib(r).wait_send()
        b_a(r).wait_send()
        b_b(r).wait_send()
        for k in range(4):
            b_a2(r, k).wait_send()
            b_b2(r, k).wait_send()
        for k in (1, 2, 3):
            b_z(r, k).wait_send()

    gen_sib(0)
    gen_sib(1)
    gen_own(0)
    gen_own(1)

    for tt in range(4):
        ga = dot(GF[...], mat(8 + tt), NN)
        gp = (ga * GP[tt].astype(F32)).astype(BF)
        GP[tt] = gp
        V[4 + tt : 5 + tt, :] = jnp.sum(gp.astype(F32), axis=0, keepdims=True)
        if tt == 2:
            st1(0)

    for p in range(PIECES):
        drain(p)
    gen_sib(2)
    gen_own(2)
    gen_sib(3)
    gen_own(3)
    st1(1)

    acc = dot(GP[0], mat(4), NT)
    for tt in range(1, 4):
        acc = acc + dot(GP[tt], mat(4 + tt), NT)
    ACC[...] += acc

    @pl.loop(0, 4)
    def _(i):
        rs = ln_rows(i)
        gn = ACC[rs, :]
        xh = XH[rs, :]
        e = gn * g1
        gr = RS1[rs, :] * (e - jnp.mean(e, axis=1, keepdims=True) - xh * jnp.mean(e * xh, axis=1, keepdims=True))
        igrad[rs, :] = gr
        GF[rs, :] = gr.astype(BF)
        V[0:1, :] += jnp.sum(gn * xh, axis=0, keepdims=True)
        V[1:2, :] += jnp.sum(gn, axis=0, keepdims=True)

    vc = [
        rc(V, VR.at[0], vs.at[0], vr.at[0], sib),
        rc(V, VR.at[1], vs.at[1], vr.at[1], xn),
        rc(V, VR.at[2], vs.at[2], vr.at[2], yn),
    ] + [rc(V, VR.at[2 + k], vs.at[2 + k], vr.at[2 + k], zn[k]) for k in (1, 2, 3)]

    def v_step(i):
        vc[i].wait()
        V[...] += VR[i]

    vc[0].start()
    st2(0)
    v_step(0)
    vc[1].start()

    FI[...] = dot(GF[...], mat(3), NN).astype(BF)
    v_step(1)
    vc[2].start()

    def attn_bwd(hp):
        ls = pair_lanes(hp)
        fl = flips(hp)
        kk = jnp.where(fl, KVO[0, :, ls], QKV[1, :, ls])
        vv = jnp.where(fl, KVO[1, :, ls], QKV[2, :, ls])
        q = QKV[0, :, ls]
        do = FI[:, ls]
        dvs, dqs, dks = [], [], []
        for e in range(2):
            a = AT[2 * hp + e]
            dvs.append(dot(a, do, TN))
            de = jnp.where(low_lane if e == 0 else ~low_lane, do, jnp.zeros_like(do))
            dp = dot(de, vv, NT)
            af = a.astype(F32)
            w = af * dp
            gs = (w - af * jnp.sum(w, axis=1, keepdims=True)).astype(BF)
            dqs.append(dot(gs, kk, NN))
            dks.append(dot(gs, q, TN))
        ACT[0, :, ls] = (jnp.where(low_lane, dqs[0], dqs[1]) * 0.125).astype(BF)
        GP[0, :, ls] = (jnp.where(low_lane, dks[0], dks[1]) * 0.125).astype(BF)
        GP[1, :, ls] = jnp.where(low_lane, dvs[0], dvs[1]).astype(BF)

    pl.loop(0, 1)(attn_bwd)
    st1(2)
    st2(1)
    v_step(2)
    for k in (1, 2, 3):
        vc[2 + k].start()
    pl.loop(1, 4)(attn_bwd)
    st1(3)
    st2(2)
    pl.loop(4, 6)(attn_bwd)
    dkvc = rc(GP.at[pl.ds(0, 2)], DKVR, es.at[2], er.at[2], sib)
    dkvc.start()
    for k in (1, 2, 3):
        vc[2 + k].wait()
    g_misc[...] = V[...] + VR[3] + VR[4] + VR[5]
    dkvc.wait()

    def pick(hp):
        ls = pair_lanes(hp)
        fl = flips(hp)
        ACT[1, :, ls] = jnp.where(fl, DKVR[0, :, ls], GP[0, :, ls])
        ACT[2, :, ls] = jnp.where(fl, DKVR[1, :, ls], GP[1, :, ls])

    pl.loop(0, 6)(pick)

    gen_sib(4)
    gen_own(4)
    gen_sib(5)
    gen_own(5)
    st2(3)
    acc = dot(ACT[0], mat(0), NT)
    for m in (1, 2):
        acc = acc + dot(ACT[m], mat(m), NT)
    igrad[...] += acc
    st1(4)
    st1(5)
    for r in range(PIECES):
        st2o(r)
    st2(4)
    for r in range(3):
        st3(r)
    st2(5)
    for r in range(3, 6):
        st3(r)
    fx = rc(FX.at[c], FX.at[c], es.at[3], er.at[3], sib)
    fx.start()
    for r in range(PIECES):
        rs_drain(r)
    for cp in mz:
        cp.wait_send()
    mx.wait_send()
    my.wait_send()
    md.wait_send()
    axc.wait_send()
    kvc.wait_send()
    fx.wait()
    g_attn[...] = FX[...].reshape(4, 96, HALF)


def finish_kernel(
    mixed, igrad, ga, gu, gd, gm, o_mixed, o_igrad, o_qkv, o_out, o_up, o_bias, o_down, o_norm, tmp, v_igrad, v_mixed, v_up, v_down, sem
):
    parts = [(igrad, v_igrad, o_igrad, i * 128, 128) for i in range(4)]
    parts += [(mixed, v_mixed, o_mixed, i * 256, 256) for i in range(2)]
    parts += [(gu, v_up, o_up, 0, 96), (gd, v_down, o_down, 0, 96)]
    loads, stores = [], []
    for i, (src, mid, dst, at, n) in enumerate(parts):
        rows = pl.ds(at, n)
        loads.append(pltpu.make_async_copy(src.at[rows], mid.at[rows], sem.at[0, i]))
        stores.append(pltpu.make_async_copy(mid.at[rows], dst.at[rows], sem.at[1, i]))
    for cp in loads:
        cp.start()
    dd = lax.axis_index("dp")
    t = lax.axis_index("tensor")
    first = jnp.full((96, 192), lax.rem(t, 2), jnp.int32) == 0
    for m in range(4):
        v = jnp.where(first, ga[m, :, 0:192], ga[m, :, 192:HALF])
        if m < 3:
            o_qkv[m] = v
        else:
            o_out[...] = v.T
    exact = dict(preferred_element_type=F32, precision=lax.Precision.HIGHEST)
    si = lax.broadcasted_iota(jnp.int32, (D, 128), 0)
    sj = lax.broadcasted_iota(jnp.int32, (D, 128), 1)
    pick = jnp.where(si == sj + dd * 96, 1.0, 0.0).astype(F32)
    for load, store in zip(loads, stores):
        load.wait()
        store.start()
    sub = lax.broadcasted_iota(jnp.int32, (8, D), 0)
    norm = lax.dot_general(gm[...], pick, NN, **exact)
    o_norm[...] = jnp.sum(jnp.where(sub[:, 0:128] == t, norm, 0.0), axis=0, keepdims=True)[:, 0:96]
    row = jnp.sum(jnp.where(sub == 4 + t, gm[...], 0.0), axis=0, keepdims=True)
    for r in range(6):
        tmp[r : r + 1] = row[:, r * 128 : r * 128 + 128]
    pick = jnp.where(si[0:128] == sj[0:128] + dd * 16, 1.0, 0.0).astype(F32)
    o_bias[...] = lax.dot_general(tmp[...], pick, NN, **exact)[0:6, 0:16]
    for cp in stores:
        cp.wait()


def scratch():
    vm = pltpu.VMEM
    dma = lambda *s: pltpu.SemaphoreType.DMA(s)
    n = PIECES
    return [
        vm((12, 4, 2, 2, 48, D), BF), vm((4, 96, 256), BF), vm((2, 96, 256), BF), vm((3, ROWS, D), BF), vm((2, ROWS, D), BF),
        vm((12, ROWS, ROWS), BF), vm((ROWS, D), BF), vm((ROWS, D), F32), vm((ROWS, 1), F32), vm((ROWS, D), BF),
        vm((4, ROWS, D), BF), vm((4, ROWS, D), BF), vm((ROWS, D), F32), vm((ROWS, D), BF), vm((2, ROWS, D), BF),
        vm((2, 2, 2, 4, 2, 8, 128), F32), vm((2, 8, D), F32), vm((8, D), F32), vm((6, 8, D), F32), vm((2, 2, 96, HALF), F32),
        vm((2, 2, 4, 2, 2, 48, HALF), BF), vm((SLOTS, 2, 4, 2, 2, 48, HALF), BF), vm((4, 2, 4, 2, 2, 48, HALF), BF),
        vm((SLOTS, 4, 2, 48, HALF), BF), vm((SLOTS, 2, 4, 48, HALF), BF), vm((SLOTS, 3, 48, HALF), BF),
        vm((SLOTS, 3, 48, HALF), BF), vm((n, 2, 48, HALF), BF), vm((n, 3, 2, 48, HALF), BF),
        dma(n, 3), dma(n, 3), dma(n, 4), dma(n, 4), dma(n, 4), dma(n, 4), dma(n, 2), dma(n, 2), dma(n, 4), dma(n, 4),
        dma(6), dma(6), dma(4), dma(4),
        dma(n), dma(n), dma(n), dma(n), dma(n), dma(n), dma(n, 4), dma(n, 4), dma(n, 4), dma(n, 4), dma(n, 3), dma(n, 3), dma(6), dma(6),
        pltpu.SemaphoreType.REGULAR, pltpu.SemaphoreType.REGULAR, pltpu.SemaphoreType.REGULAR,
        pltpu.SemaphoreType.REGULAR, pltpu.SemaphoreType.REGULAR,
    ]


def whole_layer(
    hidden_in, qkv_weight, out_weight, up_weight, up_bias, down_weight, norm_params, cotangent, head_swap, slot_kind
):
    vmem = pl.BlockSpec(memory_space=pltpu.VMEM)
    smem = pl.BlockSpec(memory_space=pltpu.SMEM)
    sds = jax.ShapeDtypeStruct
    mixed, igrad, ga, gu, gd, gm = pl.pallas_call(
        layer_kernel,
        out_shape=(
            sds((ROWS, D), BF), sds((ROWS, D), F32), sds((4, 96, HALF), F32),
            sds((96, D), F32), sds((96, D), F32), sds((8, D), F32),
        ),
        in_specs=[vmem] * 8 + [smem] * 2,
        out_specs=(vmem,) * 6,
        scratch_shapes=scratch(),
        compiler_params=pltpu.CompilerParams(
            collective_id=0, has_side_effects=True, vmem_limit_bytes=63 * 2**20
        ),
        name="layer",
    )(
        hidden_in, qkv_weight, out_weight, up_weight, up_bias, down_weight.T, norm_params, cotangent, head_swap, slot_kind
    )
    any_ = pl.BlockSpec(memory_space=pl.ANY)
    *outs, bias_grad, down_grad, norm_grad = pl.pallas_call(
        finish_kernel,
        out_shape=(
            sds((ROWS, D), BF), sds((ROWS, D), F32), sds((3, 96, 192), F32), sds((192, 96), F32),
            sds((96, D), F32), sds((6, 16), F32), sds((96, D), F32), sds((1, 96), F32),
        ),
        in_specs=[any_, any_, vmem, any_, any_, vmem],
        out_specs=(any_, any_, vmem, vmem, any_, vmem, any_, vmem),
        scratch_shapes=[
            pltpu.VMEM((8, 128), F32), pltpu.VMEM((ROWS, D), F32), pltpu.VMEM((ROWS, D), BF),
            pltpu.VMEM((96, D), F32), pltpu.VMEM((96, D), F32), pltpu.SemaphoreType.DMA((2, 8)),
        ],
        compiler_params=pltpu.CompilerParams(vmem_limit_bytes=63 * 2**20),
        name="finish",
    )(mixed, igrad, ga, gu, gd, gm)
    return (*outs, bias_grad, down_grad.T, norm_grad)


def norm_rows(residual, scales, offset):
    center = residual - jnp.mean(residual, axis=-1, keepdims=True)
    spread = jnp.mean(center * center, axis=-1, keepdims=True)
    return center * lax.rsqrt(spread + EPSILON) * scales + offset


def smooth_gate(values):
    return jax.nn.gelu(values, approximate=False)


def arrange(queries, keys_in, values_in, slot_type, local_swaps):
    slot_len, head_count, head_size = queries.shape
    half_len = slot_len // 2
    quarter = half_len // 2
    shape_four = (2, half_len, head_count, head_size)
    query_half = queries.reshape(shape_four)
    key_half = keys_in.reshape(shape_four)
    value_half = values_in.reshape(shape_four)
    flipped = (local_swaps * slot_type == 1)[None, None, :, None]
    key_pick = jnp.where(flipped, key_half[::-1], key_half)
    value_pick = jnp.where(flipped, value_half[::-1], value_half)
    blocks = jnp.arange(half_len, dtype=jnp.int32) // quarter
    matching = (
        jnp.bitwise_xor(blocks[None, :, None], local_swaps[:, None, None]) == blocks[None, None, :]
    )
    allowed = jnp.logical_or(slot_type == 1, matching)
    return (query_half, key_pick, value_pick, allowed, flipped)


def masked_scores(query_half, key_pick, allowed):
    scale = 1.0 / math.sqrt(query_half.shape[-1])
    scores = (
        jnp.einsum("jqhd,jkhd->jhqk", query_half, key_pick, preferred_element_type=jnp.float32)
        * scale
    )
    return jnp.where(allowed[None], scores, NEGATIVE)


def slot_forward(inputs, local_swaps):
    queries, keys_in, values_in, slot_type = inputs
    query_half, key_pick, value_pick, allowed, flipped = arrange(
        queries, keys_in, values_in, slot_type, local_swaps
    )
    scores = masked_scores(query_half, key_pick, allowed)
    largest = jnp.max(scores, axis=-1, keepdims=True)
    powers = jnp.exp(scores - largest)
    totals = jnp.sum(powers, axis=-1, keepdims=True)
    attention = (powers / totals).astype(jnp.bfloat16)
    context = jnp.einsum(
        "jhqk,jkhd->jqhd", attention, value_pick, preferred_element_type=jnp.float32
    )
    return (context.astype(jnp.bfloat16).reshape(queries.shape[0], -1), largest + jnp.log(totals))


def slot_backward(inputs, local_swaps):
    queries, keys_in, values_in, slot_type, log_totals, grad_out = inputs
    slot_len, head_count, head_size = queries.shape
    scale = 1.0 / math.sqrt(head_size)
    query_half, key_pick, value_pick, allowed, flipped = arrange(
        queries, keys_in, values_in, slot_type, local_swaps
    )
    attention = jnp.exp(masked_scores(query_half, key_pick, allowed) - log_totals)
    grad_half = grad_out.reshape(query_half.shape)
    grad_vpick = jnp.einsum(
        "jhqk,jqhd->jkhd",
        attention.astype(jnp.bfloat16),
        grad_half,
        preferred_element_type=jnp.float32,
    ).astype(jnp.bfloat16)
    grad_attention = jnp.einsum(
        "jqhd,jkhd->jhqk", grad_half, value_pick, preferred_element_type=jnp.float32
    )
    row_dots = jnp.sum(attention * grad_attention, axis=-1, keepdims=True)
    grad_scores = (attention * (grad_attention - row_dots)).astype(jnp.bfloat16)
    grad_query = (
        jnp.einsum("jhqk,jkhd->jqhd", grad_scores, key_pick, preferred_element_type=jnp.float32)
        * scale
    ).astype(jnp.bfloat16)
    grad_kpick = (
        jnp.einsum("jhqk,jqhd->jkhd", grad_scores, query_half, preferred_element_type=jnp.float32)
        * scale
    ).astype(jnp.bfloat16)
    grad_key = jnp.where(flipped, grad_kpick[::-1], grad_kpick)
    grad_value = jnp.where(flipped, grad_vpick[::-1], grad_vpick)
    return (
        grad_query.reshape(slot_len, -1),
        grad_key.reshape(slot_len, -1),
        grad_value.reshape(slot_len, -1),
    )


def per_device(
    hidden_in,
    qkv_weight,
    out_weight,
    up_weight,
    up_bias,
    down_weight,
    norm_params,
    cotangent,
    head_swap,
    slot_kind,
):
    tensor_count = lax.axis_size("tensor")
    tensor_rank = lax.axis_index("tensor")
    heads_here = head_swap.shape[0] // tensor_count
    local_swaps = lax.dynamic_slice_in_dim(head_swap, tensor_rank * heads_here, heads_here)
    qkv_low = qkv_weight.astype(jnp.bfloat16)
    out_low = out_weight.astype(jnp.bfloat16)
    norm_low = norm_params.astype(jnp.bfloat16)
    up_low = up_weight.astype(jnp.bfloat16)
    bias_low = up_bias.astype(jnp.bfloat16)
    down_low = down_weight.astype(jnp.bfloat16)
    qkv_full, out_full, norm_full = (
        lax.all_gather(qkv_low, "dp", axis=1, tiled=True),
        lax.all_gather(out_low, "dp", axis=1, tiled=True),
        lax.all_gather(norm_low, "dp", axis=1, tiled=True),
    )
    norm_gain = norm_full.astype(jnp.float32)
    full_in = lax.all_gather(hidden_in, "tensor", axis=0, tiled=True)
    group_rows = full_in.shape[0]
    local_width = qkv_full.shape[2]
    head_size = local_width // heads_here
    slot_count = group_rows // LONG_LEN

    def by_slot(rows):
        return rows.reshape(slot_count, LONG_LEN, heads_here, head_size)

    projected = jnp.einsum(
        "td,cde->cte", full_in, qkv_full, preferred_element_type=jnp.float32
    ).astype(jnp.bfloat16)
    context, log_totals = lax.map(
        partial(slot_forward, local_swaps=local_swaps),
        (by_slot(projected[0]), by_slot(projected[1]), by_slot(projected[2]), slot_kind),
    )
    context = context.reshape(group_rows, local_width)
    rows = context
    attn_share = lax.psum_scatter(
        jnp.dot(rows, out_full, preferred_element_type=jnp.float32).astype(jnp.bfloat16),
        "tensor",
        scatter_dimension=0,
        tiled=True,
    ).astype(jnp.float32)
    resid_one = hidden_in.astype(jnp.float32) + attn_share
    normed_one, norm_one_back = jax.vjp(norm_rows, resid_one, norm_gain[0], norm_gain[1])
    up_full, bias_full, down_full = (
        lax.all_gather(up_low, "dp", axis=0, tiled=True),
        lax.all_gather(bias_low, "dp", axis=1, tiled=True),
        lax.all_gather(down_low, "dp", axis=1, tiled=True),
    )
    ffn_in = lax.all_gather(normed_one.astype(jnp.bfloat16), "tensor", axis=0, tiled=True)
    pre = jnp.dot(ffn_in, up_full, preferred_element_type=jnp.float32) + bias_full.reshape(
        -1
    ).astype(jnp.float32)
    act_value, gate_back = jax.vjp(smooth_gate, pre)
    act = act_value.astype(jnp.bfloat16)
    rows = act
    ffn_share = lax.psum_scatter(
        jnp.dot(rows, down_full, preferred_element_type=jnp.float32).astype(jnp.bfloat16),
        "tensor",
        scatter_dimension=0,
        tiled=True,
    ).astype(jnp.float32)
    normed_two, norm_two_back = jax.vjp(
        norm_rows, normed_one + ffn_share, norm_gain[2], norm_gain[3]
    )
    mixed = normed_two.astype(jnp.bfloat16)
    grad_resid_two, grad_gain_two, grad_bias_two = norm_two_back(cotangent.astype(jnp.float32))
    grad_ffn = lax.all_gather(grad_resid_two.astype(jnp.bfloat16), "tensor", axis=0, tiled=True)
    grad_down = jnp.einsum("tf,td->fd", act, grad_ffn, preferred_element_type=jnp.float32)
    grad_act = jnp.einsum("td,fd->tf", grad_ffn, down_full, preferred_element_type=jnp.float32)
    grad_pre = gate_back(grad_act)[0].astype(jnp.bfloat16)
    grad_up = jnp.einsum("td,tf->df", ffn_in, grad_pre, preferred_element_type=jnp.float32)
    grad_bias = jnp.sum(grad_pre.astype(jnp.float32), axis=0).reshape(bias_full.shape)
    rows = grad_pre
    grad_normed_one = grad_resid_two + lax.psum_scatter(
        jnp.einsum("tf,df->td", rows, up_full, preferred_element_type=jnp.float32).astype(
            jnp.bfloat16
        ),
        "tensor",
        scatter_dimension=0,
        tiled=True,
    ).astype(jnp.float32)
    grad_resid_one, grad_gain_one, grad_bias_one = norm_one_back(grad_normed_one)
    grad_attn = lax.all_gather(grad_resid_one.astype(jnp.bfloat16), "tensor", axis=0, tiled=True)
    grad_out = jnp.einsum("tw,td->wd", context, grad_attn, preferred_element_type=jnp.float32)
    grad_context = jnp.einsum(
        "td,wd->tw", grad_attn, out_full, preferred_element_type=jnp.float32
    ).astype(jnp.bfloat16)
    grad_query, grad_key, grad_value = lax.map(
        partial(slot_backward, local_swaps=local_swaps),
        (
            by_slot(projected[0]),
            by_slot(projected[1]),
            by_slot(projected[2]),
            slot_kind,
            log_totals,
            grad_context.reshape(slot_count, LONG_LEN, local_width),
        ),
    )
    grad_proj = jnp.stack([grad_query, grad_key, grad_value]).reshape(3, group_rows, local_width)
    grad_qkv = jnp.einsum("td,cte->cde", full_in, grad_proj, preferred_element_type=jnp.float32)
    grad_in_part = jnp.einsum(
        "cte,cde->td", grad_proj, qkv_full, preferred_element_type=jnp.float32
    )
    norm_part = jnp.stack([grad_gain_one, grad_bias_one, grad_gain_two, grad_bias_two])
    grad_in_share, norm_row = (
        lax.psum_scatter(
            grad_in_part.astype(jnp.bfloat16), "tensor", scatter_dimension=0, tiled=True
        ).astype(jnp.float32),
        lax.psum_scatter(
            norm_part.astype(jnp.bfloat16), "tensor", scatter_dimension=0, tiled=True
        ).astype(jnp.float32),
    )
    input_grad = grad_resid_one + grad_in_share
    qkv_grad, out_grad, up_grad, up_bias_grad, down_grad, norm_grad = (
        lax.psum_scatter(grad_qkv, "dp", scatter_dimension=1, tiled=True),
        lax.psum_scatter(grad_out, "dp", scatter_dimension=1, tiled=True),
        lax.psum_scatter(grad_up, "dp", scatter_dimension=0, tiled=True),
        lax.psum_scatter(grad_bias, "dp", scatter_dimension=1, tiled=True),
        lax.psum_scatter(grad_down, "dp", scatter_dimension=1, tiled=True),
        lax.psum_scatter(norm_row, "dp", scatter_dimension=1, tiled=True),
    )
    return (mixed, input_grad, qkv_grad, out_grad, up_grad, up_bias_grad, down_grad, norm_grad)


def solution(mesh):
    placed = (
        P(("dp", "tensor"), None),
        P(None, "dp", "tensor"),
        P("tensor", "dp"),
        P("dp", "tensor"),
        P("tensor", "dp"),
        P("tensor", "dp"),
        P(None, "dp"),
        P(("dp", "tensor"), None),
        P(),
        P("dp"),
    )
    planned = mesh.shape["dp"] == 8 and mesh.shape["tensor"] == 4
    return jax.shard_map(
        whole_layer if planned else per_device,
        mesh=mesh,
        in_specs=placed,
        out_specs=(
            P(("dp", "tensor"), None),
            P(("dp", "tensor"), None),
            P(None, "dp", "tensor"),
            P("tensor", "dp"),
            P("dp", "tensor"),
            P("tensor", "dp"),
            P("tensor", "dp"),
            P("tensor", "dp"),
        ),
        check_vma=False,
    )
```

```python
from functools import partial
import math

import jax
import jax.numpy as jnp
from jax import lax
from jax.experimental import pallas as pl
from jax.experimental.pallas import tpu as pltpu
from jax.sharding import PartitionSpec as P

LONG_LEN = 1024
EPSILON = 1e-05
NEGATIVE = -1e30

BF = jnp.bfloat16
F32 = jnp.float32
NN = (((1,), (0,)), ((), ()))
NT = (((1,), (1,)), ((), ()))
TN = (((0,), (0,)), ((), ()))
PIECES = 6
SLOTS = 3
SIB_SLOT = (2, 0, 1, 0, 1, 2)
ROWS = 512
D = 768
HALF = 384


def dot(a, b, dims):
    return lax.dot_general(a, b, dims, preferred_element_type=F32)


def layer_kernel(
    hid_in, qkv_w, out_w, up_w, up_b, down_w, norm_p, cot_in, swap, kind,
    mixed_out, igrad, g_attn, g_up, g_down, g_misc,
    hid, cot, mixed, W, SH, AX, QKV, KVO, AT, CTX, XH, RS1, FI, ACT, GP, GF, DKVR,
    M, NB, V, VR,
    SQ, SR, PB, RA, RB, RA2, RB2, RO, RZ, RU, RD, R0,
    zs, zr, xs, xr, ys, yr, hs, hr, ds_, dr, ms, mr, es, er,
    qs, qr, as_, ar, bs, br, a2s, a2r, b2s, b2r, rzs, rzr, vs, vr, ls_, lr, lds, ldr, zls, zlr, z0s, z0r, io,
    c_sib, c_a, c_b, c_a2, c_b2,
):
    d = lax.axis_index("dp")
    t = lax.axis_index("tensor")
    z, y = d // 2, lax.rem(d, 2)
    x, c = t // 2, lax.rem(t, 2)
    ox, oy, oc = 1 - x, 1 - y, 1 - c

    def zk(k):
        hi, lo = z // 2, lax.rem(z, 2)
        kh, kl = k // 2, k % 2
        h2 = hi if kh == 0 else 1 - hi
        l2 = lo if kl == 0 else 1 - lo
        return 2 * h2 + l2

    zz = [zk(k) for k in range(4)]
    sib = (d, 2 * x + oc)
    xn = (d, 2 * ox + c)
    yn = (2 * z + oy, t)
    zn = [(2 * zz[k] + y, t) for k in range(4)]

    def rc(src, dst, s, r, dev):
        return pltpu.make_async_remote_copy(
            src_ref=src, dst_ref=dst, send_sem=s, recv_sem=r,
            device_id=dev, device_id_type=pl.DeviceIdType.MESH,
        )

    load_hid = pltpu.make_async_copy(hid_in, hid, io.at[0])
    load_cot = pltpu.make_async_copy(cot_in, cot, io.at[1])
    save_mixed = pltpu.make_async_copy(mixed, mixed_out, io.at[2])
    load_hid.start()
    load_cot.start()

    bar = pltpu.get_barrier_semaphore()
    for dev in (sib, xn, yn, zn[1], zn[2], zn[3]):
        pl.semaphore_signal(bar, inc=1, device_id=dev, device_id_type=pl.DeviceIdType.MESH)

    def where(p, xx, core):
        if p < 2:
            return 2 * core + p, pl.multiple_of(xx * HALF, 128)
        if p < 4:
            return 4 + 2 * xx + core, (p - 2) * HALF
        return 8 + 2 * xx + core, (p - 4) * HALF

    def slab(p, xx, zi, yi, core=None):
        m, lane = where(p, xx, c if core is None else core)
        return W.at[m, zi, yi, :, :, pl.ds(lane, HALF)]

    def col(p, xx, yi, core=None):
        m, lane = where(p, xx, c if core is None else core)
        return W.at[m, :, yi, :, :, pl.ds(lane, HALF)]

    def hcol(p, xx, yi, half):
        m, lane = where(p, xx, c)
        return W.at[m, :, yi, half, :, pl.ds(lane, HALF)]

    def zcp(p, k, recv=False):
        s = slab(p, x, zz[k] if recv else z, y)
        return rc(s, s, zs.at[p, k - 1], zr.at[p, k - 1], zn[k])

    def xcp(p, k, recv=False):
        s = slab(p, ox if recv else x, zz[k], y)
        return rc(s, s, xs.at[p, k], xr.at[p, k], xn)

    def ycp(p, k, recv=False):
        s = slab(p, x, zz[k], oy if recv else y)
        return rc(s, s, ys.at[p, k], yr.at[p, k], yn)

    def acp(p, recv=False):
        s = hcol(p, ox, oy if recv else y, 0)
        return rc(s, s, hs.at[p, 0], hr.at[p, 0], yn)

    def bcp(p, recv=False):
        s = hcol(p, ox if recv else x, oy, 1)
        return rc(s, s, hs.at[p, 1], hr.at[p, 1], xn)

    groups = [(x, y), (ox, y), (x, oy), (ox, oy)]

    def dcp(p, g, recv=False):
        xx, yy = groups[g]
        s = col(p, xx, yy, oc if recv else c)
        return rc(s, s, ds_.at[p, g], dr.at[p, g], sib)

    last = PIECES - 1

    def lx(recv=False):
        s = slab(last, ox if recv else x, z, y)
        return rc(s, s, xs.at[last, 0], xr.at[last, 0], xn)

    def ly(recv=False):
        s = slab(last, x, z, oy if recv else y)
        return rc(s, s, ys.at[last, 0], yr.at[last, 0], yn)

    def lhalf(i, recv=False):
        if i == 0:
            xx, yy, dev = ox, oy if recv else y, yn
        else:
            xx, yy, dev = ox if recv else x, oy, xn
        m, lane = where(last, xx, c)
        s = W.at[m, z, yy, i, :, pl.ds(lane, HALF)]
        return rc(s, s, hs.at[last, i], hr.at[last, i], dev)

    def lcol(core, xx, zi):
        m, lane = where(last, xx, core)
        return W.at[m, zi, :, :, :, pl.ds(lane, HALF)]

    up_dev, down_dev = (d + 2, t), (d - 2, t)

    def line(way, j, xx, recv=False):
        zi = z - j if way == 0 else z + j
        s = lcol(c, xx, zi)
        i = j if recv else j + 1
        dev = up_dev if way == 0 else down_dev
        return rc(s, s, ls_.at[way, i - 1, xx], lr.at[way, i - 1, xx], dev)

    def ldc(way, j, xx, recv=False):
        zi = z - j if way == 0 else z + j
        s = lcol(oc if recv else c, xx, zi)
        i = 6 if j == 0 else way * 3 + j - 1
        return rc(s, s, lds.at[i, xx], ldr.at[i, xx], sib)

    def lsend(way, j):
        if way == 0:
            return (z < 3) & (z >= j)
        return (z > 0) & (z + j <= 3)

    def lgot(way, j):
        return z >= j if way == 0 else z + j <= 3

    def last_xy():
        lx(True).wait_recv()
        lhalf(0).start()
        ly(True).wait_recv()
        lhalf(1).start()

    def last_start():
        lhalf(0, True).wait_recv()
        lhalf(1, True).wait_recv()
        for xx in range(2):
            for way in range(2):
                pl.when(lsend(way, 0))(lambda: line(way, 0, xx).start())
        for xx in range(2):
            ldc(0, 0, xx).start()

    def last_step(j):
        for xx in range(2):
            for way in range(2):
                @pl.when(lgot(way, j))
                def _():
                    line(way, j, xx, True).wait_recv()
                    if j < 3:
                        pl.when(lsend(way, j))(lambda: line(way, j, xx).start())
                    ldc(way, j, xx).start()

    def last_ready():
        for xx in range(2):
            ldc(0, 0, xx, True).wait_recv()
            for way in range(2):
                for j in (1, 2, 3):
                    pl.when(lgot(way, j))(lambda: ldc(way, j, xx, True).wait_recv())

    def last_drain():
        lx().wait_send()
        ly().wait_send()
        lhalf(0).wait_send()
        lhalf(1).wait_send()
        for xx in range(2):
            ldc(0, 0, xx).wait_send()
            for way in range(2):
                for j in range(3):
                    pl.when(lsend(way, j))(lambda: line(way, j, xx).wait_send())
                for j in (1, 2, 3):
                    pl.when(lgot(way, j))(lambda: ldc(way, j, xx).wait_send())

    def own_xy(p):
        if p == last:
            lx().start()
            ly().start()
            return
        xcp(p, 0).start()
        ycp(p, 0).start()

    def own_z(p):
        for k in (1, 2, 3):
            zcp(p, k).start()

    def zf(p):
        for k in (1, 2, 3):
            zcp(p, k, True).wait_recv()
            xcp(p, k).start()
            ycp(p, k).start()
        dcp(p, 0).start()

    def xf(p):
        for k in range(4):
            xcp(p, k, True).wait_recv()
        acp(p).start()
        dcp(p, 1).start()
        for k in range(4):
            ycp(p, k, True).wait_recv()
        bcp(p).start()
        dcp(p, 2).start()

    def fin(p):
        acp(p, True).wait_recv()
        bcp(p, True).wait_recv()
        dcp(p, 3).start()

    def ready(p):
        for g in range(4):
            dcp(p, g, True).wait_recv()

    def drain(p):
        for k in (1, 2, 3):
            zcp(p, k).wait_send()
        for k in range(4):
            xcp(p, k).wait_send()
            ycp(p, k).wait_send()
        acp(p).wait_send()
        bcp(p).wait_send()
        for g in range(4):
            dcp(p, g).wait_send()

    SH[3, :, 0:192] = out_w[...].astype(BF).T
    for m, i in enumerate((1, 0, 2)):
        SH[m, :, 0:192] = qkv_w[i].astype(BF)
    W[4 + t, z, y] = up_w[...].astype(BF).reshape(2, 48, D)
    W[8 + t, z, y] = down_w[...].astype(BF).reshape(2, 48, D)
    M[c, x, y, z, 0, 0:4, 0:96] = norm_p[...].astype(BF).astype(F32)
    M[c, x, y, z, 1, 0:6, 0:16] = up_b[...].astype(BF).astype(F32)
    pl.semaphore_wait(bar, 6)
    axc = rc(SH.at[pl.ds(2 * oc, 2)], AX, es.at[0], er.at[0], sib)
    axc.start()
    own_xy(5)
    own_xy(2)
    mz = [rc(M.at[c, x, y, z], M.at[c, x, y, z], ms.at[k - 1], mr.at[k - 1], zn[k]) for k in (1, 2, 3)]
    for cp in mz:
        cp.start()
    axc.wait_recv()
    own_lane = pl.ds(pl.multiple_of(x * HALF, 128), HALF)
    first = jnp.full((96, 192), c, jnp.int32) == 0
    for i in range(2):
        mine, theirs = SH[2 * c + i, :, 0:192], AX[i, :, 0:192]
        both = jnp.concatenate([jnp.where(first, mine, theirs), jnp.where(first, theirs, mine)], axis=1)
        W[2 * c + i, z, y, :, :, own_lane] = both.reshape(2, 48, HALF)
        own_z(i)
        own_xy(i)
    for p in (2, 3, 4):
        own_z(p)

    for cp in mz:
        cp.wait_recv()
    mx = rc(M.at[c, x, y], M.at[c, x, y], ms.at[3], mr.at[3], xn)
    mx.start()
    zf(0)
    own_xy(3)
    zf(1)
    own_xy(4)
    xf(0)
    xf(1)
    mx.wait_recv()
    my = rc(M.at[c, :, y], M.at[c, :, y], ms.at[4], mr.at[4], yn)
    my.start()
    zf(2)
    last_xy()
    fin(0)
    ready(0)

    def mat(m):
        return W[m].reshape(D, D)

    load_hid.wait()
    QKV[1] = dot(hid[...], mat(0), NN).astype(BF)
    QKV[2] = dot(hid[...], mat(2), NN).astype(BF)
    kvc = rc(QKV.at[pl.ds(1, 2)], KVO, es.at[1], er.at[1], sib)
    kvc.start()
    fin(1)
    zf(3)
    my.wait_recv()
    md = rc(M.at[c], M.at[c], ms.at[5], mr.at[5], sib)
    md.start()
    ready(1)
    QKV[0] = dot(hid[...], mat(1), NN).astype(BF)
    kvc.wait_recv()

    kd = kind[x]
    lane = lax.broadcasted_iota(jnp.int32, (1, 128), 1)
    keylane = lax.broadcasted_iota(jnp.int32, (1, ROWS), 1)
    low_lane = lane < 64

    def flips(hp):
        fa = kd * swap[2 * hp]
        fb = kd * swap[2 * hp + 1]
        return jnp.where(low_lane, jnp.full((1, 128), fa, jnp.int32), jnp.full((1, 128), fb, jnp.int32)) == 1

    def pair_lanes(hp):
        return pl.ds(pl.multiple_of(hp * 128, 128), 128)

    def attn_fwd(hp):
        ls = pair_lanes(hp)
        fl = flips(hp)
        kk = jnp.where(fl, KVO[0, :, ls], QKV[1, :, ls])
        vv = jnp.where(fl, KVO[1, :, ls], QKV[2, :, ls])
        for rb in range(2):
            rows = slice(rb * 256, rb * 256 + 256)
            q = QKV[0, rows, ls] * jnp.asarray(0.125, BF)
            outs = []
            for e in range(2):
                sw = swap[2 * hp + e]
                qe = jnp.where(low_lane if e == 0 else ~low_lane, q, jnp.zeros_like(q))
                s = dot(qe, kk, NT)
                kb = jnp.where(keylane >= 256, 1, 0)
                same = jnp.where(kb == rb, 0, 1)
                seen = (same == jnp.full((1, ROWS), sw, jnp.int32)) | (jnp.full((1, ROWS), kd, jnp.int32) == 1)
                s = s + jnp.where(seen, 0.0, NEGATIVE)
                top = jnp.max(s, axis=1, keepdims=True)
                pw = jnp.exp(s - top)
                tot = jnp.sum(pw, axis=1, keepdims=True)
                a = (pw * (1.0 / tot)).astype(BF)
                AT[2 * hp + e, rows, :] = a
                outs.append(dot(a, vv, NN))
            CTX[rows, ls] = jnp.where(low_lane, outs[0], outs[1]).astype(BF)

    pl.loop(0, 1)(attn_fwd)
    xf(2)
    zf(4)
    pl.loop(1, 2)(attn_fwd)
    last_start()
    pl.loop(2, 3)(attn_fwd)
    fin(2)
    xf(3)
    pl.loop(3, 4)(attn_fwd)
    last_step(1)
    pl.loop(4, 5)(attn_fwd)
    xf(4)
    md.wait_recv()
    def picks(width, step, count):
        si = lax.broadcasted_iota(jnp.int32, (128, width), 0)
        sj = lax.broadcasted_iota(jnp.int32, (128, width), 1)
        return lambda dd: jnp.where((si < count) & (sj == si + dd * step), 1.0, 0.0).astype(BF)

    norm_pick, bias_pick = picks(D, 96, 96), picks(128, 16, 16)
    norm_acc = jnp.zeros((16, D), F32)
    bias_acc = jnp.zeros((32, 128), F32)
    for zi in range(4):
        for yi in range(2):
            dd = 2 * zi + yi
            norm_acc = norm_acc + dot(M[c, x, yi, zi].reshape(16, 128).astype(BF), norm_pick(dd), NN)
            bias_acc = bias_acc + dot(M[:, :, yi, zi, 1].reshape(32, 128).astype(BF), bias_pick(dd), NN)
    NB[0] = norm_acc[0:8]
    for tt in range(4):
        row = (tt % 2 * 2 + tt // 2) * 8
        for r in range(6):
            NB[1, tt : tt + 1, r * 128 : r * 128 + 128] = bias_acc[row + r : row + r + 1]

    fin(3)
    pl.loop(5, 6)(attn_fwd)
    last_step(2)
    ready(2)
    ready(3)

    igrad[...] = dot(CTX[...], mat(3), NT)

    def ln_rows(i):
        return pl.ds(pl.multiple_of(i * 128, 128), 128)

    g1, b1 = NB[0, 0:1, :], NB[0, 1:2, :]
    g2, b2 = NB[0, 2:3, :], NB[0, 3:4, :]

    @pl.loop(0, 4)
    def _(i):
        rs = ln_rows(i)
        r = hid[rs, :].astype(F32) + igrad[rs, :]
        cen = r - jnp.mean(r, axis=1, keepdims=True)
        rstd = lax.rsqrt(jnp.mean(cen * cen, axis=1, keepdims=True) + EPSILON)
        xh = cen * rstd
        XH[rs, :] = xh
        RS1[rs, :] = rstd
        FI[rs, :] = (xh * g1 + b1).astype(BF)

    fin(4)
    for tt in range(4):
        pre = dot(FI[...], mat(4 + tt), NN) + NB[1, tt : tt + 1, :]
        cdf = 0.5 * (1.0 + lax.erf(pre * math.sqrt(0.5)))
        ACT[tt] = (pre * cdf).astype(BF)
        GP[tt] = (cdf + pre * (jnp.exp(-0.5 * pre * pre) * (1.0 / math.sqrt(2.0 * math.pi)))).astype(BF)

    last_step(3)
    ready(4)

    def half_mat(m, h):
        return W[m, :, :, :, :, h * HALF : h * HALF + HALF].reshape(D, HALF)

    acc = dot(ACT[0, :, 0:HALF], half_mat(8, 0), NT)
    for tt in range(1, 4):
        acc = acc + dot(ACT[tt, :, 0:HALF], half_mat(8 + tt, 0), NT)
    igrad[...] = acc
    last_ready()
    acc = dot(ACT[0, :, HALF:D], half_mat(8, 1), NT)
    for tt in range(1, 4):
        acc = acc + dot(ACT[tt, :, HALF:D], half_mat(8 + tt, 1), NT)
    igrad[...] += acc

    V[...] = jnp.zeros_like(V)
    load_cot.wait()

    @pl.loop(0, 4)
    def _(i):
        rs = ln_rows(i)
        r = XH[rs, :] * g1 + b1 + igrad[rs, :]
        cen = r - jnp.mean(r, axis=1, keepdims=True)
        rstd = lax.rsqrt(jnp.mean(cen * cen, axis=1, keepdims=True) + EPSILON)
        n2 = cen * rstd
        mixed[rs, :] = (n2 * g2 + b2).astype(BF)
        co = cot[rs, :].astype(F32)
        e = co * g2
        gr = rstd * (e - jnp.mean(e, axis=1, keepdims=True) - n2 * jnp.mean(e * n2, axis=1, keepdims=True))
        igrad[rs, :] = gr
        GF[rs, :] = gr.astype(BF)
        V[2:3, :] += jnp.sum(co * n2, axis=0, keepdims=True)
        V[3:4, :] += jnp.sum(co, axis=0, keepdims=True)

    save_mixed.start()

    def sq(r, xx):
        if r < 2:
            return SQ.at[r, xx]
        return W.at[8 + 2 * (r // 2 - 1) + xx, :, :, :, :, pl.ds((r % 2) * HALF, HALF)]

    def pb(r, xx, *rest):
        if r < 4:
            return PB.at[(r, xx) + rest]
        rest = rest + (slice(None),) * (4 - len(rest))
        return W.at[(4 + xx,) + rest + (pl.ds((r % 2) * HALF, HALF),)]

    def pb_all(r, *rest):
        if r < 4:
            return PB.at[(r, slice(None)) + rest]
        rest = rest + (slice(None),) * (4 - len(rest))
        return W.at[(pl.ds(4, 2),) + rest + (pl.ds((r % 2) * HALF, HALF),)]

    def b_sib(r, xx):
        return rc(sq(r, xx), SR.at[SIB_SLOT[r], xx], qs.at[r, xx], qr.at[r, xx], sib)

    ALL = slice(None)

    def b_a(r):
        return rc(pb(r, ox, ALL, ALL, 0), RA.at[r % SLOTS], as_.at[r], ar.at[r], xn)

    def b_b(r):
        return rc(pb_all(r, ALL, oy, 1), RB.at[r % SLOTS], bs.at[r], br.at[r], yn)

    def b_a2(r, k):
        dst = RO.at[r, 0] if k == 0 else RA2.at[r % SLOTS, k - 1]
        return rc(pb(r, x, zz[k], oy, 0), dst, a2s.at[r, k], a2r.at[r, k], yn)

    def b_b2(r, k):
        dst = RO.at[r, 1] if k == 0 else RB2.at[r % SLOTS, k - 1]
        return rc(pb(r, ox, zz[k], y, 1), dst, b2s.at[r, k], b2r.at[r, k], xn)

    def b_z(r, k):
        return rc(pb(r, x, zz[k], y), RZ.at[r, k - 1], rzs.at[r, k - 1], rzr.at[r, k - 1], zn[k])

    def zl(way, tgt, xx, recv=False):
        dst = (RU if way == 0 else RD).at[tgt, xx]
        dev = up_dev if way == 0 else down_dev
        return rc(PB.at[0, xx, tgt], dst, zls.at[way, tgt, xx], zlr.at[way, tgt, xx], dev)

    def zl_sends(way, tgt):
        return z < tgt if way == 0 else z > tgt

    def zl_got(way, tgt):
        return (z > 0) & (z <= tgt) if way == 0 else (z < 3) & (z >= tgt)

    def zl_first():
        for tgt in range(3):
            for xx in range(2):
                pl.when(z == 0)(lambda: zl(0, 3 - tgt, xx).start())
                pl.when(z == 3)(lambda: zl(1, tgt, xx).start())

    def zl_pass(way, at, tgt):
        for xx in range(2):
            @pl.when(z == at)
            def _():
                zl(way, tgt, xx).wait_recv()
                add(PB.at[0, xx, tgt], (RU if way == 0 else RD).at[tgt, xx])
                zl(way, tgt, xx).start()

    def zl_last():
        for way in range(2):
            for tgt in range(4):
                @pl.when((z == tgt) & ((z > 0) if way == 0 else (z < 3)))
                def _():
                    for xx in range(2):
                        zl(way, tgt, xx).wait_recv()
                        add(PB.at[0, xx, tgt], (RU if way == 0 else RD).at[tgt, xx])

    def b0(i):
        src, dst, dev = (
            (PB.at[0, ox, z, :, 0], R0.at[0], xn),
            (PB.at[0, :, z, oy, 1], R0.at[1], yn),
            (PB.at[0, x, z, oy, 0], R0.at[2, 0], yn),
            (PB.at[0, ox, z, y, 1], R0.at[2, 1], xn),
        )[i]
        return rc(src, dst, z0s.at[i], z0r.at[i], dev)

    def xy0_first():
        b0(0).start()
        b0(1).start()

    def xy0_second():
        b0(0).wait_recv()
        add(PB.at[0, x, z, :, 0], R0.at[0])
        b0(2).start()
        b0(1).wait_recv()
        add(PB.at[0, :, z, y, 1], R0.at[1])
        b0(3).start()

    def xy0_last():
        b0(2).wait_recv()
        b0(3).wait_recv()
        tot = PB[0, x, z, y].astype(F32) + R0[2].astype(F32)
        g_down[:, 0:HALF] = tot.reshape(96, HALF)

    def rs0_drain():
        for xx in range(2):
            b_sib(0, xx).wait_send()
        for i in range(4):
            b0(i).wait_send()
        for way in range(2):
            for tgt in range(4):
                for xx in range(2):
                    pl.when(zl_sends(way, tgt))(lambda: zl(way, tgt, xx).wait_send())

    def credit(sem, dev, r):
        if r + SLOTS < PIECES:
            pl.semaphore_signal(sem, inc=1, device_id=dev, device_id_type=pl.DeviceIdType.MESH)

    def need(sem, r):
        if r >= SLOTS + (sem is not c_sib):
            pl.semaphore_wait(sem, 1)

    def part(r, xx, core):
        if r < 4:
            src = ACT if r < 2 else GP
            lhs = GF if r < 2 else FI
            h = r % 2
            return dot(lhs[...], src[2 * xx + core, :, h * HALF : h * HALF + HALF], TN)
        raise ValueError

    def part_attn(m, xx):
        if m < 3:
            return dot(hid[...], ACT[(1, 0, 2)[m], :, xx * HALF : xx * HALF + HALF], TN)
        return dot(GF[...], CTX[:, xx * HALF : xx * HALF + HALF], TN)

    def gen_sib(r):
        need(c_sib, r)
        for xx in range(2):
            if r < 4:
                sq(r, xx)[...] = part(r, xx, oc).astype(BF).reshape(4, 2, 2, 48, HALF)
            else:
                for core in range(2):
                    @pl.when(oc == core)
                    def _():
                        sq(r, xx)[...] = part_attn(2 * core + 5 - r, xx).astype(BF).reshape(4, 2, 2, 48, HALF)
            b_sib(r, xx).start()

    def own_part(r, xx, grad):
        v = grad.reshape(4, 2, 2, 48, HALF) + SR[SIB_SLOT[r], xx].astype(F32)
        pb(r, xx)[...] = v.astype(BF)

    def gen_own(r):
        for xx in range(2):
            b_sib(r, xx).wait_recv()
            if r < 4:
                own_part(r, xx, part(r, xx, c))
            else:
                for core in range(2):
                    @pl.when(c == core)
                    def _():
                        own_part(r, xx, part_attn(2 * core + 5 - r, xx))
        credit(c_sib, sib, r)
        if r == 0:
            zl_first()
            return
        need(c_a, r)
        b_a(r).start()
        need(c_b, r)
        b_b(r).start()

    def add(dst, src):
        dst[...] = (dst[...].astype(F32) + src[...].astype(F32)).astype(BF)

    def st1(r):
        q = r % SLOTS
        b_a(r).wait_recv()
        add(pb(r, x, ALL, ALL, 0), RA.at[q])
        credit(c_a, xn, r)
        need(c_a2, r)
        for k in (2, 3, 1):
            b_a2(r, k).start()
        b_b(r).wait_recv()
        add(pb_all(r, ALL, y, 1), RB.at[q])
        credit(c_b, yn, r)
        need(c_b2, r)
        for k in (2, 3, 1):
            b_b2(r, k).start()

    def st2o(r):
        b_a2(r, 0).start()
        b_b2(r, 0).start()

    def st2(r):
        q = r % SLOTS
        for k in (2, 3, 1):
            b_a2(r, k).wait_recv()
            add(pb(r, x, zz[k], y, 0), RA2.at[q, k - 1])
            b_b2(r, k).wait_recv()
            add(pb(r, x, zz[k], y, 1), RB2.at[q, k - 1])
            b_z(r, k).start()
        credit(c_a2, yn, r)
        credit(c_b2, xn, r)

    def fx(r):
        m = g_attn.at[2 * c + 5 - r]
        return rc(m, m, es.at[r - 1], er.at[r - 1], sib)

    def st3(r):
        tot = pb(r, x, z, y)[...].astype(F32)
        for k in (2, 3, 1):
            b_z(r, k).wait_recv()
            tot = tot + RZ[r, k - 1].astype(F32)
        b_a2(r, 0).wait_recv()
        b_b2(r, 0).wait_recv()
        tot = (tot + RO[r].astype(F32)).reshape(96, HALF)
        h = r % 2
        if r < 2:
            g_down[:, h * HALF : h * HALF + HALF] = tot
        elif r < 4:
            g_up[:, h * HALF : h * HALF + HALF] = tot
        else:
            g_attn[2 * c + 5 - r] = tot
            fx(r).start()

    def rs_drain(r):
        for xx in range(2):
            b_sib(r, xx).wait_send()
        b_a(r).wait_send()
        b_b(r).wait_send()
        for k in range(4):
            b_a2(r, k).wait_send()
            b_b2(r, k).wait_send()
        for k in (1, 2, 3):
            b_z(r, k).wait_send()

    def gact(h):
        ls = slice(h * HALF, h * HALF + HALF)
        for tt in range(4):
            ga = dot(GF[...], half_mat(8 + tt, h), NN)
            gp = (ga * GP[tt, :, ls].astype(F32)).astype(BF)
            GP[tt, :, ls] = gp
            V[4 + tt : 5 + tt, ls] = jnp.sum(gp.astype(F32), axis=0, keepdims=True)

    gen_sib(1)
    for p in range(PIECES - 1):
        drain(p)
    last_drain()
    gen_own(1)
    gact(0)
    gen_sib(2)
    gen_sib(0)
    gen_own(2)
    gen_own(0)
    gact(1)
    gen_sib(3)
    st1(1)
    zl_pass(0, 1, 3)
    zl_pass(1, 2, 0)

    acc = dot(GP[0], mat(4), NT)
    for tt in range(1, 4):
        acc = acc + dot(GP[tt], mat(4 + tt), NT)
    igrad[...] += acc
    gen_own(3)

    @pl.loop(0, 4)
    def _(i):
        rs = ln_rows(i)
        gn = igrad[rs, :]
        xh = XH[rs, :]
        e = gn * g1
        gr = RS1[rs, :] * (e - jnp.mean(e, axis=1, keepdims=True) - xh * jnp.mean(e * xh, axis=1, keepdims=True))
        igrad[rs, :] = gr
        GF[rs, :] = gr.astype(BF)
        V[0:1, :] += jnp.sum(gn * xh, axis=0, keepdims=True)
        V[1:2, :] += jnp.sum(gn, axis=0, keepdims=True)

    vc = [
        rc(V, VR.at[0], vs.at[0], vr.at[0], sib),
        rc(V, VR.at[1], vs.at[1], vr.at[1], xn),
        rc(V, VR.at[2], vs.at[2], vr.at[2], yn),
    ] + [rc(V, VR.at[2 + k], vs.at[2 + k], vr.at[2 + k], zn[k]) for k in (1, 2, 3)]

    def v_step(i):
        vc[i].wait()
        V[...] += VR[i]

    vc[0].start()
    zl_pass(0, 1, 2)
    zl_pass(1, 2, 1)
    zl_pass(0, 2, 3)
    zl_pass(1, 1, 0)

    FI[...] = dot(GF[...], mat(3), NN).astype(BF)
    v_step(0)
    vc[1].start()

    def attn_bwd(hp):
        ls = pair_lanes(hp)
        fl = flips(hp)
        kk = jnp.where(fl, KVO[0, :, ls], QKV[1, :, ls])
        vv = jnp.where(fl, KVO[1, :, ls], QKV[2, :, ls])
        q = QKV[0, :, ls]
        do = FI[:, ls]
        dvs, dqs, dks = [], [], []
        for e in range(2):
            a = AT[2 * hp + e]
            dvs.append(dot(a, do, TN))
            de = jnp.where(low_lane if e == 0 else ~low_lane, do, jnp.zeros_like(do))
            dp = dot(de, vv, NT)
            af = a.astype(F32)
            w = af * dp
            gs = (w - af * jnp.sum(w, axis=1, keepdims=True)).astype(BF)
            dqs.append(dot(gs, kk, NN))
            dks.append(dot(gs, q, TN))
        ACT[0, :, ls] = (jnp.where(low_lane, dqs[0], dqs[1]) * 0.125).astype(BF)
        GP[0, :, ls] = (jnp.where(low_lane, dks[0], dks[1]) * 0.125).astype(BF)
        GP[1, :, ls] = jnp.where(low_lane, dvs[0], dvs[1]).astype(BF)

    pl.loop(0, 2)(attn_bwd)
    st1(2)
    st2(1)
    pl.loop(2, 4)(attn_bwd)
    st1(3)
    st2(2)
    st2o(1)
    st2o(2)
    pl.loop(4, 6)(attn_bwd)
    dkvc = rc(GP.at[pl.ds(0, 2)], DKVR, es.at[2], er.at[2], sib)
    dkvc.start()
    gen_sib(4)
    v_step(1)
    vc[2].start()
    dkvc.wait()

    def pick(hp):
        ls = pair_lanes(hp)
        fl = flips(hp)
        ACT[1, :, ls] = jnp.where(fl, DKVR[0, :, ls], GP[0, :, ls])
        ACT[2, :, ls] = jnp.where(fl, DKVR[1, :, ls], GP[1, :, ls])

    pl.loop(0, 6)(pick)

    gen_own(4)
    gen_sib(5)
    zl_last()
    xy0_first()
    st2(3)
    v_step(2)
    for k in (1, 2, 3):
        vc[2 + k].start()
    acc = dot(ACT[0], mat(1), NT)
    for m in (1, 2):
        acc = acc + dot(ACT[m], mat((1, 0, 2)[m]), NT)
    igrad[...] += acc
    st2o(3)
    st1(4)
    gen_own(5)
    st2(4)
    xy0_second()
    st2o(4)
    for r in (1, 2, 3):
        st3(r)
    st1(5)
    st2o(5)
    xy0_last()
    st2(5)
    st3(4)
    st3(5)
    for k in (1, 2, 3):
        vc[2 + k].wait()
    g_misc[...] = V[...] + VR[3] + VR[4] + VR[5]
    save_mixed.wait()
    rs0_drain()
    for r in range(1, PIECES):
        rs_drain(r)
    for cp in mz:
        cp.wait_send()
    mx.wait_send()
    my.wait_send()
    md.wait_send()
    axc.wait_send()
    kvc.wait_send()
    fx(4).wait()
    fx(5).wait()


def finish_kernel(
    mixed, igrad, ga, gu, gd, gm, o_mixed, o_igrad, o_qkv, o_out, o_up, o_bias, o_down, o_norm, tmp, v_igrad, v_mixed, v_up, v_down, sem
):
    parts = [(igrad, v_igrad, o_igrad, i * 128, 128) for i in range(4)]
    parts += [(mixed, v_mixed, o_mixed, i * 256, 256) for i in range(2)]
    parts += [(gu, v_up, o_up, 0, 96), (gd, v_down, o_down, 0, 96)]
    loads, stores = [], []
    for i, (src, mid, dst, at, n) in enumerate(parts):
        rows = pl.ds(at, n)
        loads.append(pltpu.make_async_copy(src.at[rows], mid.at[rows], sem.at[0, i]))
        stores.append(pltpu.make_async_copy(mid.at[rows], dst.at[rows], sem.at[1, i]))
    for cp in loads:
        cp.start()
    dd = lax.axis_index("dp")
    t = lax.axis_index("tensor")
    first = jnp.full((96, 192), lax.rem(t, 2), jnp.int32) == 0
    for m in range(4):
        v = jnp.where(first, ga[m, :, 0:192], ga[m, :, 192:HALF])
        if m < 3:
            o_qkv[(1, 0, 2)[m]] = v
        else:
            o_out[...] = v.T
    exact = dict(preferred_element_type=F32, precision=lax.Precision.HIGHEST)
    si = lax.broadcasted_iota(jnp.int32, (D, 128), 0)
    sj = lax.broadcasted_iota(jnp.int32, (D, 128), 1)
    pick = jnp.where(si == sj + dd * 96, 1.0, 0.0).astype(F32)
    for load, store in zip(loads, stores):
        load.wait()
        store.start()
    sub = lax.broadcasted_iota(jnp.int32, (8, D), 0)
    norm = lax.dot_general(gm[...], pick, NN, **exact)
    o_norm[...] = jnp.sum(jnp.where(sub[:, 0:128] == t, norm, 0.0), axis=0, keepdims=True)[:, 0:96]
    row = jnp.sum(jnp.where(sub == 4 + t, gm[...], 0.0), axis=0, keepdims=True)
    for r in range(6):
        tmp[r : r + 1] = row[:, r * 128 : r * 128 + 128]
    pick = jnp.where(si[0:128] == sj[0:128] + dd * 16, 1.0, 0.0).astype(F32)
    o_bias[...] = lax.dot_general(tmp[...], pick, NN, **exact)[0:6, 0:16]
    for cp in stores:
        cp.wait()


def scratch():
    vm = pltpu.VMEM
    dma = lambda *s: pltpu.SemaphoreType.DMA(s)
    n = PIECES
    return [
        vm((ROWS, D), BF), vm((ROWS, D), BF), vm((ROWS, D), BF), vm((12, 4, 2, 2, 48, D), BF), vm((4, 96, 256), BF), vm((2, 96, 256), BF), vm((3, ROWS, D), BF), vm((2, ROWS, D), BF),
        vm((12, ROWS, ROWS), BF), vm((ROWS, D), BF), vm((ROWS, D), F32), vm((ROWS, 1), F32), vm((ROWS, D), BF),
        vm((4, ROWS, D), BF), vm((4, ROWS, D), BF), vm((ROWS, D), BF), vm((2, ROWS, D), BF),
        vm((2, 2, 2, 4, 2, 8, 128), F32), vm((2, 8, D), F32), vm((8, D), F32), vm((6, 8, D), F32),
        vm((2, 2, 4, 2, 2, 48, HALF), BF), vm((SLOTS, 2, 4, 2, 2, 48, HALF), BF), vm((4, 2, 4, 2, 2, 48, HALF), BF),
        vm((SLOTS, 4, 2, 48, HALF), BF), vm((SLOTS, 2, 4, 48, HALF), BF), vm((SLOTS, 3, 48, HALF), BF),
        vm((SLOTS, 3, 48, HALF), BF), vm((n, 2, 48, HALF), BF), vm((n, 3, 2, 48, HALF), BF),
        vm((4, 2, 2, 2, 48, HALF), BF), vm((4, 2, 2, 2, 48, HALF), BF), vm((3, 2, 48, HALF), BF),
        dma(n, 3), dma(n, 3), dma(n, 4), dma(n, 4), dma(n, 4), dma(n, 4), dma(n, 2), dma(n, 2), dma(n, 4), dma(n, 4),
        dma(6), dma(6), dma(5), dma(5),
        dma(n, 2), dma(n, 2), dma(n), dma(n), dma(n), dma(n), dma(n, 4), dma(n, 4), dma(n, 4), dma(n, 4), dma(n, 3), dma(n, 3), dma(6), dma(6),
        dma(2, 3, 2), dma(2, 3, 2), dma(7, 2), dma(7, 2), dma(2, 4, 2), dma(2, 4, 2), dma(4), dma(4), dma(3),
        pltpu.SemaphoreType.REGULAR, pltpu.SemaphoreType.REGULAR, pltpu.SemaphoreType.REGULAR,
        pltpu.SemaphoreType.REGULAR, pltpu.SemaphoreType.REGULAR,
    ]


def whole_layer(
    hidden_in, qkv_weight, out_weight, up_weight, up_bias, down_weight, norm_params, cotangent, head_swap, slot_kind
):
    any_ = pl.BlockSpec(memory_space=pl.ANY)
    vmem = pl.BlockSpec(memory_space=pltpu.VMEM)
    smem = pl.BlockSpec(memory_space=pltpu.SMEM)
    sds = jax.ShapeDtypeStruct
    mixed, igrad, ga, gu, gd, gm = pl.pallas_call(
        layer_kernel,
        out_shape=(
            sds((ROWS, D), BF), sds((ROWS, D), F32), sds((4, 96, HALF), F32),
            sds((96, D), F32), sds((96, D), F32), sds((8, D), F32),
        ),
        in_specs=[any_] + [vmem] * 6 + [any_] + [smem] * 2,
        out_specs=(any_,) + (vmem,) * 5,
        scratch_shapes=scratch(),
        compiler_params=pltpu.CompilerParams(
            collective_id=0, has_side_effects=True, vmem_limit_bytes=63 * 2**20
        ),
        name="layer",
    )(
        hidden_in, qkv_weight, out_weight, up_weight, up_bias, down_weight.T, norm_params, cotangent, head_swap, slot_kind
    )
    *outs, bias_grad, down_grad, norm_grad = pl.pallas_call(
        finish_kernel,
        out_shape=(
            sds((ROWS, D), BF), sds((ROWS, D), F32), sds((3, 96, 192), F32), sds((192, 96), F32),
            sds((96, D), F32), sds((6, 16), F32), sds((96, D), F32), sds((1, 96), F32),
        ),
        in_specs=[any_, any_, vmem, any_, any_, vmem],
        out_specs=(any_, any_, vmem, vmem, any_, vmem, any_, vmem),
        scratch_shapes=[
            pltpu.VMEM((8, 128), F32), pltpu.VMEM((ROWS, D), F32), pltpu.VMEM((ROWS, D), BF),
            pltpu.VMEM((96, D), F32), pltpu.VMEM((96, D), F32), pltpu.SemaphoreType.DMA((2, 8)),
        ],
        compiler_params=pltpu.CompilerParams(vmem_limit_bytes=63 * 2**20),
        name="finish",
    )(mixed, igrad, ga, gu, gd, gm)
    return (*outs, bias_grad, down_grad.T, norm_grad)


def norm_rows(residual, scales, offset):
    center = residual - jnp.mean(residual, axis=-1, keepdims=True)
    spread = jnp.mean(center * center, axis=-1, keepdims=True)
    return center * lax.rsqrt(spread + EPSILON) * scales + offset


def smooth_gate(values):
    return jax.nn.gelu(values, approximate=False)


def arrange(queries, keys_in, values_in, slot_type, local_swaps):
    slot_len, head_count, head_size = queries.shape
    half_len = slot_len // 2
    quarter = half_len // 2
    shape_four = (2, half_len, head_count, head_size)
    query_half = queries.reshape(shape_four)
    key_half = keys_in.reshape(shape_four)
    value_half = values_in.reshape(shape_four)
    flipped = (local_swaps * slot_type == 1)[None, None, :, None]
    key_pick = jnp.where(flipped, key_half[::-1], key_half)
    value_pick = jnp.where(flipped, value_half[::-1], value_half)
    blocks = jnp.arange(half_len, dtype=jnp.int32) // quarter
    matching = (
        jnp.bitwise_xor(blocks[None, :, None], local_swaps[:, None, None]) == blocks[None, None, :]
    )
    allowed = jnp.logical_or(slot_type == 1, matching)
    return (query_half, key_pick, value_pick, allowed, flipped)


def masked_scores(query_half, key_pick, allowed):
    scale = 1.0 / math.sqrt(query_half.shape[-1])
    scores = (
        jnp.einsum("jqhd,jkhd->jhqk", query_half, key_pick, preferred_element_type=jnp.float32)
        * scale
    )
    return jnp.where(allowed[None], scores, NEGATIVE)


def slot_forward(inputs, local_swaps):
    queries, keys_in, values_in, slot_type = inputs
    query_half, key_pick, value_pick, allowed, flipped = arrange(
        queries, keys_in, values_in, slot_type, local_swaps
    )
    scores = masked_scores(query_half, key_pick, allowed)
    largest = jnp.max(scores, axis=-1, keepdims=True)
    powers = jnp.exp(scores - largest)
    totals = jnp.sum(powers, axis=-1, keepdims=True)
    attention = (powers / totals).astype(jnp.bfloat16)
    context = jnp.einsum(
        "jhqk,jkhd->jqhd", attention, value_pick, preferred_element_type=jnp.float32
    )
    return (context.astype(jnp.bfloat16).reshape(queries.shape[0], -1), largest + jnp.log(totals))


def slot_backward(inputs, local_swaps):
    queries, keys_in, values_in, slot_type, log_totals, grad_out = inputs
    slot_len, head_count, head_size = queries.shape
    scale = 1.0 / math.sqrt(head_size)
    query_half, key_pick, value_pick, allowed, flipped = arrange(
        queries, keys_in, values_in, slot_type, local_swaps
    )
    attention = jnp.exp(masked_scores(query_half, key_pick, allowed) - log_totals)
    grad_half = grad_out.reshape(query_half.shape)
    grad_vpick = jnp.einsum(
        "jhqk,jqhd->jkhd",
        attention.astype(jnp.bfloat16),
        grad_half,
        preferred_element_type=jnp.float32,
    ).astype(jnp.bfloat16)
    grad_attention = jnp.einsum(
        "jqhd,jkhd->jhqk", grad_half, value_pick, preferred_element_type=jnp.float32
    )
    row_dots = jnp.sum(attention * grad_attention, axis=-1, keepdims=True)
    grad_scores = (attention * (grad_attention - row_dots)).astype(jnp.bfloat16)
    grad_query = (
        jnp.einsum("jhqk,jkhd->jqhd", grad_scores, key_pick, preferred_element_type=jnp.float32)
        * scale
    ).astype(jnp.bfloat16)
    grad_kpick = (
        jnp.einsum("jhqk,jqhd->jkhd", grad_scores, query_half, preferred_element_type=jnp.float32)
        * scale
    ).astype(jnp.bfloat16)
    grad_key = jnp.where(flipped, grad_kpick[::-1], grad_kpick)
    grad_value = jnp.where(flipped, grad_vpick[::-1], grad_vpick)
    return (
        grad_query.reshape(slot_len, -1),
        grad_key.reshape(slot_len, -1),
        grad_value.reshape(slot_len, -1),
    )


def per_device(
    hidden_in,
    qkv_weight,
    out_weight,
    up_weight,
    up_bias,
    down_weight,
    norm_params,
    cotangent,
    head_swap,
    slot_kind,
):
    tensor_count = lax.axis_size("tensor")
    tensor_rank = lax.axis_index("tensor")
    heads_here = head_swap.shape[0] // tensor_count
    local_swaps = lax.dynamic_slice_in_dim(head_swap, tensor_rank * heads_here, heads_here)
    qkv_low = qkv_weight.astype(jnp.bfloat16)
    out_low = out_weight.astype(jnp.bfloat16)
    norm_low = norm_params.astype(jnp.bfloat16)
    up_low = up_weight.astype(jnp.bfloat16)
    bias_low = up_bias.astype(jnp.bfloat16)
    down_low = down_weight.astype(jnp.bfloat16)
    qkv_full, out_full, norm_full = (
        lax.all_gather(qkv_low, "dp", axis=1, tiled=True),
        lax.all_gather(out_low, "dp", axis=1, tiled=True),
        lax.all_gather(norm_low, "dp", axis=1, tiled=True),
    )
    norm_gain = norm_full.astype(jnp.float32)
    full_in = lax.all_gather(hidden_in, "tensor", axis=0, tiled=True)
    group_rows = full_in.shape[0]
    local_width = qkv_full.shape[2]
    head_size = local_width // heads_here
    slot_count = group_rows // LONG_LEN

    def by_slot(rows):
        return rows.reshape(slot_count, LONG_LEN, heads_here, head_size)

    projected = jnp.einsum(
        "td,cde->cte", full_in, qkv_full, preferred_element_type=jnp.float32
    ).astype(jnp.bfloat16)
    context, log_totals = lax.map(
        partial(slot_forward, local_swaps=local_swaps),
        (by_slot(projected[0]), by_slot(projected[1]), by_slot(projected[2]), slot_kind),
    )
    context = context.reshape(group_rows, local_width)
    rows = context
    attn_share = lax.psum_scatter(
        jnp.dot(rows, out_full, preferred_element_type=jnp.float32).astype(jnp.bfloat16),
        "tensor",
        scatter_dimension=0,
        tiled=True,
    ).astype(jnp.float32)
    resid_one = hidden_in.astype(jnp.float32) + attn_share
    normed_one, norm_one_back = jax.vjp(norm_rows, resid_one, norm_gain[0], norm_gain[1])
    up_full, bias_full, down_full = (
        lax.all_gather(up_low, "dp", axis=0, tiled=True),
        lax.all_gather(bias_low, "dp", axis=1, tiled=True),
        lax.all_gather(down_low, "dp", axis=1, tiled=True),
    )
    ffn_in = lax.all_gather(normed_one.astype(jnp.bfloat16), "tensor", axis=0, tiled=True)
    pre = jnp.dot(ffn_in, up_full, preferred_element_type=jnp.float32) + bias_full.reshape(
        -1
    ).astype(jnp.float32)
    act_value, gate_back = jax.vjp(smooth_gate, pre)
    act = act_value.astype(jnp.bfloat16)
    rows = act
    ffn_share = lax.psum_scatter(
        jnp.dot(rows, down_full, preferred_element_type=jnp.float32).astype(jnp.bfloat16),
        "tensor",
        scatter_dimension=0,
        tiled=True,
    ).astype(jnp.float32)
    normed_two, norm_two_back = jax.vjp(
        norm_rows, normed_one + ffn_share, norm_gain[2], norm_gain[3]
    )
    mixed = normed_two.astype(jnp.bfloat16)
    grad_resid_two, grad_gain_two, grad_bias_two = norm_two_back(cotangent.astype(jnp.float32))
    grad_ffn = lax.all_gather(grad_resid_two.astype(jnp.bfloat16), "tensor", axis=0, tiled=True)
    grad_down = jnp.einsum("tf,td->fd", act, grad_ffn, preferred_element_type=jnp.float32)
    grad_act = jnp.einsum("td,fd->tf", grad_ffn, down_full, preferred_element_type=jnp.float32)
    grad_pre = gate_back(grad_act)[0].astype(jnp.bfloat16)
    grad_up = jnp.einsum("td,tf->df", ffn_in, grad_pre, preferred_element_type=jnp.float32)
    grad_bias = jnp.sum(grad_pre.astype(jnp.float32), axis=0).reshape(bias_full.shape)
    rows = grad_pre
    grad_normed_one = grad_resid_two + lax.psum_scatter(
        jnp.einsum("tf,df->td", rows, up_full, preferred_element_type=jnp.float32).astype(
            jnp.bfloat16
        ),
        "tensor",
        scatter_dimension=0,
        tiled=True,
    ).astype(jnp.float32)
    grad_resid_one, grad_gain_one, grad_bias_one = norm_one_back(grad_normed_one)
    grad_attn = lax.all_gather(grad_resid_one.astype(jnp.bfloat16), "tensor", axis=0, tiled=True)
    grad_out = jnp.einsum("tw,td->wd", context, grad_attn, preferred_element_type=jnp.float32)
    grad_context = jnp.einsum(
        "td,wd->tw", grad_attn, out_full, preferred_element_type=jnp.float32
    ).astype(jnp.bfloat16)
    grad_query, grad_key, grad_value = lax.map(
        partial(slot_backward, local_swaps=local_swaps),
        (
            by_slot(projected[0]),
            by_slot(projected[1]),
            by_slot(projected[2]),
            slot_kind,
            log_totals,
            grad_context.reshape(slot_count, LONG_LEN, local_width),
        ),
    )
    grad_proj = jnp.stack([grad_query, grad_key, grad_value]).reshape(3, group_rows, local_width)
    grad_qkv = jnp.einsum("td,cte->cde", full_in, grad_proj, preferred_element_type=jnp.float32)
    grad_in_part = jnp.einsum(
        "cte,cde->td", grad_proj, qkv_full, preferred_element_type=jnp.float32
    )
    norm_part = jnp.stack([grad_gain_one, grad_bias_one, grad_gain_two, grad_bias_two])
    grad_in_share, norm_row = (
        lax.psum_scatter(
            grad_in_part.astype(jnp.bfloat16), "tensor", scatter_dimension=0, tiled=True
        ).astype(jnp.float32),
        lax.psum_scatter(
            norm_part.astype(jnp.bfloat16), "tensor", scatter_dimension=0, tiled=True
        ).astype(jnp.float32),
    )
    input_grad = grad_resid_one + grad_in_share
    qkv_grad, out_grad, up_grad, up_bias_grad, down_grad, norm_grad = (
        lax.psum_scatter(grad_qkv, "dp", scatter_dimension=1, tiled=True),
        lax.psum_scatter(grad_out, "dp", scatter_dimension=1, tiled=True),
        lax.psum_scatter(grad_up, "dp", scatter_dimension=0, tiled=True),
        lax.psum_scatter(grad_bias, "dp", scatter_dimension=1, tiled=True),
        lax.psum_scatter(grad_down, "dp", scatter_dimension=1, tiled=True),
        lax.psum_scatter(norm_row, "dp", scatter_dimension=1, tiled=True),
    )
    return (mixed, input_grad, qkv_grad, out_grad, up_grad, up_bias_grad, down_grad, norm_grad)


def solution(mesh):
    placed = (
        P(("dp", "tensor"), None),
        P(None, "dp", "tensor"),
        P("tensor", "dp"),
        P("dp", "tensor"),
        P("tensor", "dp"),
        P("tensor", "dp"),
        P(None, "dp"),
        P(("dp", "tensor"), None),
        P(),
        P("dp"),
    )
    planned = mesh.shape["dp"] == 8 and mesh.shape["tensor"] == 4
    return jax.shard_map(
        whole_layer if planned else per_device,
        mesh=mesh,
        in_specs=placed,
        out_specs=(
            P(("dp", "tensor"), None),
            P(("dp", "tensor"), None),
            P(None, "dp", "tensor"),
            P("tensor", "dp"),
            P("dp", "tensor"),
            P("tensor", "dp"),
            P("tensor", "dp"),
            P("tensor", "dp"),
        ),
        check_vma=False,
    )
```

```python
from functools import partial
import math

import jax
import jax.numpy as jnp
from jax import lax
from jax.experimental import pallas as pl
from jax.experimental.pallas import tpu as pltpu
from jax.sharding import PartitionSpec as P

LONG_LEN = 1024
EPSILON = 1e-05
NEGATIVE = -1e30

BF = jnp.bfloat16
F32 = jnp.float32
NN = (((1,), (0,)), ((), ()))
NT = (((1,), (1,)), ((), ()))
TN = (((0,), (0,)), ((), ()))
PIECES = 6
SLOTS = 3
SIB_SLOT = (2, 0, 1, 0, 1, 2)
ROWS = 512
D = 768
HALF = 384


def dot(a, b, dims):
    return lax.dot_general(a, b, dims, preferred_element_type=F32)


def layer_kernel(
    hid_in, qkv_w, out_w, up_w, up_b, down_w, norm_p, cot_in, swap, kind,
    mixed_out, igrad, g_attn, g_up, g_down, g_misc,
    hid, cot, mixed, W, SH, AX, QKV, KVO, AT, CTX, XH, RS1, FI, ACT, GP, GF, DKVR,
    M, NB, V, VR,
    SQ, SR, PB, RA, RB, RA2, RB2, RO, RZ, RU, RD, R0,
    zs, zr, xs, xr, ys, yr, hs, hr, ds_, dr, ms, mr, es, er,
    qs, qr, as_, ar, bs, br, a2s, a2r, b2s, b2r, rzs, rzr, vs, vr, ls_, lr, lds, ldr, zls, zlr, z0s, z0r, io,
    c_sib, c_a, c_b, c_a2, c_b2,
):
    d = lax.axis_index("dp")
    t = lax.axis_index("tensor")
    z, y = d // 2, lax.rem(d, 2)
    x, c = t // 2, lax.rem(t, 2)
    ox, oy, oc = 1 - x, 1 - y, 1 - c

    def zk(k):
        hi, lo = z // 2, lax.rem(z, 2)
        kh, kl = k // 2, k % 2
        h2 = hi if kh == 0 else 1 - hi
        l2 = lo if kl == 0 else 1 - lo
        return 2 * h2 + l2

    zz = [zk(k) for k in range(4)]
    sib = (d, 2 * x + oc)
    xn = (d, 2 * ox + c)
    yn = (2 * z + oy, t)
    zn = [(2 * zz[k] + y, t) for k in range(4)]

    def rc(src, dst, s, r, dev):
        return pltpu.make_async_remote_copy(
            src_ref=src, dst_ref=dst, send_sem=s, recv_sem=r,
            device_id=dev, device_id_type=pl.DeviceIdType.MESH,
        )

    load_hid = pltpu.make_async_copy(hid_in, hid, io.at[0])
    load_cot = pltpu.make_async_copy(cot_in, cot, io.at[1])
    save_mixed = pltpu.make_async_copy(mixed, mixed_out, io.at[2])
    load_hid.start()
    load_cot.start()

    bar = pltpu.get_barrier_semaphore()
    for dev in (sib, xn, yn, zn[1], zn[2], zn[3]):
        pl.semaphore_signal(bar, inc=1, device_id=dev, device_id_type=pl.DeviceIdType.MESH)

    def where(p, xx, core):
        if p < 2:
            return 2 * core + p, pl.multiple_of(xx * HALF, 128)
        if p < 4:
            return 4 + 2 * xx + core, (p - 2) * HALF
        return 8 + 2 * xx + core, (p - 4) * HALF

    def slab(p, xx, zi, yi, core=None):
        m, lane = where(p, xx, c if core is None else core)
        return W.at[m, zi, yi, :, :, pl.ds(lane, HALF)]

    def col(p, xx, yi, core=None):
        m, lane = where(p, xx, c if core is None else core)
        return W.at[m, :, yi, :, :, pl.ds(lane, HALF)]

    def hcol(p, xx, yi, half):
        m, lane = where(p, xx, c)
        return W.at[m, :, yi, half, :, pl.ds(lane, HALF)]

    def zcp(p, k, recv=False):
        s = slab(p, x, zz[k] if recv else z, y)
        return rc(s, s, zs.at[p, k - 1], zr.at[p, k - 1], zn[k])

    def xcp(p, k, recv=False):
        s = slab(p, ox if recv else x, zz[k], y)
        return rc(s, s, xs.at[p, k], xr.at[p, k], xn)

    def ycp(p, k, recv=False):
        s = slab(p, x, zz[k], oy if recv else y)
        return rc(s, s, ys.at[p, k], yr.at[p, k], yn)

    def acp(p, recv=False):
        s = hcol(p, ox, oy if recv else y, 0)
        return rc(s, s, hs.at[p, 0], hr.at[p, 0], yn)

    def bcp(p, recv=False):
        s = hcol(p, ox if recv else x, oy, 1)
        return rc(s, s, hs.at[p, 1], hr.at[p, 1], xn)

    groups = [(x, y), (ox, y), (x, oy), (ox, oy)]

    def dcp(p, g, recv=False):
        xx, yy = groups[g]
        s = col(p, xx, yy, oc if recv else c)
        return rc(s, s, ds_.at[p, g], dr.at[p, g], sib)

    last = PIECES - 1

    def lx(recv=False):
        s = slab(last, ox if recv else x, z, y)
        return rc(s, s, xs.at[last, 0], xr.at[last, 0], xn)

    def ly(recv=False):
        s = slab(last, x, z, oy if recv else y)
        return rc(s, s, ys.at[last, 0], yr.at[last, 0], yn)

    def lhalf(i, recv=False):
        if i == 0:
            xx, yy, dev = ox, oy if recv else y, yn
        else:
            xx, yy, dev = ox if recv else x, oy, xn
        m, lane = where(last, xx, c)
        s = W.at[m, z, yy, i, :, pl.ds(lane, HALF)]
        return rc(s, s, hs.at[last, i], hr.at[last, i], dev)

    def lcol(core, xx, zi):
        m, lane = where(last, xx, core)
        return W.at[m, zi, :, :, :, pl.ds(lane, HALF)]

    up_dev, down_dev = (d + 2, t), (d - 2, t)

    def line(way, j, xx, recv=False):
        zi = z - j if way == 0 else z + j
        s = lcol(c, xx, zi)
        i = j if recv else j + 1
        dev = up_dev if way == 0 else down_dev
        return rc(s, s, ls_.at[way, i - 1, xx], lr.at[way, i - 1, xx], dev)

    def ldc(way, j, xx, recv=False):
        zi = z - j if way == 0 else z + j
        s = lcol(oc if recv else c, xx, zi)
        i = 6 if j == 0 else way * 3 + j - 1
        return rc(s, s, lds.at[i, xx], ldr.at[i, xx], sib)

    def lsend(way, j):
        if way == 0:
            return (z < 3) & (z >= j)
        return (z > 0) & (z + j <= 3)

    def lgot(way, j):
        return z >= j if way == 0 else z + j <= 3

    def last_xy():
        lx(True).wait_recv()
        lhalf(0).start()
        ly(True).wait_recv()
        lhalf(1).start()

    def last_start():
        lhalf(0, True).wait_recv()
        lhalf(1, True).wait_recv()
        for xx in range(2):
            for way in range(2):
                pl.when(lsend(way, 0))(lambda: line(way, 0, xx).start())
        for xx in range(2):
            ldc(0, 0, xx).start()

    def last_step(j):
        for xx in range(2):
            for way in range(2):
                @pl.when(lgot(way, j))
                def _():
                    line(way, j, xx, True).wait_recv()
                    if j < 3:
                        pl.when(lsend(way, j))(lambda: line(way, j, xx).start())
                    ldc(way, j, xx).start()

    def last_ready():
        for xx in range(2):
            ldc(0, 0, xx, True).wait_recv()
            for way in range(2):
                for j in (1, 2, 3):
                    pl.when(lgot(way, j))(lambda: ldc(way, j, xx, True).wait_recv())

    def last_drain():
        lx().wait_send()
        ly().wait_send()
        lhalf(0).wait_send()
        lhalf(1).wait_send()
        for xx in range(2):
            ldc(0, 0, xx).wait_send()
            for way in range(2):
                for j in range(3):
                    pl.when(lsend(way, j))(lambda: line(way, j, xx).wait_send())
                for j in (1, 2, 3):
                    pl.when(lgot(way, j))(lambda: ldc(way, j, xx).wait_send())

    def own_xy(p):
        if p == last:
            lx().start()
            ly().start()
            return
        xcp(p, 0).start()
        ycp(p, 0).start()

    def own_z(p):
        for k in (1, 2, 3):
            zcp(p, k).start()

    def zf(p):
        for k in (1, 2, 3):
            zcp(p, k, True).wait_recv()
            xcp(p, k).start()
            ycp(p, k).start()
        dcp(p, 0).start()

    def xf(p):
        for k in range(4):
            xcp(p, k, True).wait_recv()
        acp(p).start()
        dcp(p, 1).start()
        for k in range(4):
            ycp(p, k, True).wait_recv()
        bcp(p).start()
        dcp(p, 2).start()

    def fin(p):
        acp(p, True).wait_recv()
        bcp(p, True).wait_recv()
        dcp(p, 3).start()

    def ready(p):
        for g in range(4):
            dcp(p, g, True).wait_recv()

    def drain(p):
        for k in (1, 2, 3):
            zcp(p, k).wait_send()
        for k in range(4):
            xcp(p, k).wait_send()
            ycp(p, k).wait_send()
        acp(p).wait_send()
        bcp(p).wait_send()
        for g in range(4):
            dcp(p, g).wait_send()

    SH[3, :, 0:192] = out_w[...].astype(BF).T
    for m, i in enumerate((1, 0, 2)):
        SH[m, :, 0:192] = qkv_w[i].astype(BF)
    W[4 + t, z, y] = up_w[...].astype(BF).reshape(2, 48, D)
    W[8 + t, z, y] = down_w[...].astype(BF).reshape(2, 48, D)
    M[c, x, y, z, 0, 0:4, 0:96] = norm_p[...].astype(BF).astype(F32)
    M[c, x, y, z, 1, 0:6, 0:16] = up_b[...].astype(BF).astype(F32)
    pl.semaphore_wait(bar, 6)
    axc = rc(SH.at[pl.ds(2 * oc, 2)], AX, es.at[0], er.at[0], sib)
    axc.start()
    own_xy(5)
    own_xy(2)
    mz = [rc(M.at[c, x, y, z], M.at[c, x, y, z], ms.at[k - 1], mr.at[k - 1], zn[k]) for k in (1, 2, 3)]
    for cp in mz:
        cp.start()
    axc.wait_recv()
    own_lane = pl.ds(pl.multiple_of(x * HALF, 128), HALF)
    first = jnp.full((96, 192), c, jnp.int32) == 0
    for i in range(2):
        mine, theirs = SH[2 * c + i, :, 0:192], AX[i, :, 0:192]
        both = jnp.concatenate([jnp.where(first, mine, theirs), jnp.where(first, theirs, mine)], axis=1)
        W[2 * c + i, z, y, :, :, own_lane] = both.reshape(2, 48, HALF)
        own_z(i)
        own_xy(i)

    for cp in mz:
        cp.wait_recv()
    mx = rc(M.at[c, x, y], M.at[c, x, y], ms.at[3], mr.at[3], xn)
    mx.start()
    zf(0)
    own_z(2)
    last_xy()
    own_xy(3)
    zf(1)
    own_z(3)
    own_xy(4)
    xf(0)
    xf(1)
    mx.wait_recv()
    my = rc(M.at[c, :, y], M.at[c, :, y], ms.at[4], mr.at[4], yn)
    my.start()
    last_start()
    own_z(4)
    zf(2)
    fin(0)
    ready(0)

    def mat(m):
        return W[m].reshape(D, D)

    load_hid.wait()
    QKV[1] = dot(hid[...], mat(0), NN).astype(BF)
    QKV[2] = dot(hid[...], mat(2), NN).astype(BF)
    kvc = rc(QKV.at[pl.ds(1, 2)], KVO, es.at[1], er.at[1], sib)
    kvc.start()
    fin(1)
    my.wait_recv()
    md = rc(M.at[c], M.at[c], ms.at[5], mr.at[5], sib)
    md.start()
    ready(1)
    QKV[0] = dot(hid[...], mat(1), NN).astype(BF)
    kvc.wait_recv()

    kd = kind[x]
    lane = lax.broadcasted_iota(jnp.int32, (1, 128), 1)
    keylane = lax.broadcasted_iota(jnp.int32, (1, ROWS), 1)
    low_lane = lane < 64

    def flips(hp):
        fa = kd * swap[2 * hp]
        fb = kd * swap[2 * hp + 1]
        return jnp.where(low_lane, jnp.full((1, 128), fa, jnp.int32), jnp.full((1, 128), fb, jnp.int32)) == 1

    def pair_lanes(hp):
        return pl.ds(pl.multiple_of(hp * 128, 128), 128)

    def attn_fwd(hp):
        ls = pair_lanes(hp)
        fl = flips(hp)
        kk = jnp.where(fl, KVO[0, :, ls], QKV[1, :, ls])
        vv = jnp.where(fl, KVO[1, :, ls], QKV[2, :, ls])
        for rb in range(2):
            rows = slice(rb * 256, rb * 256 + 256)
            q = QKV[0, rows, ls] * jnp.asarray(0.125, BF)
            outs = []
            for e in range(2):
                sw = swap[2 * hp + e]
                qe = jnp.where(low_lane if e == 0 else ~low_lane, q, jnp.zeros_like(q))
                s = dot(qe, kk, NT)
                kb = jnp.where(keylane >= 256, 1, 0)
                same = jnp.where(kb == rb, 0, 1)
                seen = (same == jnp.full((1, ROWS), sw, jnp.int32)) | (jnp.full((1, ROWS), kd, jnp.int32) == 1)
                s = s + jnp.where(seen, 0.0, NEGATIVE)
                top = jnp.max(s, axis=1, keepdims=True)
                pw = jnp.exp(s - top)
                tot = jnp.sum(pw, axis=1, keepdims=True)
                a = (pw * (1.0 / tot)).astype(BF)
                AT[2 * hp + e, rows, :] = a
                outs.append(dot(a, vv, NN))
            CTX[rows, ls] = jnp.where(low_lane, outs[0], outs[1]).astype(BF)

    zf(3)

    @pl.loop(0, 6)
    def forward_pairs(hp):
        attn_fwd(hp)
        pl.when(hp == 0)(lambda: xf(2))
        pl.when(hp == 1)(lambda: last_step(1))
        pl.when(hp == 2)(lambda: xf(3))

        @pl.when(hp == 4)
        def _():
            zf(4)
            fin(2)

    md.wait_recv()
    def picks(width, step, count):
        si = lax.broadcasted_iota(jnp.int32, (128, width), 0)
        sj = lax.broadcasted_iota(jnp.int32, (128, width), 1)
        return lambda dd: jnp.where((si < count) & (sj == si + dd * step), 1.0, 0.0).astype(BF)

    norm_pick, bias_pick = picks(D, 96, 96), picks(128, 16, 16)
    norm_acc = jnp.zeros((16, D), F32)
    bias_acc = jnp.zeros((32, 128), F32)
    for zi in range(4):
        for yi in range(2):
            dd = 2 * zi + yi
            norm_acc = norm_acc + dot(M[c, x, yi, zi].reshape(16, 128).astype(BF), norm_pick(dd), NN)
            bias_acc = bias_acc + dot(M[:, :, yi, zi, 1].reshape(32, 128).astype(BF), bias_pick(dd), NN)
    NB[0] = norm_acc[0:8]
    for tt in range(4):
        row = (tt % 2 * 2 + tt // 2) * 8
        for r in range(6):
            NB[1, tt : tt + 1, r * 128 : r * 128 + 128] = bias_acc[row + r : row + r + 1]

    igrad[...] = dot(CTX[...], mat(3), NT)
    fin(3)
    last_step(2)

    def ln_rows(i):
        return pl.ds(pl.multiple_of(i * 128, 128), 128)

    g1, b1 = NB[0, 0:1, :], NB[0, 1:2, :]
    g2, b2 = NB[0, 2:3, :], NB[0, 3:4, :]

    @pl.loop(0, 4)
    def _(i):
        rs = ln_rows(i)
        r = hid[rs, :].astype(F32) + igrad[rs, :]
        cen = r - jnp.mean(r, axis=1, keepdims=True)
        rstd = lax.rsqrt(jnp.mean(cen * cen, axis=1, keepdims=True) + EPSILON)
        xh = cen * rstd
        XH[rs, :] = xh
        RS1[rs, :] = rstd
        FI[rs, :] = (xh * g1 + b1).astype(BF)

    xf(4)
    ready(2)
    ready(3)
    for tt in range(4):
        if tt == 3:
            fin(4)
        pre = dot(FI[...], mat(4 + tt), NN) + NB[1, tt : tt + 1, :]
        cdf = 0.5 * (1.0 + lax.erf(pre * math.sqrt(0.5)))
        ACT[tt] = (pre * cdf).astype(BF)
        GP[tt] = (cdf + pre * (jnp.exp(-0.5 * pre * pre) * (1.0 / math.sqrt(2.0 * math.pi)))).astype(BF)

    last_step(3)
    ready(4)

    def half_mat(m, h):
        return W[m, :, :, :, :, h * HALF : h * HALF + HALF].reshape(D, HALF)

    acc = dot(ACT[0, :, 0:HALF], half_mat(8, 0), NT)
    for tt in range(1, 4):
        acc = acc + dot(ACT[tt, :, 0:HALF], half_mat(8 + tt, 0), NT)
    igrad[...] = acc
    last_ready()
    acc = dot(ACT[0, :, HALF:D], half_mat(8, 1), NT)
    for tt in range(1, 4):
        acc = acc + dot(ACT[tt, :, HALF:D], half_mat(8 + tt, 1), NT)
    igrad[...] += acc

    V[...] = jnp.zeros_like(V)
    load_cot.wait()

    @pl.loop(0, 4)
    def _(i):
        rs = ln_rows(i)
        r = XH[rs, :] * g1 + b1 + igrad[rs, :]
        cen = r - jnp.mean(r, axis=1, keepdims=True)
        rstd = lax.rsqrt(jnp.mean(cen * cen, axis=1, keepdims=True) + EPSILON)
        n2 = cen * rstd
        mixed[rs, :] = (n2 * g2 + b2).astype(BF)
        co = cot[rs, :].astype(F32)
        e = co * g2
        gr = rstd * (e - jnp.mean(e, axis=1, keepdims=True) - n2 * jnp.mean(e * n2, axis=1, keepdims=True))
        igrad[rs, :] = gr
        GF[rs, :] = gr.astype(BF)
        V[2:3, :] += jnp.sum(co * n2, axis=0, keepdims=True)
        V[3:4, :] += jnp.sum(co, axis=0, keepdims=True)

    save_mixed.start()

    def sq(r, xx):
        if r < 2:
            return SQ.at[r, xx]
        return W.at[8 + 2 * (r // 2 - 1) + xx, :, :, :, :, pl.ds((r % 2) * HALF, HALF)]

    def pb(r, xx, *rest):
        if r < 4:
            return PB.at[(r, xx) + rest]
        rest = rest + (slice(None),) * (4 - len(rest))
        return W.at[(4 + xx,) + rest + (pl.ds((r % 2) * HALF, HALF),)]

    def pb_all(r, *rest):
        if r < 4:
            return PB.at[(r, slice(None)) + rest]
        rest = rest + (slice(None),) * (4 - len(rest))
        return W.at[(pl.ds(4, 2),) + rest + (pl.ds((r % 2) * HALF, HALF),)]

    def b_sib(r, xx):
        return rc(sq(r, xx), SR.at[SIB_SLOT[r], xx], qs.at[r, xx], qr.at[r, xx], sib)

    ALL = slice(None)

    def b_a(r):
        return rc(pb(r, ox, ALL, ALL, 0), RA.at[r % SLOTS], as_.at[r], ar.at[r], xn)

    def b_b(r):
        return rc(pb_all(r, ALL, oy, 1), RB.at[r % SLOTS], bs.at[r], br.at[r], yn)

    def b_a2(r, k):
        dst = RO.at[r, 0] if k == 0 else RA2.at[r % SLOTS, k - 1]
        return rc(pb(r, x, zz[k], oy, 0), dst, a2s.at[r, k], a2r.at[r, k], yn)

    def b_b2(r, k):
        dst = RO.at[r, 1] if k == 0 else RB2.at[r % SLOTS, k - 1]
        return rc(pb(r, ox, zz[k], y, 1), dst, b2s.at[r, k], b2r.at[r, k], xn)

    def b_z(r, k):
        return rc(pb(r, x, zz[k], y), RZ.at[r, k - 1], rzs.at[r, k - 1], rzr.at[r, k - 1], zn[k])

    def zl(way, tgt, xx, recv=False):
        dst = (RU if way == 0 else RD).at[tgt, xx]
        dev = up_dev if way == 0 else down_dev
        return rc(PB.at[0, xx, tgt], dst, zls.at[way, tgt, xx], zlr.at[way, tgt, xx], dev)

    def zl_sends(way, tgt):
        return z < tgt if way == 0 else z > tgt

    def zl_got(way, tgt):
        return (z > 0) & (z <= tgt) if way == 0 else (z < 3) & (z >= tgt)

    def zl_first():
        for tgt in range(3):
            for xx in range(2):
                pl.when(z == 0)(lambda: zl(0, 3 - tgt, xx).start())
                pl.when(z == 3)(lambda: zl(1, tgt, xx).start())

    def zl_pass(way, at, tgt):
        for xx in range(2):
            @pl.when(z == at)
            def _():
                zl(way, tgt, xx).wait_recv()
                add(PB.at[0, xx, tgt], (RU if way == 0 else RD).at[tgt, xx])
                zl(way, tgt, xx).start()

    def zl_last():
        for way in range(2):
            for tgt in range(4):
                @pl.when((z == tgt) & ((z > 0) if way == 0 else (z < 3)))
                def _():
                    for xx in range(2):
                        zl(way, tgt, xx).wait_recv()
                        add(PB.at[0, xx, tgt], (RU if way == 0 else RD).at[tgt, xx])

    def b0(i):
        src, dst, dev = (
            (PB.at[0, ox, z, :, 0], R0.at[0], xn),
            (PB.at[0, :, z, oy, 1], R0.at[1], yn),
            (PB.at[0, x, z, oy, 0], R0.at[2, 0], yn),
            (PB.at[0, ox, z, y, 1], R0.at[2, 1], xn),
        )[i]
        return rc(src, dst, z0s.at[i], z0r.at[i], dev)

    def xy0_first():
        b0(0).start()
        b0(1).start()

    def xy0_second():
        b0(0).wait_recv()
        add(PB.at[0, x, z, :, 0], R0.at[0])
        b0(2).start()
        b0(1).wait_recv()
        add(PB.at[0, :, z, y, 1], R0.at[1])
        b0(3).start()

    def xy0_last():
        b0(2).wait_recv()
        b0(3).wait_recv()
        tot = PB[0, x, z, y].astype(F32) + R0[2].astype(F32)
        g_down[:, 0:HALF] = tot.reshape(96, HALF)

    def rs0_drain():
        for xx in range(2):
            b_sib(0, xx).wait_send()
        for i in range(4):
            b0(i).wait_send()
        for way in range(2):
            for tgt in range(4):
                for xx in range(2):
                    pl.when(zl_sends(way, tgt))(lambda: zl(way, tgt, xx).wait_send())

    def credit(sem, dev, r):
        if r + SLOTS < PIECES:
            pl.semaphore_signal(sem, inc=1, device_id=dev, device_id_type=pl.DeviceIdType.MESH)

    def need(sem, r):
        if r >= SLOTS + (sem is not c_sib):
            pl.semaphore_wait(sem, 1)

    def part(r, xx, core):
        if r < 4:
            src = ACT if r < 2 else GP
            lhs = GF if r < 2 else FI
            h = r % 2
            return dot(lhs[...], src[2 * xx + core, :, h * HALF : h * HALF + HALF], TN)
        raise ValueError

    def part_attn(m, xx):
        if m < 3:
            return dot(hid[...], ACT[(1, 0, 2)[m], :, xx * HALF : xx * HALF + HALF], TN)
        return dot(GF[...], CTX[:, xx * HALF : xx * HALF + HALF], TN)

    def gen_sib(r):
        need(c_sib, r)
        for xx in range(2):
            if r < 4:
                sq(r, xx)[...] = part(r, xx, oc).astype(BF).reshape(4, 2, 2, 48, HALF)
            else:
                for core in range(2):
                    @pl.when(oc == core)
                    def _():
                        sq(r, xx)[...] = part_attn(2 * core + 5 - r, xx).astype(BF).reshape(4, 2, 2, 48, HALF)
            b_sib(r, xx).start()

    def own_part(r, xx, grad):
        v = grad.reshape(4, 2, 2, 48, HALF) + SR[SIB_SLOT[r], xx].astype(F32)
        pb(r, xx)[...] = v.astype(BF)

    def gen_own(r):
        for xx in range(2):
            b_sib(r, xx).wait_recv()
            if r < 4:
                own_part(r, xx, part(r, xx, c))
            else:
                for core in range(2):
                    @pl.when(c == core)
                    def _():
                        own_part(r, xx, part_attn(2 * core + 5 - r, xx))
        credit(c_sib, sib, r)
        if r == 0:
            zl_first()
            return
        need(c_a, r)
        b_a(r).start()
        need(c_b, r)
        b_b(r).start()

    def add(dst, src):
        dst[...] = (dst[...].astype(F32) + src[...].astype(F32)).astype(BF)

    def st1(r):
        q = r % SLOTS
        b_a(r).wait_recv()
        add(pb(r, x, ALL, ALL, 0), RA.at[q])
        credit(c_a, xn, r)
        need(c_a2, r)
        for k in (2, 3, 1):
            b_a2(r, k).start()
        b_b(r).wait_recv()
        add(pb_all(r, ALL, y, 1), RB.at[q])
        credit(c_b, yn, r)
        need(c_b2, r)
        for k in (2, 3, 1):
            b_b2(r, k).start()

    def st2o(r):
        b_a2(r, 0).start()
        b_b2(r, 0).start()

    def st2(r):
        q = r % SLOTS
        for k in (2, 3, 1):
            b_a2(r, k).wait_recv()
            add(pb(r, x, zz[k], y, 0), RA2.at[q, k - 1])
            b_b2(r, k).wait_recv()
            add(pb(r, x, zz[k], y, 1), RB2.at[q, k - 1])
            b_z(r, k).start()
        credit(c_a2, yn, r)
        credit(c_b2, xn, r)

    def fx(r):
        m = g_attn.at[2 * c + 5 - r]
        return rc(m, m, es.at[r - 1], er.at[r - 1], sib)

    def st3(r):
        tot = pb(r, x, z, y)[...].astype(F32)
        for k in (2, 3, 1):
            b_z(r, k).wait_recv()
            tot = tot + RZ[r, k - 1].astype(F32)
        b_a2(r, 0).wait_recv()
        b_b2(r, 0).wait_recv()
        tot = (tot + RO[r].astype(F32)).reshape(96, HALF)
        h = r % 2
        if r < 2:
            g_down[:, h * HALF : h * HALF + HALF] = tot
        elif r < 4:
            g_up[:, h * HALF : h * HALF + HALF] = tot
        else:
            g_attn[2 * c + 5 - r] = tot
            fx(r).start()

    def rs_drain(r):
        for xx in range(2):
            b_sib(r, xx).wait_send()
        b_a(r).wait_send()
        b_b(r).wait_send()
        for k in range(4):
            b_a2(r, k).wait_send()
            b_b2(r, k).wait_send()
        for k in (1, 2, 3):
            b_z(r, k).wait_send()

    def gact(h):
        ls = slice(h * HALF, h * HALF + HALF)
        for tt in range(4):
            ga = dot(GF[...], half_mat(8 + tt, h), NN)
            gp = (ga * GP[tt, :, ls].astype(F32)).astype(BF)
            GP[tt, :, ls] = gp
            V[4 + tt : 5 + tt, ls] = jnp.sum(gp.astype(F32), axis=0, keepdims=True)

    gen_sib(1)
    gen_sib(0)
    for p in range(PIECES - 1):
        drain(p)
    last_drain()
    gen_own(1)
    gen_own(0)
    gact(0)
    gen_sib(2)
    gact(1)
    gen_own(2)
    zl_pass(0, 1, 3)
    zl_pass(1, 2, 0)
    gen_sib(3)
    st1(1)

    acc = dot(GP[0], mat(4), NT)
    for tt in range(1, 4):
        acc = acc + dot(GP[tt], mat(4 + tt), NT)
    igrad[...] += acc
    gen_own(3)

    @pl.loop(0, 4)
    def _(i):
        rs = ln_rows(i)
        gn = igrad[rs, :]
        xh = XH[rs, :]
        e = gn * g1
        gr = RS1[rs, :] * (e - jnp.mean(e, axis=1, keepdims=True) - xh * jnp.mean(e * xh, axis=1, keepdims=True))
        igrad[rs, :] = gr
        GF[rs, :] = gr.astype(BF)
        V[0:1, :] += jnp.sum(gn * xh, axis=0, keepdims=True)
        V[1:2, :] += jnp.sum(gn, axis=0, keepdims=True)

    vc = [
        rc(V, VR.at[0], vs.at[0], vr.at[0], sib),
        rc(V, VR.at[1], vs.at[1], vr.at[1], xn),
        rc(V, VR.at[2], vs.at[2], vr.at[2], yn),
    ] + [rc(V, VR.at[2 + k], vs.at[2 + k], vr.at[2 + k], zn[k]) for k in (1, 2, 3)]

    def v_step(i):
        vc[i].wait()
        V[...] += VR[i]

    vc[0].start()
    zl_pass(0, 1, 2)
    zl_pass(1, 2, 1)
    zl_pass(0, 2, 3)
    zl_pass(1, 1, 0)

    FI[...] = dot(GF[...], mat(3), NN).astype(BF)
    v_step(0)
    vc[1].start()

    def attn_bwd(hp):
        ls = pair_lanes(hp)
        fl = flips(hp)
        kk = jnp.where(fl, KVO[0, :, ls], QKV[1, :, ls])
        vv = jnp.where(fl, KVO[1, :, ls], QKV[2, :, ls])
        q = QKV[0, :, ls]
        do = FI[:, ls]
        dvs, dqs, dks = [], [], []
        for e in range(2):
            a = AT[2 * hp + e]
            dvs.append(dot(a, do, TN))
            de = jnp.where(low_lane if e == 0 else ~low_lane, do, jnp.zeros_like(do))
            dp = dot(de, vv, NT)
            af = a.astype(F32)
            w = af * dp
            gs = (w - af * jnp.sum(w, axis=1, keepdims=True)).astype(BF)
            dqs.append(dot(gs, kk, NN))
            dks.append(dot(gs, q, TN))
        ACT[0, :, ls] = (jnp.where(low_lane, dqs[0], dqs[1]) * 0.125).astype(BF)
        GP[0, :, ls] = (jnp.where(low_lane, dks[0], dks[1]) * 0.125).astype(BF)
        GP[1, :, ls] = jnp.where(low_lane, dvs[0], dvs[1]).astype(BF)

    def dkv(i):
        ls = pl.ds(i * HALF, HALF)
        return rc(GP.at[pl.ds(0, 2), :, ls], DKVR.at[:, :, ls], es.at[2 + 3 * i], er.at[2 + 3 * i], sib)

    @pl.loop(0, 6)
    def backward_pairs(hp):
        attn_bwd(hp)

        @pl.when(hp == 1)
        def _():
            st1(2)
            st2(1)

        pl.when(hp == 2)(lambda: dkv(0).start())

        @pl.when(hp == 3)
        def _():
            st1(3)
            st2(2)
            st2o(1)
            st2o(2)

    gen_sib(4)
    dkv(1).start()
    v_step(1)
    vc[2].start()
    gen_own(4)
    dkv(0).wait()
    dkv(1).wait()

    def pick(hp):
        ls = pair_lanes(hp)
        fl = flips(hp)
        ACT[1, :, ls] = jnp.where(fl, DKVR[0, :, ls], GP[0, :, ls])
        ACT[2, :, ls] = jnp.where(fl, DKVR[1, :, ls], GP[1, :, ls])

    pl.loop(0, 6)(pick)

    gen_sib(5)
    zl_last()
    xy0_first()
    st2(3)
    v_step(2)
    for k in (1, 2, 3):
        vc[2 + k].start()
    acc = dot(ACT[0], mat(1), NT)
    for m in (1, 2):
        acc = acc + dot(ACT[m], mat((1, 0, 2)[m]), NT)
    igrad[...] += acc
    st2o(3)
    st1(4)
    gen_own(5)
    st2(4)
    xy0_second()
    st2o(4)
    for r in (1, 2, 3):
        st3(r)
    st1(5)
    st2o(5)
    xy0_last()
    st2(5)
    st3(4)
    st3(5)
    for k in (1, 2, 3):
        vc[2 + k].wait()
    g_misc[...] = V[...] + VR[3] + VR[4] + VR[5]
    save_mixed.wait()
    rs0_drain()
    for r in range(1, PIECES):
        rs_drain(r)
    for cp in mz:
        cp.wait_send()
    mx.wait_send()
    my.wait_send()
    md.wait_send()
    axc.wait_send()
    kvc.wait_send()
    fx(4).wait()
    fx(5).wait()


def finish_kernel(
    mixed, igrad, ga, gu, gd, gm, o_mixed, o_igrad, o_qkv, o_out, o_up, o_bias, o_down, o_norm,
    v_igrad, v_mixed, v_up, v_down, v_ga, v_gm, w_qkv, w_out, w_bias, w_norm, tmp, sem,
):
    copy = pltpu.make_async_copy
    load_small = [copy(gm, v_gm, sem.at[0, 8]), copy(ga, v_ga, sem.at[0, 9])]
    parts = [(igrad, v_igrad, o_igrad, i * 128, 128) for i in range(4)]
    parts += [(mixed, v_mixed, o_mixed, i * 256, 256) for i in range(2)]
    parts += [(gu, v_up, o_up, 0, 96), (gd, v_down, o_down, 0, 96)]
    loads, stores = [], []
    for i, (src, mid, dst, at, n) in enumerate(parts):
        rows = pl.ds(at, n)
        loads.append(copy(src.at[rows], mid.at[rows], sem.at[0, i]))
        stores.append(copy(mid.at[rows], dst.at[rows], sem.at[1, i]))
    for cp in load_small + loads:
        cp.start()
    dd = lax.axis_index("dp")
    t = lax.axis_index("tensor")
    exact = dict(preferred_element_type=F32, precision=lax.Precision.HIGHEST)
    si = lax.broadcasted_iota(jnp.int32, (D, 128), 0)
    sj = lax.broadcasted_iota(jnp.int32, (D, 128), 1)
    norm_pick = jnp.where(si == sj + dd * 96, 1.0, 0.0).astype(F32)
    bias_pick = jnp.where(si[0:128] == sj[0:128] + dd * 16, 1.0, 0.0).astype(F32)
    sub = lax.broadcasted_iota(jnp.int32, (8, D), 0)
    load_small[0].wait()
    norm = lax.dot_general(v_gm[...], norm_pick, NN, **exact)
    w_norm[...] = jnp.sum(jnp.where(sub[:, 0:128] == t, norm, 0.0), axis=0, keepdims=True)[:, 0:96]
    row = jnp.sum(jnp.where(sub == 4 + t, v_gm[...], 0.0), axis=0, keepdims=True)
    for r in range(6):
        tmp[r : r + 1] = row[:, r * 128 : r * 128 + 128]
    w_bias[...] = lax.dot_general(tmp[...], bias_pick, NN, **exact)[0:6, 0:16]
    load_small[1].wait()
    first = jnp.full((96, 192), lax.rem(t, 2), jnp.int32) == 0
    for m in range(4):
        v = jnp.where(first, v_ga[m, :, 0:192], v_ga[m, :, 192:HALF])
        if m < 3:
            w_qkv[(1, 0, 2)[m]] = v
        else:
            w_out[...] = v.T
    small = ((w_norm, o_norm), (w_bias, o_bias), (w_qkv, o_qkv), (w_out, o_out))
    for i, (src, dst) in enumerate(small):
        stores.append(copy(src, dst, sem.at[1, 8 + i]))
        stores[-1].start()
    for load, store in zip(loads, stores):
        load.wait()
        store.start()
    for cp in stores:
        cp.wait()


def scratch():
    vm = pltpu.VMEM
    dma = lambda *s: pltpu.SemaphoreType.DMA(s)
    n = PIECES
    return [
        vm((ROWS, D), BF), vm((ROWS, D), BF), vm((ROWS, D), BF), vm((12, 4, 2, 2, 48, D), BF), vm((4, 96, 256), BF), vm((2, 96, 256), BF), vm((3, ROWS, D), BF), vm((2, ROWS, D), BF),
        vm((12, ROWS, ROWS), BF), vm((ROWS, D), BF), vm((ROWS, D), F32), vm((ROWS, 1), F32), vm((ROWS, D), BF),
        vm((4, ROWS, D), BF), vm((4, ROWS, D), BF), vm((ROWS, D), BF), vm((2, ROWS, D), BF),
        vm((2, 2, 2, 4, 2, 8, 128), F32), vm((2, 8, D), F32), vm((8, D), F32), vm((6, 8, D), F32),
        vm((2, 2, 4, 2, 2, 48, HALF), BF), vm((SLOTS, 2, 4, 2, 2, 48, HALF), BF), vm((4, 2, 4, 2, 2, 48, HALF), BF),
        vm((SLOTS, 4, 2, 48, HALF), BF), vm((SLOTS, 2, 4, 48, HALF), BF), vm((SLOTS, 3, 48, HALF), BF),
        vm((SLOTS, 3, 48, HALF), BF), vm((n, 2, 48, HALF), BF), vm((n, 3, 2, 48, HALF), BF),
        vm((4, 2, 2, 2, 48, HALF), BF), vm((4, 2, 2, 2, 48, HALF), BF), vm((3, 2, 48, HALF), BF),
        dma(n, 3), dma(n, 3), dma(n, 4), dma(n, 4), dma(n, 4), dma(n, 4), dma(n, 2), dma(n, 2), dma(n, 4), dma(n, 4),
        dma(6), dma(6), dma(6), dma(6),
        dma(n, 2), dma(n, 2), dma(n), dma(n), dma(n), dma(n), dma(n, 4), dma(n, 4), dma(n, 4), dma(n, 4), dma(n, 3), dma(n, 3), dma(6), dma(6),
        dma(2, 3, 2), dma(2, 3, 2), dma(7, 2), dma(7, 2), dma(2, 4, 2), dma(2, 4, 2), dma(4), dma(4), dma(3),
        pltpu.SemaphoreType.REGULAR, pltpu.SemaphoreType.REGULAR, pltpu.SemaphoreType.REGULAR,
        pltpu.SemaphoreType.REGULAR, pltpu.SemaphoreType.REGULAR,
    ]


def whole_layer(
    hidden_in, qkv_weight, out_weight, up_weight, up_bias, down_weight, norm_params, cotangent, head_swap, slot_kind
):
    any_ = pl.BlockSpec(memory_space=pl.ANY)
    vmem = pl.BlockSpec(memory_space=pltpu.VMEM)
    smem = pl.BlockSpec(memory_space=pltpu.SMEM)
    sds = jax.ShapeDtypeStruct
    mixed, igrad, ga, gu, gd, gm = pl.pallas_call(
        layer_kernel,
        out_shape=(
            sds((ROWS, D), BF), sds((ROWS, D), F32), sds((4, 96, HALF), F32),
            sds((96, D), F32), sds((96, D), F32), sds((8, D), F32),
        ),
        in_specs=[any_] + [vmem] * 6 + [any_] + [smem] * 2,
        out_specs=(any_,) + (vmem,) * 5,
        scratch_shapes=scratch(),
        compiler_params=pltpu.CompilerParams(
            collective_id=0, has_side_effects=True, vmem_limit_bytes=63 * 2**20
        ),
        name="layer",
    )(
        hidden_in, qkv_weight, out_weight, up_weight, up_bias, down_weight.T, norm_params, cotangent, head_swap, slot_kind
    )
    *outs, bias_grad, down_grad, norm_grad = pl.pallas_call(
        finish_kernel,
        out_shape=(
            sds((ROWS, D), BF), sds((ROWS, D), F32), sds((3, 96, 192), F32), sds((192, 96), F32),
            sds((96, D), F32), sds((6, 16), F32), sds((96, D), F32), sds((1, 96), F32),
        ),
        in_specs=[any_] * 6,
        out_specs=(any_,) * 8,
        scratch_shapes=[
            pltpu.VMEM((ROWS, D), F32), pltpu.VMEM((ROWS, D), BF), pltpu.VMEM((96, D), F32), pltpu.VMEM((96, D), F32),
            pltpu.VMEM((4, 96, HALF), F32), pltpu.VMEM((8, D), F32), pltpu.VMEM((3, 96, 192), F32),
            pltpu.VMEM((192, 96), F32), pltpu.VMEM((6, 16), F32), pltpu.VMEM((1, 96), F32), pltpu.VMEM((8, 128), F32),
            pltpu.SemaphoreType.DMA((2, 12)),
        ],
        compiler_params=pltpu.CompilerParams(vmem_limit_bytes=63 * 2**20),
        name="finish",
    )(mixed, igrad, ga, gu, gd, gm)
    return (*outs, bias_grad, down_grad.T, norm_grad)


def norm_rows(residual, scales, offset):
    center = residual - jnp.mean(residual, axis=-1, keepdims=True)
    spread = jnp.mean(center * center, axis=-1, keepdims=True)
    return center * lax.rsqrt(spread + EPSILON) * scales + offset


def smooth_gate(values):
    return jax.nn.gelu(values, approximate=False)


def arrange(queries, keys_in, values_in, slot_type, local_swaps):
    slot_len, head_count, head_size = queries.shape
    half_len = slot_len // 2
    quarter = half_len // 2
    shape_four = (2, half_len, head_count, head_size)
    query_half = queries.reshape(shape_four)
    key_half = keys_in.reshape(shape_four)
    value_half = values_in.reshape(shape_four)
    flipped = (local_swaps * slot_type == 1)[None, None, :, None]
    key_pick = jnp.where(flipped, key_half[::-1], key_half)
    value_pick = jnp.where(flipped, value_half[::-1], value_half)
    blocks = jnp.arange(half_len, dtype=jnp.int32) // quarter
    matching = (
        jnp.bitwise_xor(blocks[None, :, None], local_swaps[:, None, None]) == blocks[None, None, :]
    )
    allowed = jnp.logical_or(slot_type == 1, matching)
    return (query_half, key_pick, value_pick, allowed, flipped)


def masked_scores(query_half, key_pick, allowed):
    scale = 1.0 / math.sqrt(query_half.shape[-1])
    scores = (
        jnp.einsum("jqhd,jkhd->jhqk", query_half, key_pick, preferred_element_type=jnp.float32)
        * scale
    )
    return jnp.where(allowed[None], scores, NEGATIVE)


def slot_forward(inputs, local_swaps):
    queries, keys_in, values_in, slot_type = inputs
    query_half, key_pick, value_pick, allowed, flipped = arrange(
        queries, keys_in, values_in, slot_type, local_swaps
    )
    scores = masked_scores(query_half, key_pick, allowed)
    largest = jnp.max(scores, axis=-1, keepdims=True)
    powers = jnp.exp(scores - largest)
    totals = jnp.sum(powers, axis=-1, keepdims=True)
    attention = (powers / totals).astype(jnp.bfloat16)
    context = jnp.einsum(
        "jhqk,jkhd->jqhd", attention, value_pick, preferred_element_type=jnp.float32
    )
    return (context.astype(jnp.bfloat16).reshape(queries.shape[0], -1), largest + jnp.log(totals))


def slot_backward(inputs, local_swaps):
    queries, keys_in, values_in, slot_type, log_totals, grad_out = inputs
    slot_len, head_count, head_size = queries.shape
    scale = 1.0 / math.sqrt(head_size)
    query_half, key_pick, value_pick, allowed, flipped = arrange(
        queries, keys_in, values_in, slot_type, local_swaps
    )
    attention = jnp.exp(masked_scores(query_half, key_pick, allowed) - log_totals)
    grad_half = grad_out.reshape(query_half.shape)
    grad_vpick = jnp.einsum(
        "jhqk,jqhd->jkhd",
        attention.astype(jnp.bfloat16),
        grad_half,
        preferred_element_type=jnp.float32,
    ).astype(jnp.bfloat16)
    grad_attention = jnp.einsum(
        "jqhd,jkhd->jhqk", grad_half, value_pick, preferred_element_type=jnp.float32
    )
    row_dots = jnp.sum(attention * grad_attention, axis=-1, keepdims=True)
    grad_scores = (attention * (grad_attention - row_dots)).astype(jnp.bfloat16)
    grad_query = (
        jnp.einsum("jhqk,jkhd->jqhd", grad_scores, key_pick, preferred_element_type=jnp.float32)
        * scale
    ).astype(jnp.bfloat16)
    grad_kpick = (
        jnp.einsum("jhqk,jqhd->jkhd", grad_scores, query_half, preferred_element_type=jnp.float32)
        * scale
    ).astype(jnp.bfloat16)
    grad_key = jnp.where(flipped, grad_kpick[::-1], grad_kpick)
    grad_value = jnp.where(flipped, grad_vpick[::-1], grad_vpick)
    return (
        grad_query.reshape(slot_len, -1),
        grad_key.reshape(slot_len, -1),
        grad_value.reshape(slot_len, -1),
    )


def per_device(
    hidden_in,
    qkv_weight,
    out_weight,
    up_weight,
    up_bias,
    down_weight,
    norm_params,
    cotangent,
    head_swap,
    slot_kind,
):
    tensor_count = lax.axis_size("tensor")
    tensor_rank = lax.axis_index("tensor")
    heads_here = head_swap.shape[0] // tensor_count
    local_swaps = lax.dynamic_slice_in_dim(head_swap, tensor_rank * heads_here, heads_here)
    qkv_low = qkv_weight.astype(jnp.bfloat16)
    out_low = out_weight.astype(jnp.bfloat16)
    norm_low = norm_params.astype(jnp.bfloat16)
    up_low = up_weight.astype(jnp.bfloat16)
    bias_low = up_bias.astype(jnp.bfloat16)
    down_low = down_weight.astype(jnp.bfloat16)
    qkv_full, out_full, norm_full = (
        lax.all_gather(qkv_low, "dp", axis=1, tiled=True),
        lax.all_gather(out_low, "dp", axis=1, tiled=True),
        lax.all_gather(norm_low, "dp", axis=1, tiled=True),
    )
    norm_gain = norm_full.astype(jnp.float32)
    full_in = lax.all_gather(hidden_in, "tensor", axis=0, tiled=True)
    group_rows = full_in.shape[0]
    local_width = qkv_full.shape[2]
    head_size = local_width // heads_here
    slot_count = group_rows // LONG_LEN

    def by_slot(rows):
        return rows.reshape(slot_count, LONG_LEN, heads_here, head_size)

    projected = jnp.einsum(
        "td,cde->cte", full_in, qkv_full, preferred_element_type=jnp.float32
    ).astype(jnp.bfloat16)
    context, log_totals = lax.map(
        partial(slot_forward, local_swaps=local_swaps),
        (by_slot(projected[0]), by_slot(projected[1]), by_slot(projected[2]), slot_kind),
    )
    context = context.reshape(group_rows, local_width)
    rows = context
    attn_share = lax.psum_scatter(
        jnp.dot(rows, out_full, preferred_element_type=jnp.float32).astype(jnp.bfloat16),
        "tensor",
        scatter_dimension=0,
        tiled=True,
    ).astype(jnp.float32)
    resid_one = hidden_in.astype(jnp.float32) + attn_share
    normed_one, norm_one_back = jax.vjp(norm_rows, resid_one, norm_gain[0], norm_gain[1])
    up_full, bias_full, down_full = (
        lax.all_gather(up_low, "dp", axis=0, tiled=True),
        lax.all_gather(bias_low, "dp", axis=1, tiled=True),
        lax.all_gather(down_low, "dp", axis=1, tiled=True),
    )
    ffn_in = lax.all_gather(normed_one.astype(jnp.bfloat16), "tensor", axis=0, tiled=True)
    pre = jnp.dot(ffn_in, up_full, preferred_element_type=jnp.float32) + bias_full.reshape(
        -1
    ).astype(jnp.float32)
    act_value, gate_back = jax.vjp(smooth_gate, pre)
    act = act_value.astype(jnp.bfloat16)
    rows = act
    ffn_share = lax.psum_scatter(
        jnp.dot(rows, down_full, preferred_element_type=jnp.float32).astype(jnp.bfloat16),
        "tensor",
        scatter_dimension=0,
        tiled=True,
    ).astype(jnp.float32)
    normed_two, norm_two_back = jax.vjp(
        norm_rows, normed_one + ffn_share, norm_gain[2], norm_gain[3]
    )
    mixed = normed_two.astype(jnp.bfloat16)
    grad_resid_two, grad_gain_two, grad_bias_two = norm_two_back(cotangent.astype(jnp.float32))
    grad_ffn = lax.all_gather(grad_resid_two.astype(jnp.bfloat16), "tensor", axis=0, tiled=True)
    grad_down = jnp.einsum("tf,td->fd", act, grad_ffn, preferred_element_type=jnp.float32)
    grad_act = jnp.einsum("td,fd->tf", grad_ffn, down_full, preferred_element_type=jnp.float32)
    grad_pre = gate_back(grad_act)[0].astype(jnp.bfloat16)
    grad_up = jnp.einsum("td,tf->df", ffn_in, grad_pre, preferred_element_type=jnp.float32)
    grad_bias = jnp.sum(grad_pre.astype(jnp.float32), axis=0).reshape(bias_full.shape)
    rows = grad_pre
    grad_normed_one = grad_resid_two + lax.psum_scatter(
        jnp.einsum("tf,df->td", rows, up_full, preferred_element_type=jnp.float32).astype(
            jnp.bfloat16
        ),
        "tensor",
        scatter_dimension=0,
        tiled=True,
    ).astype(jnp.float32)
    grad_resid_one, grad_gain_one, grad_bias_one = norm_one_back(grad_normed_one)
    grad_attn = lax.all_gather(grad_resid_one.astype(jnp.bfloat16), "tensor", axis=0, tiled=True)
    grad_out = jnp.einsum("tw,td->wd", context, grad_attn, preferred_element_type=jnp.float32)
    grad_context = jnp.einsum(
        "td,wd->tw", grad_attn, out_full, preferred_element_type=jnp.float32
    ).astype(jnp.bfloat16)
    grad_query, grad_key, grad_value = lax.map(
        partial(slot_backward, local_swaps=local_swaps),
        (
            by_slot(projected[0]),
            by_slot(projected[1]),
            by_slot(projected[2]),
            slot_kind,
            log_totals,
            grad_context.reshape(slot_count, LONG_LEN, local_width),
        ),
    )
    grad_proj = jnp.stack([grad_query, grad_key, grad_value]).reshape(3, group_rows, local_width)
    grad_qkv = jnp.einsum("td,cte->cde", full_in, grad_proj, preferred_element_type=jnp.float32)
    grad_in_part = jnp.einsum(
        "cte,cde->td", grad_proj, qkv_full, preferred_element_type=jnp.float32
    )
    norm_part = jnp.stack([grad_gain_one, grad_bias_one, grad_gain_two, grad_bias_two])
    grad_in_share, norm_row = (
        lax.psum_scatter(
            grad_in_part.astype(jnp.bfloat16), "tensor", scatter_dimension=0, tiled=True
        ).astype(jnp.float32),
        lax.psum_scatter(
            norm_part.astype(jnp.bfloat16), "tensor", scatter_dimension=0, tiled=True
        ).astype(jnp.float32),
    )
    input_grad = grad_resid_one + grad_in_share
    qkv_grad, out_grad, up_grad, up_bias_grad, down_grad, norm_grad = (
        lax.psum_scatter(grad_qkv, "dp", scatter_dimension=1, tiled=True),
        lax.psum_scatter(grad_out, "dp", scatter_dimension=1, tiled=True),
        lax.psum_scatter(grad_up, "dp", scatter_dimension=0, tiled=True),
        lax.psum_scatter(grad_bias, "dp", scatter_dimension=1, tiled=True),
        lax.psum_scatter(grad_down, "dp", scatter_dimension=1, tiled=True),
        lax.psum_scatter(norm_row, "dp", scatter_dimension=1, tiled=True),
    )
    return (mixed, input_grad, qkv_grad, out_grad, up_grad, up_bias_grad, down_grad, norm_grad)


def solution(mesh):
    placed = (
        P(("dp", "tensor"), None),
        P(None, "dp", "tensor"),
        P("tensor", "dp"),
        P("dp", "tensor"),
        P("tensor", "dp"),
        P("tensor", "dp"),
        P(None, "dp"),
        P(("dp", "tensor"), None),
        P(),
        P("dp"),
    )
    planned = mesh.shape["dp"] == 8 and mesh.shape["tensor"] == 4
    return jax.shard_map(
        whole_layer if planned else per_device,
        mesh=mesh,
        in_specs=placed,
        out_specs=(
            P(("dp", "tensor"), None),
            P(("dp", "tensor"), None),
            P(None, "dp", "tensor"),
            P("tensor", "dp"),
            P("dp", "tensor"),
            P("tensor", "dp"),
            P("tensor", "dp"),
            P("tensor", "dp"),
        ),
        check_vma=False,
    )
```

```python
from functools import partial
import math

import jax
import jax.numpy as jnp
from jax import lax
from jax.experimental import pallas as pl
from jax.experimental.pallas import tpu as pltpu
from jax.sharding import PartitionSpec as P

LONG_LEN = 1024
EPSILON = 1e-05
NEGATIVE = -1e30

BF = jnp.bfloat16
F32 = jnp.float32
NN = (((1,), (0,)), ((), ()))
NT = (((1,), (1,)), ((), ()))
TN = (((0,), (0,)), ((), ()))
PIECES = 6
SLOTS = 3
SIB_SLOT = (2, 0, 1, 0, 1, 2)
ROWS = 512
D = 768
HALF = 384


def dot(a, b, dims):
    return lax.dot_general(a, b, dims, preferred_element_type=F32)


def layer_kernel(
    hid_in, qkv_w, out_w, up_w, up_b, down_w, norm_p, cot_in, swap, kind,
    mixed_out, igrad, g_attn, g_up, g_down, g_misc,
    hid, cot, mixed, W, SH, AX, QKV, KVO, AT, CTX, XH, RS1, FI, ACT, GP, GF, DKVR,
    M, NB, V, VR,
    SQ, SR, PB, RA, RB, RA2, RB2, RO, RZ, RU, RD, R0,
    zs, zr, xs, xr, ys, yr, hs, hr, ds_, dr, ms, mr, es, er,
    qs, qr, as_, ar, bs, br, a2s, a2r, b2s, b2r, rzs, rzr, vs, vr, ls_, lr, lds, ldr, zls, zlr, z0s, z0r, io,
    c_sib, c_a, c_b, c_a2, c_b2,
):
    d = lax.axis_index("dp")
    t = lax.axis_index("tensor")
    z, y = d // 2, lax.rem(d, 2)
    x, c = t // 2, lax.rem(t, 2)
    ox, oy, oc = 1 - x, 1 - y, 1 - c

    def zk(k):
        hi, lo = z // 2, lax.rem(z, 2)
        kh, kl = k // 2, k % 2
        h2 = hi if kh == 0 else 1 - hi
        l2 = lo if kl == 0 else 1 - lo
        return 2 * h2 + l2

    zz = [zk(k) for k in range(4)]
    sib = (d, 2 * x + oc)
    xn = (d, 2 * ox + c)
    yn = (2 * z + oy, t)
    zn = [(2 * zz[k] + y, t) for k in range(4)]

    def rc(src, dst, s, r, dev):
        return pltpu.make_async_remote_copy(
            src_ref=src, dst_ref=dst, send_sem=s, recv_sem=r,
            device_id=dev, device_id_type=pl.DeviceIdType.MESH,
        )

    load_hid = pltpu.make_async_copy(hid_in, hid, io.at[0])
    load_cot = pltpu.make_async_copy(cot_in, cot, io.at[1])
    save_mixed = pltpu.make_async_copy(mixed, mixed_out, io.at[2])
    load_hid.start()
    load_cot.start()

    bar = pltpu.get_barrier_semaphore()
    for dev in (sib, xn, yn, zn[1], zn[2], zn[3]):
        pl.semaphore_signal(bar, inc=1, device_id=dev, device_id_type=pl.DeviceIdType.MESH)

    def where(p, xx, core):
        if p < 2:
            return 2 * core + p, pl.multiple_of(xx * HALF, 128)
        if p < 4:
            return 4 + 2 * xx + core, (p - 2) * HALF
        return 8 + 2 * xx + core, (p - 4) * HALF

    def slab(p, xx, zi, yi, core=None):
        m, lane = where(p, xx, c if core is None else core)
        return W.at[m, zi, yi, :, :, pl.ds(lane, HALF)]

    def col(p, xx, yi, core=None):
        m, lane = where(p, xx, c if core is None else core)
        return W.at[m, :, yi, :, :, pl.ds(lane, HALF)]

    def hcol(p, xx, yi, half):
        m, lane = where(p, xx, c)
        return W.at[m, :, yi, half, :, pl.ds(lane, HALF)]

    def zcp(p, k, recv=False):
        s = slab(p, x, zz[k] if recv else z, y)
        return rc(s, s, zs.at[p, k - 1], zr.at[p, k - 1], zn[k])

    def xcp(p, k, recv=False):
        s = slab(p, ox if recv else x, zz[k], y)
        return rc(s, s, xs.at[p, k], xr.at[p, k], xn)

    def ycp(p, k, recv=False):
        s = slab(p, x, zz[k], oy if recv else y)
        return rc(s, s, ys.at[p, k], yr.at[p, k], yn)

    def acp(p, recv=False):
        s = hcol(p, ox, oy if recv else y, 0)
        return rc(s, s, hs.at[p, 0], hr.at[p, 0], yn)

    def bcp(p, recv=False):
        s = hcol(p, ox if recv else x, oy, 1)
        return rc(s, s, hs.at[p, 1], hr.at[p, 1], xn)

    groups = [(x, y), (ox, y), (x, oy), (ox, oy)]

    def dcp(p, g, recv=False):
        xx, yy = groups[g]
        s = col(p, xx, yy, oc if recv else c)
        return rc(s, s, ds_.at[p, g], dr.at[p, g], sib)

    last = PIECES - 1

    def lx(recv=False):
        s = slab(last, ox if recv else x, z, y)
        return rc(s, s, xs.at[last, 0], xr.at[last, 0], xn)

    def ly(recv=False):
        s = slab(last, x, z, oy if recv else y)
        return rc(s, s, ys.at[last, 0], yr.at[last, 0], yn)

    def lhalf(i, recv=False):
        if i == 0:
            xx, yy, dev = ox, oy if recv else y, yn
        else:
            xx, yy, dev = ox if recv else x, oy, xn
        m, lane = where(last, xx, c)
        s = W.at[m, z, yy, i, :, pl.ds(lane, HALF)]
        return rc(s, s, hs.at[last, i], hr.at[last, i], dev)

    def lcol(core, xx, zi):
        m, lane = where(last, xx, core)
        return W.at[m, zi, :, :, :, pl.ds(lane, HALF)]

    up_dev, down_dev = (d + 2, t), (d - 2, t)

    def line(way, j, xx, recv=False):
        zi = z - j if way == 0 else z + j
        s = lcol(c, xx, zi)
        i = j if recv else j + 1
        dev = up_dev if way == 0 else down_dev
        return rc(s, s, ls_.at[way, i - 1, xx], lr.at[way, i - 1, xx], dev)

    def ldc(way, j, xx, recv=False):
        zi = z - j if way == 0 else z + j
        s = lcol(oc if recv else c, xx, zi)
        i = 6 if j == 0 else way * 3 + j - 1
        return rc(s, s, lds.at[i, xx], ldr.at[i, xx], sib)

    def lsend(way, j):
        if way == 0:
            return (z < 3) & (z >= j)
        return (z > 0) & (z + j <= 3)

    def lgot(way, j):
        return z >= j if way == 0 else z + j <= 3

    def last_xy():
        lx(True).wait_recv()
        lhalf(0).start()
        ly(True).wait_recv()
        lhalf(1).start()

    def last_start():
        lhalf(0, True).wait_recv()
        lhalf(1, True).wait_recv()
        for xx in range(2):
            for way in range(2):
                pl.when(lsend(way, 0))(lambda: line(way, 0, xx).start())
        for xx in range(2):
            ldc(0, 0, xx).start()

    def last_step(j):
        for xx in range(2):
            for way in range(2):
                @pl.when(lgot(way, j))
                def _():
                    line(way, j, xx, True).wait_recv()
                    if j < 3:
                        pl.when(lsend(way, j))(lambda: line(way, j, xx).start())
                    ldc(way, j, xx).start()

    def last_ready():
        for xx in range(2):
            ldc(0, 0, xx, True).wait_recv()
            for way in range(2):
                for j in (1, 2, 3):
                    pl.when(lgot(way, j))(lambda: ldc(way, j, xx, True).wait_recv())

    def last_drain():
        lx().wait_send()
        ly().wait_send()
        lhalf(0).wait_send()
        lhalf(1).wait_send()
        for xx in range(2):
            ldc(0, 0, xx).wait_send()
            for way in range(2):
                for j in range(3):
                    pl.when(lsend(way, j))(lambda: line(way, j, xx).wait_send())
                for j in (1, 2, 3):
                    pl.when(lgot(way, j))(lambda: ldc(way, j, xx).wait_send())

    def own_xy(p):
        if p == last:
            lx().start()
            ly().start()
            return
        xcp(p, 0).start()
        ycp(p, 0).start()

    def own_z(p):
        for k in (1, 2, 3):
            zcp(p, k).start()

    def zf(p):
        for k in (1, 2, 3):
            zcp(p, k, True).wait_recv()
            xcp(p, k).start()
            ycp(p, k).start()
        dcp(p, 0).start()

    def xf(p):
        for k in range(4):
            xcp(p, k, True).wait_recv()
        acp(p).start()
        dcp(p, 1).start()
        for k in range(4):
            ycp(p, k, True).wait_recv()
        bcp(p).start()
        dcp(p, 2).start()

    def fin(p):
        acp(p, True).wait_recv()
        bcp(p, True).wait_recv()
        dcp(p, 3).start()

    def ready(p):
        for g in range(4):
            dcp(p, g, True).wait_recv()

    def drain(p):
        for k in (1, 2, 3):
            zcp(p, k).wait_send()
        for k in range(4):
            xcp(p, k).wait_send()
            ycp(p, k).wait_send()
        acp(p).wait_send()
        bcp(p).wait_send()
        for g in range(4):
            dcp(p, g).wait_send()

    SH[3, :, 0:192] = out_w[...].astype(BF).T
    for m, i in enumerate((1, 0, 2)):
        SH[m, :, 0:192] = qkv_w[i].astype(BF)
    W[4 + t, z, y] = up_w[...].astype(BF).reshape(2, 48, D)
    W[8 + t, z, y] = down_w[...].astype(BF).reshape(2, 48, D)
    M[c, x, y, z, 0, 0:4, 0:96] = norm_p[...].astype(BF).astype(F32)
    M[c, x, y, z, 1, 0:6, 0:16] = up_b[...].astype(BF).astype(F32)
    pl.semaphore_wait(bar, 6)
    axc = rc(SH.at[pl.ds(2 * oc, 2)], AX, es.at[0], er.at[0], sib)
    axc.start()
    own_xy(5)
    own_xy(2)
    mz = [rc(M.at[c, x, y, z], M.at[c, x, y, z], ms.at[k - 1], mr.at[k - 1], zn[k]) for k in (1, 2, 3)]
    for cp in mz:
        cp.start()
    axc.wait_recv()
    own_lane = pl.ds(pl.multiple_of(x * HALF, 128), HALF)
    first = jnp.full((96, 192), c, jnp.int32) == 0
    for i in range(2):
        mine, theirs = SH[2 * c + i, :, 0:192], AX[i, :, 0:192]
        both = jnp.concatenate([jnp.where(first, mine, theirs), jnp.where(first, theirs, mine)], axis=1)
        W[2 * c + i, z, y, :, :, own_lane] = both.reshape(2, 48, HALF)
        own_z(i)
        own_xy(i)

    for cp in mz:
        cp.wait_recv()
    mx = rc(M.at[c, x, y], M.at[c, x, y], ms.at[3], mr.at[3], xn)
    mx.start()
    zf(0)
    own_z(2)
    last_xy()
    own_xy(3)
    zf(1)
    own_z(3)
    own_xy(4)
    xf(0)
    xf(1)
    mx.wait_recv()
    my = rc(M.at[c, :, y], M.at[c, :, y], ms.at[4], mr.at[4], yn)
    my.start()
    last_start()
    own_z(4)
    zf(2)
    fin(0)
    ready(0)

    def mat(m):
        return W[m].reshape(D, D)

    load_hid.wait()
    QKV[1] = dot(hid[...], mat(0), NN).astype(BF)
    QKV[2] = dot(hid[...], mat(2), NN).astype(BF)
    kvc = rc(QKV.at[pl.ds(1, 2)], KVO, es.at[1], er.at[1], sib)
    kvc.start()
    fin(1)
    my.wait_recv()
    md = rc(M.at[c], M.at[c], ms.at[5], mr.at[5], sib)
    md.start()
    ready(1)
    QKV[0] = dot(hid[...], mat(1), NN).astype(BF)
    kvc.wait_recv()

    kd = kind[x]
    lane = lax.broadcasted_iota(jnp.int32, (1, 128), 1)
    keylane = lax.broadcasted_iota(jnp.int32, (1, ROWS), 1)
    low_lane = lane < 64

    def flips(hp):
        fa = kd * swap[2 * hp]
        fb = kd * swap[2 * hp + 1]
        return jnp.where(low_lane, jnp.full((1, 128), fa, jnp.int32), jnp.full((1, 128), fb, jnp.int32)) == 1

    def pair_lanes(hp):
        return pl.ds(pl.multiple_of(hp * 128, 128), 128)

    def attn_fwd(hp):
        ls = pair_lanes(hp)
        fl = flips(hp)
        kk = jnp.where(fl, KVO[0, :, ls], QKV[1, :, ls])
        vv = jnp.where(fl, KVO[1, :, ls], QKV[2, :, ls])
        for rb in range(2):
            rows = slice(rb * 256, rb * 256 + 256)
            q = QKV[0, rows, ls] * jnp.asarray(0.125, BF)
            for e in range(2):
                sw = swap[2 * hp + e]
                qe = jnp.where(low_lane if e == 0 else ~low_lane, q, jnp.zeros_like(q))
                s = dot(qe, kk, NT)
                kb = jnp.where(keylane >= 256, 1, 0)
                same = jnp.where(kb == rb, 0, 1)
                seen = (same == jnp.full((1, ROWS), sw, jnp.int32)) | (jnp.full((1, ROWS), kd, jnp.int32) == 1)
                s = s + jnp.where(seen, 0.0, NEGATIVE)
                top = jnp.max(s, axis=1, keepdims=True)
                pw = jnp.exp(s - top)
                tot = jnp.sum(pw, axis=1, keepdims=True)
                a = (pw * (1.0 / tot)).astype(BF)
                AT[2 * hp + e, rows, :] = a
        outs = [dot(AT[2 * hp + e], vv, NN) for e in range(2)]
        CTX[:, ls] = jnp.where(low_lane, outs[0], outs[1]).astype(BF)

    zf(3)

    @pl.loop(0, 6)
    def forward_pairs(hp):
        attn_fwd(hp)
        pl.when(hp == 0)(lambda: xf(2))
        pl.when(hp == 1)(lambda: last_step(1))
        pl.when(hp == 2)(lambda: xf(3))

        @pl.when(hp == 4)
        def _():
            zf(4)
            fin(2)

    md.wait_recv()
    def picks(width, step, count):
        si = lax.broadcasted_iota(jnp.int32, (128, width), 0)
        sj = lax.broadcasted_iota(jnp.int32, (128, width), 1)
        return lambda dd: jnp.where((si < count) & (sj == si + dd * step), 1.0, 0.0).astype(BF)

    norm_pick, bias_pick = picks(D, 96, 96), picks(128, 16, 16)
    norm_acc = jnp.zeros((16, D), F32)
    bias_acc = jnp.zeros((32, 128), F32)
    for zi in range(4):
        for yi in range(2):
            dd = 2 * zi + yi
            norm_acc = norm_acc + dot(M[c, x, yi, zi].reshape(16, 128).astype(BF), norm_pick(dd), NN)
            bias_acc = bias_acc + dot(M[:, :, yi, zi, 1].reshape(32, 128).astype(BF), bias_pick(dd), NN)
    NB[0] = norm_acc[0:8]
    for tt in range(4):
        row = (tt % 2 * 2 + tt // 2) * 8
        for r in range(6):
            NB[1, tt : tt + 1, r * 128 : r * 128 + 128] = bias_acc[row + r : row + r + 1]

    igrad[...] = dot(CTX[...], mat(3), NT)
    fin(3)
    last_step(2)

    def ln_rows(i):
        return pl.ds(pl.multiple_of(i * 128, 128), 128)

    g1, b1 = NB[0, 0:1, :], NB[0, 1:2, :]
    g2, b2 = NB[0, 2:3, :], NB[0, 3:4, :]

    @pl.loop(0, 4)
    def _(i):
        rs = ln_rows(i)
        r = hid[rs, :].astype(F32) + igrad[rs, :]
        cen = r - jnp.mean(r, axis=1, keepdims=True)
        rstd = lax.rsqrt(jnp.mean(cen * cen, axis=1, keepdims=True) + EPSILON)
        xh = cen * rstd
        XH[rs, :] = xh
        RS1[rs, :] = rstd
        FI[rs, :] = (xh * g1 + b1).astype(BF)

    xf(4)
    ready(2)
    ready(3)
    for tt in range(4):
        if tt == 3:
            fin(4)
        pre = dot(FI[...], mat(4 + tt), NN) + NB[1, tt : tt + 1, :]
        cdf = 0.5 * (1.0 + lax.erf(pre * math.sqrt(0.5)))
        ACT[tt] = (pre * cdf).astype(BF)
        GP[tt] = (cdf + pre * (jnp.exp(-0.5 * pre * pre) * (1.0 / math.sqrt(2.0 * math.pi)))).astype(BF)

    last_step(3)
    ready(4)

    def half_mat(m, h):
        return W[m, :, :, :, :, h * HALF : h * HALF + HALF].reshape(D, HALF)

    acc = dot(ACT[0, :, 0:HALF], half_mat(8, 0), NT)
    for tt in range(1, 4):
        acc = acc + dot(ACT[tt, :, 0:HALF], half_mat(8 + tt, 0), NT)
    igrad[...] = acc
    last_ready()
    acc = dot(ACT[0, :, HALF:D], half_mat(8, 1), NT)
    for tt in range(1, 4):
        acc = acc + dot(ACT[tt, :, HALF:D], half_mat(8 + tt, 1), NT)
    igrad[...] += acc

    V[...] = jnp.zeros_like(V)
    load_cot.wait()

    @pl.loop(0, 4)
    def _(i):
        rs = ln_rows(i)
        r = XH[rs, :] * g1 + b1 + igrad[rs, :]
        cen = r - jnp.mean(r, axis=1, keepdims=True)
        rstd = lax.rsqrt(jnp.mean(cen * cen, axis=1, keepdims=True) + EPSILON)
        n2 = cen * rstd
        mixed[rs, :] = (n2 * g2 + b2).astype(BF)
        co = cot[rs, :].astype(F32)
        e = co * g2
        gr = rstd * (e - jnp.mean(e, axis=1, keepdims=True) - n2 * jnp.mean(e * n2, axis=1, keepdims=True))
        igrad[rs, :] = gr
        GF[rs, :] = gr.astype(BF)
        V[2:3, :] += jnp.sum(co * n2, axis=0, keepdims=True)
        V[3:4, :] += jnp.sum(co, axis=0, keepdims=True)

    save_mixed.start()

    def sq(r, xx):
        if r < 2:
            return SQ.at[r, xx]
        return W.at[8 + 2 * (r // 2 - 1) + xx, :, :, :, :, pl.ds((r % 2) * HALF, HALF)]

    def pb(r, xx, *rest):
        if r < 4:
            return PB.at[(r, xx) + rest]
        rest = rest + (slice(None),) * (4 - len(rest))
        return W.at[(4 + xx,) + rest + (pl.ds((r % 2) * HALF, HALF),)]

    def pb_all(r, *rest):
        if r < 4:
            return PB.at[(r, slice(None)) + rest]
        rest = rest + (slice(None),) * (4 - len(rest))
        return W.at[(pl.ds(4, 2),) + rest + (pl.ds((r % 2) * HALF, HALF),)]

    def b_sib(r, xx):
        return rc(sq(r, xx), SR.at[SIB_SLOT[r], xx], qs.at[r, xx], qr.at[r, xx], sib)

    ALL = slice(None)

    def b_a(r):
        return rc(pb(r, ox, ALL, ALL, 0), RA.at[r % SLOTS], as_.at[r], ar.at[r], xn)

    def b_b(r):
        return rc(pb_all(r, ALL, oy, 1), RB.at[r % SLOTS], bs.at[r], br.at[r], yn)

    def b_a2(r, k):
        dst = RO.at[r, 0] if k == 0 else RA2.at[r % SLOTS, k - 1]
        return rc(pb(r, x, zz[k], oy, 0), dst, a2s.at[r, k], a2r.at[r, k], yn)

    def b_b2(r, k):
        dst = RO.at[r, 1] if k == 0 else RB2.at[r % SLOTS, k - 1]
        return rc(pb(r, ox, zz[k], y, 1), dst, b2s.at[r, k], b2r.at[r, k], xn)

    def b_z(r, k):
        return rc(pb(r, x, zz[k], y), RZ.at[r, k - 1], rzs.at[r, k - 1], rzr.at[r, k - 1], zn[k])

    def zl(way, tgt, xx, recv=False):
        dst = (RU if way == 0 else RD).at[tgt, xx]
        dev = up_dev if way == 0 else down_dev
        return rc(PB.at[0, xx, tgt], dst, zls.at[way, tgt, xx], zlr.at[way, tgt, xx], dev)

    def zl_sends(way, tgt):
        return z < tgt if way == 0 else z > tgt

    def zl_got(way, tgt):
        return (z > 0) & (z <= tgt) if way == 0 else (z < 3) & (z >= tgt)

    def zl_first():
        for tgt in range(3):
            for xx in range(2):
                pl.when(z == 0)(lambda: zl(0, 3 - tgt, xx).start())
                pl.when(z == 3)(lambda: zl(1, tgt, xx).start())

    def zl_pass(way, at, tgt):
        for xx in range(2):
            @pl.when(z == at)
            def _():
                zl(way, tgt, xx).wait_recv()
                add(PB.at[0, xx, tgt], (RU if way == 0 else RD).at[tgt, xx])
                zl(way, tgt, xx).start()

    def zl_last():
        for way in range(2):
            for tgt in range(4):
                @pl.when((z == tgt) & ((z > 0) if way == 0 else (z < 3)))
                def _():
                    for xx in range(2):
                        zl(way, tgt, xx).wait_recv()
                        add(PB.at[0, xx, tgt], (RU if way == 0 else RD).at[tgt, xx])

    def b0(i):
        src, dst, dev = (
            (PB.at[0, ox, z, :, 0], R0.at[0], xn),
            (PB.at[0, :, z, oy, 1], R0.at[1], yn),
            (PB.at[0, x, z, oy, 0], R0.at[2, 0], yn),
            (PB.at[0, ox, z, y, 1], R0.at[2, 1], xn),
        )[i]
        return rc(src, dst, z0s.at[i], z0r.at[i], dev)

    def xy0_first():
        b0(0).start()
        b0(1).start()

    def xy0_second():
        b0(0).wait_recv()
        add(PB.at[0, x, z, :, 0], R0.at[0])
        b0(2).start()
        b0(1).wait_recv()
        add(PB.at[0, :, z, y, 1], R0.at[1])
        b0(3).start()

    def xy0_last():
        b0(2).wait_recv()
        b0(3).wait_recv()
        tot = PB[0, x, z, y].astype(F32) + R0[2].astype(F32)
        g_down[:, 0:HALF] = tot.reshape(96, HALF)

    def rs0_drain():
        for xx in range(2):
            b_sib(0, xx).wait_send()
        for i in range(4):
            b0(i).wait_send()
        for way in range(2):
            for tgt in range(4):
                for xx in range(2):
                    pl.when(zl_sends(way, tgt))(lambda: zl(way, tgt, xx).wait_send())

    def credit(sem, dev, r):
        if r + SLOTS < PIECES:
            pl.semaphore_signal(sem, inc=1, device_id=dev, device_id_type=pl.DeviceIdType.MESH)

    def need(sem, r):
        if r >= SLOTS + (sem is not c_sib):
            pl.semaphore_wait(sem, 1)

    def part(r, xx, core):
        if r < 4:
            src = ACT if r < 2 else GP
            lhs = GF if r < 2 else FI
            h = r % 2
            return dot(lhs[...], src[2 * xx + core, :, h * HALF : h * HALF + HALF], TN)
        raise ValueError

    def part_attn(m, xx):
        if m < 3:
            return dot(hid[...], ACT[(1, 0, 2)[m], :, xx * HALF : xx * HALF + HALF], TN)
        return dot(GF[...], CTX[:, xx * HALF : xx * HALF + HALF], TN)

    def gen_sib(r):
        need(c_sib, r)
        for xx in range(2):
            if r < 4:
                sq(r, xx)[...] = part(r, xx, oc).astype(BF).reshape(4, 2, 2, 48, HALF)
            else:
                for core in range(2):
                    @pl.when(oc == core)
                    def _():
                        sq(r, xx)[...] = part_attn(2 * core + 5 - r, xx).astype(BF).reshape(4, 2, 2, 48, HALF)
            b_sib(r, xx).start()

    def own_part(r, xx, grad):
        v = grad.reshape(4, 2, 2, 48, HALF) + SR[SIB_SLOT[r], xx].astype(F32)
        pb(r, xx)[...] = v.astype(BF)

    def gen_own(r):
        for xx in range(2):
            b_sib(r, xx).wait_recv()
            if r < 4:
                own_part(r, xx, part(r, xx, c))
            else:
                for core in range(2):
                    @pl.when(c == core)
                    def _():
                        own_part(r, xx, part_attn(2 * core + 5 - r, xx))
        credit(c_sib, sib, r)
        if r == 0:
            zl_first()
            return
        need(c_a, r)
        b_a(r).start()
        need(c_b, r)
        b_b(r).start()

    def add(dst, src):
        dst[...] = (dst[...].astype(F32) + src[...].astype(F32)).astype(BF)

    def st1(r):
        q = r % SLOTS
        b_a(r).wait_recv()
        add(pb(r, x, ALL, ALL, 0), RA.at[q])
        credit(c_a, xn, r)
        need(c_a2, r)
        for k in (2, 3, 1):
            b_a2(r, k).start()
        b_b(r).wait_recv()
        add(pb_all(r, ALL, y, 1), RB.at[q])
        credit(c_b, yn, r)
        need(c_b2, r)
        for k in (2, 3, 1):
            b_b2(r, k).start()

    def st2o(r):
        b_a2(r, 0).start()
        b_b2(r, 0).start()

    def st2(r):
        q = r % SLOTS
        for k in (2, 3, 1):
            b_a2(r, k).wait_recv()
            add(pb(r, x, zz[k], y, 0), RA2.at[q, k - 1])
            b_b2(r, k).wait_recv()
            add(pb(r, x, zz[k], y, 1), RB2.at[q, k - 1])
            b_z(r, k).start()
        credit(c_a2, yn, r)
        credit(c_b2, xn, r)

    def fx(r):
        m = g_attn.at[2 * c + 5 - r]
        return rc(m, m, es.at[r - 1], er.at[r - 1], sib)

    def st3(r):
        tot = pb(r, x, z, y)[...].astype(F32)
        for k in (2, 3, 1):
            b_z(r, k).wait_recv()
            tot = tot + RZ[r, k - 1].astype(F32)
        b_a2(r, 0).wait_recv()
        b_b2(r, 0).wait_recv()
        tot = (tot + RO[r].astype(F32)).reshape(96, HALF)
        h = r % 2
        if r < 2:
            g_down[:, h * HALF : h * HALF + HALF] = tot
        elif r < 4:
            g_up[:, h * HALF : h * HALF + HALF] = tot
        else:
            g_attn[2 * c + 5 - r] = tot
            fx(r).start()

    def rs_drain(r):
        for xx in range(2):
            b_sib(r, xx).wait_send()
        b_a(r).wait_send()
        b_b(r).wait_send()
        for k in range(4):
            b_a2(r, k).wait_send()
            b_b2(r, k).wait_send()
        for k in (1, 2, 3):
            b_z(r, k).wait_send()

    def gact(h):
        ls = slice(h * HALF, h * HALF + HALF)
        for tt in range(4):
            ga = dot(GF[...], half_mat(8 + tt, h), NN)
            gp = (ga * GP[tt, :, ls].astype(F32)).astype(BF)
            GP[tt, :, ls] = gp
            V[4 + tt : 5 + tt, ls] = jnp.sum(gp.astype(F32), axis=0, keepdims=True)

    gen_sib(1)
    gen_sib(0)
    for p in range(PIECES - 1):
        drain(p)
    last_drain()
    gen_own(1)
    gen_own(0)
    gact(0)
    gen_sib(2)
    gact(1)
    gen_own(2)
    zl_pass(0, 1, 3)
    zl_pass(1, 2, 0)
    gen_sib(3)
    st1(1)

    acc = dot(GP[0], mat(4), NT)
    for tt in range(1, 4):
        acc = acc + dot(GP[tt], mat(4 + tt), NT)
    igrad[...] += acc
    gen_own(3)

    @pl.loop(0, 4)
    def _(i):
        rs = ln_rows(i)
        gn = igrad[rs, :]
        xh = XH[rs, :]
        e = gn * g1
        gr = RS1[rs, :] * (e - jnp.mean(e, axis=1, keepdims=True) - xh * jnp.mean(e * xh, axis=1, keepdims=True))
        igrad[rs, :] = gr
        GF[rs, :] = gr.astype(BF)
        V[0:1, :] += jnp.sum(gn * xh, axis=0, keepdims=True)
        V[1:2, :] += jnp.sum(gn, axis=0, keepdims=True)

    vc = [
        rc(V, VR.at[0], vs.at[0], vr.at[0], sib),
        rc(V, VR.at[1], vs.at[1], vr.at[1], xn),
        rc(V, VR.at[2], vs.at[2], vr.at[2], yn),
    ] + [rc(V, VR.at[2 + k], vs.at[2 + k], vr.at[2 + k], zn[k]) for k in (1, 2, 3)]

    def v_step(i):
        vc[i].wait()
        V[...] += VR[i]

    vc[0].start()
    zl_pass(0, 1, 2)
    zl_pass(1, 2, 1)
    zl_pass(0, 2, 3)
    zl_pass(1, 1, 0)

    FI[...] = dot(GF[...], mat(3), NN).astype(BF)
    v_step(0)
    vc[1].start()

    def attn_bwd(hp):
        ls = pair_lanes(hp)
        fl = flips(hp)
        kk = jnp.where(fl, KVO[0, :, ls], QKV[1, :, ls])
        vv = jnp.where(fl, KVO[1, :, ls], QKV[2, :, ls])
        q = QKV[0, :, ls]
        do = FI[:, ls]
        dvs, dqs, dks = [], [], []
        for e in range(2):
            dvs.append(dot(AT[2 * hp + e], do, TN))
            for rb in range(2):
                rows = slice(rb * 256, rb * 256 + 256)
                dr = do[rows]
                dp = dot(jnp.where(low_lane if e == 0 else ~low_lane, dr, jnp.zeros_like(dr)), vv, NT)
                af = AT[2 * hp + e, rows, :].astype(F32)
                w = af * dp
                GP[2 + e, rows, 0:ROWS] = (w - af * jnp.sum(w, axis=1, keepdims=True)).astype(BF)
            gs = GP[2 + e, :, 0:ROWS]
            dqs.append(dot(gs, kk, NN))
            dks.append(dot(gs, q, TN))
        ACT[0, :, ls] = (jnp.where(low_lane, dqs[0], dqs[1]) * 0.125).astype(BF)
        GP[0, :, ls] = (jnp.where(low_lane, dks[0], dks[1]) * 0.125).astype(BF)
        GP[1, :, ls] = jnp.where(low_lane, dvs[0], dvs[1]).astype(BF)

    def dkv(i):
        ls = pl.ds(i * HALF, HALF)
        return rc(GP.at[pl.ds(0, 2), :, ls], DKVR.at[:, :, ls], es.at[2 + 3 * i], er.at[2 + 3 * i], sib)

    @pl.loop(0, 6)
    def backward_pairs(hp):
        attn_bwd(hp)

        @pl.when(hp == 1)
        def _():
            st1(2)
            st2(1)

        pl.when(hp == 2)(lambda: dkv(0).start())

        @pl.when(hp == 3)
        def _():
            st1(3)
            st2o(1)
            st2o(2)
            st2o(3)

    gen_sib(4)
    dkv(1).start()
    st2(2)
    v_step(1)
    vc[2].start()
    gen_own(4)
    dkv(0).wait()
    dkv(1).wait()

    def pick(hp):
        ls = pair_lanes(hp)
        fl = flips(hp)
        ACT[1, :, ls] = jnp.where(fl, DKVR[0, :, ls], GP[0, :, ls])
        ACT[2, :, ls] = jnp.where(fl, DKVR[1, :, ls], GP[1, :, ls])

    pl.loop(0, 6)(pick)

    gen_sib(5)
    zl_last()
    xy0_first()
    st2(3)
    v_step(2)
    for k in (1, 2, 3):
        vc[2 + k].start()
    acc = dot(ACT[0], mat(1), NT)
    for m in (1, 2):
        acc = acc + dot(ACT[m], mat((1, 0, 2)[m]), NT)
    igrad[...] += acc
    st1(4)
    gen_own(5)
    st2(4)
    xy0_second()
    st2o(4)
    for r in (1, 2, 3):
        st3(r)
    st1(5)
    st2o(5)
    xy0_last()
    st2(5)
    st3(4)
    st3(5)
    for k in (1, 2, 3):
        vc[2 + k].wait()
    g_misc[...] = V[...] + VR[3] + VR[4] + VR[5]
    save_mixed.wait()
    rs0_drain()
    for r in range(1, PIECES):
        rs_drain(r)
    for cp in mz:
        cp.wait_send()
    mx.wait_send()
    my.wait_send()
    md.wait_send()
    axc.wait_send()
    kvc.wait_send()
    fx(4).wait()
    fx(5).wait()


def finish_kernel(
    mixed, igrad, ga, gu, gd, gm, o_mixed, o_igrad, o_qkv, o_out, o_up, o_bias, o_down, o_norm,
    v_igrad, v_mixed, v_up, v_down, v_ga, v_gm, w_qkv, w_out, w_bias, w_norm, tmp, sem,
):
    copy = pltpu.make_async_copy
    load_small = [copy(gm, v_gm, sem.at[0, 8]), copy(ga, v_ga, sem.at[0, 9])]
    parts = [(igrad, v_igrad, o_igrad, i * 128, 128) for i in range(4)]
    parts += [(mixed, v_mixed, o_mixed, i * 256, 256) for i in range(2)]
    parts += [(gu, v_up, o_up, 0, 96), (gd, v_down, o_down, 0, 96)]
    loads, stores = [], []
    for i, (src, mid, dst, at, n) in enumerate(parts):
        rows = pl.ds(at, n)
        loads.append(copy(src.at[rows], mid.at[rows], sem.at[0, i]))
        stores.append(copy(mid.at[rows], dst.at[rows], sem.at[1, i]))
    for cp in load_small + loads:
        cp.start()
    dd = lax.axis_index("dp")
    t = lax.axis_index("tensor")
    exact = dict(preferred_element_type=F32, precision=lax.Precision.HIGHEST)
    si = lax.broadcasted_iota(jnp.int32, (D, 128), 0)
    sj = lax.broadcasted_iota(jnp.int32, (D, 128), 1)
    norm_pick = jnp.where(si == sj + dd * 96, 1.0, 0.0).astype(F32)
    bias_pick = jnp.where(si[0:128] == sj[0:128] + dd * 16, 1.0, 0.0).astype(F32)
    sub = lax.broadcasted_iota(jnp.int32, (8, D), 0)
    load_small[0].wait()
    norm = lax.dot_general(v_gm[...], norm_pick, NN, **exact)
    w_norm[...] = jnp.sum(jnp.where(sub[:, 0:128] == t, norm, 0.0), axis=0, keepdims=True)[:, 0:96]
    row = jnp.sum(jnp.where(sub == 4 + t, v_gm[...], 0.0), axis=0, keepdims=True)
    for r in range(6):
        tmp[r : r + 1] = row[:, r * 128 : r * 128 + 128]
    w_bias[...] = lax.dot_general(tmp[...], bias_pick, NN, **exact)[0:6, 0:16]
    load_small[1].wait()
    first = jnp.full((96, 192), lax.rem(t, 2), jnp.int32) == 0
    for m in range(4):
        v = jnp.where(first, v_ga[m, :, 0:192], v_ga[m, :, 192:HALF])
        if m < 3:
            w_qkv[(1, 0, 2)[m]] = v
        else:
            w_out[...] = v.T
    small = ((w_norm, o_norm), (w_bias, o_bias), (w_qkv, o_qkv), (w_out, o_out))
    for i, (src, dst) in enumerate(small):
        stores.append(copy(src, dst, sem.at[1, 8 + i]))
        stores[-1].start()
    for load, store in zip(loads, stores):
        load.wait()
        store.start()
    for cp in stores:
        cp.wait()


def scratch():
    vm = pltpu.VMEM
    dma = lambda *s: pltpu.SemaphoreType.DMA(s)
    n = PIECES
    return [
        vm((ROWS, D), BF), vm((ROWS, D), BF), vm((ROWS, D), BF), vm((12, 4, 2, 2, 48, D), BF), vm((4, 96, 256), BF), vm((2, 96, 256), BF), vm((3, ROWS, D), BF), vm((2, ROWS, D), BF),
        vm((12, ROWS, ROWS), BF), vm((ROWS, D), BF), vm((ROWS, D), F32), vm((ROWS, 1), F32), vm((ROWS, D), BF),
        vm((4, ROWS, D), BF), vm((4, ROWS, D), BF), vm((ROWS, D), BF), vm((2, ROWS, D), BF),
        vm((2, 2, 2, 4, 2, 8, 128), F32), vm((2, 8, D), F32), vm((8, D), F32), vm((6, 8, D), F32),
        vm((2, 2, 4, 2, 2, 48, HALF), BF), vm((SLOTS, 2, 4, 2, 2, 48, HALF), BF), vm((4, 2, 4, 2, 2, 48, HALF), BF),
        vm((SLOTS, 4, 2, 48, HALF), BF), vm((SLOTS, 2, 4, 48, HALF), BF), vm((SLOTS, 3, 48, HALF), BF),
        vm((SLOTS, 3, 48, HALF), BF), vm((n, 2, 48, HALF), BF), vm((n, 3, 2, 48, HALF), BF),
        vm((4, 2, 2, 2, 48, HALF), BF), vm((4, 2, 2, 2, 48, HALF), BF), vm((3, 2, 48, HALF), BF),
        dma(n, 3), dma(n, 3), dma(n, 4), dma(n, 4), dma(n, 4), dma(n, 4), dma(n, 2), dma(n, 2), dma(n, 4), dma(n, 4),
        dma(6), dma(6), dma(6), dma(6),
        dma(n, 2), dma(n, 2), dma(n), dma(n), dma(n), dma(n), dma(n, 4), dma(n, 4), dma(n, 4), dma(n, 4), dma(n, 3), dma(n, 3), dma(6), dma(6),
        dma(2, 3, 2), dma(2, 3, 2), dma(7, 2), dma(7, 2), dma(2, 4, 2), dma(2, 4, 2), dma(4), dma(4), dma(3),
        pltpu.SemaphoreType.REGULAR, pltpu.SemaphoreType.REGULAR, pltpu.SemaphoreType.REGULAR,
        pltpu.SemaphoreType.REGULAR, pltpu.SemaphoreType.REGULAR,
    ]


def whole_layer(
    hidden_in, qkv_weight, out_weight, up_weight, up_bias, down_weight, norm_params, cotangent, head_swap, slot_kind
):
    any_ = pl.BlockSpec(memory_space=pl.ANY)
    vmem = pl.BlockSpec(memory_space=pltpu.VMEM)
    smem = pl.BlockSpec(memory_space=pltpu.SMEM)
    sds = jax.ShapeDtypeStruct
    mixed, igrad, ga, gu, gd, gm = pl.pallas_call(
        layer_kernel,
        out_shape=(
            sds((ROWS, D), BF), sds((ROWS, D), F32), sds((4, 96, HALF), F32),
            sds((96, D), F32), sds((96, D), F32), sds((8, D), F32),
        ),
        in_specs=[any_] + [vmem] * 6 + [any_] + [smem] * 2,
        out_specs=(any_,) + (vmem,) * 5,
        scratch_shapes=scratch(),
        compiler_params=pltpu.CompilerParams(
            collective_id=0, has_side_effects=True, vmem_limit_bytes=63 * 2**20
        ),
        name="layer",
    )(
        hidden_in, qkv_weight, out_weight, up_weight, up_bias, down_weight.T, norm_params, cotangent, head_swap, slot_kind
    )
    *outs, bias_grad, down_grad, norm_grad = pl.pallas_call(
        finish_kernel,
        out_shape=(
            sds((ROWS, D), BF), sds((ROWS, D), F32), sds((3, 96, 192), F32), sds((192, 96), F32),
            sds((96, D), F32), sds((6, 16), F32), sds((96, D), F32), sds((1, 96), F32),
        ),
        in_specs=[any_] * 6,
        out_specs=(any_,) * 8,
        scratch_shapes=[
            pltpu.VMEM((ROWS, D), F32), pltpu.VMEM((ROWS, D), BF), pltpu.VMEM((96, D), F32), pltpu.VMEM((96, D), F32),
            pltpu.VMEM((4, 96, HALF), F32), pltpu.VMEM((8, D), F32), pltpu.VMEM((3, 96, 192), F32),
            pltpu.VMEM((192, 96), F32), pltpu.VMEM((6, 16), F32), pltpu.VMEM((1, 96), F32), pltpu.VMEM((8, 128), F32),
            pltpu.SemaphoreType.DMA((2, 12)),
        ],
        compiler_params=pltpu.CompilerParams(vmem_limit_bytes=63 * 2**20),
        name="finish",
    )(mixed, igrad, ga, gu, gd, gm)
    return (*outs, bias_grad, down_grad.T, norm_grad)


def norm_rows(residual, scales, offset):
    center = residual - jnp.mean(residual, axis=-1, keepdims=True)
    spread = jnp.mean(center * center, axis=-1, keepdims=True)
    return center * lax.rsqrt(spread + EPSILON) * scales + offset


def smooth_gate(values):
    return jax.nn.gelu(values, approximate=False)


def arrange(queries, keys_in, values_in, slot_type, local_swaps):
    slot_len, head_count, head_size = queries.shape
    half_len = slot_len // 2
    quarter = half_len // 2
    shape_four = (2, half_len, head_count, head_size)
    query_half = queries.reshape(shape_four)
    key_half = keys_in.reshape(shape_four)
    value_half = values_in.reshape(shape_four)
    flipped = (local_swaps * slot_type == 1)[None, None, :, None]
    key_pick = jnp.where(flipped, key_half[::-1], key_half)
    value_pick = jnp.where(flipped, value_half[::-1], value_half)
    blocks = jnp.arange(half_len, dtype=jnp.int32) // quarter
    matching = (
        jnp.bitwise_xor(blocks[None, :, None], local_swaps[:, None, None]) == blocks[None, None, :]
    )
    allowed = jnp.logical_or(slot_type == 1, matching)
    return (query_half, key_pick, value_pick, allowed, flipped)


def masked_scores(query_half, key_pick, allowed):
    scale = 1.0 / math.sqrt(query_half.shape[-1])
    scores = (
        jnp.einsum("jqhd,jkhd->jhqk", query_half, key_pick, preferred_element_type=jnp.float32)
        * scale
    )
    return jnp.where(allowed[None], scores, NEGATIVE)


def slot_forward(inputs, local_swaps):
    queries, keys_in, values_in, slot_type = inputs
    query_half, key_pick, value_pick, allowed, flipped = arrange(
        queries, keys_in, values_in, slot_type, local_swaps
    )
    scores = masked_scores(query_half, key_pick, allowed)
    largest = jnp.max(scores, axis=-1, keepdims=True)
    powers = jnp.exp(scores - largest)
    totals = jnp.sum(powers, axis=-1, keepdims=True)
    attention = (powers / totals).astype(jnp.bfloat16)
    context = jnp.einsum(
        "jhqk,jkhd->jqhd", attention, value_pick, preferred_element_type=jnp.float32
    )
    return (context.astype(jnp.bfloat16).reshape(queries.shape[0], -1), largest + jnp.log(totals))


def slot_backward(inputs, local_swaps):
    queries, keys_in, values_in, slot_type, log_totals, grad_out = inputs
    slot_len, head_count, head_size = queries.shape
    scale = 1.0 / math.sqrt(head_size)
    query_half, key_pick, value_pick, allowed, flipped = arrange(
        queries, keys_in, values_in, slot_type, local_swaps
    )
    attention = jnp.exp(masked_scores(query_half, key_pick, allowed) - log_totals)
    grad_half = grad_out.reshape(query_half.shape)
    grad_vpick = jnp.einsum(
        "jhqk,jqhd->jkhd",
        attention.astype(jnp.bfloat16),
        grad_half,
        preferred_element_type=jnp.float32,
    ).astype(jnp.bfloat16)
    grad_attention = jnp.einsum(
        "jqhd,jkhd->jhqk", grad_half, value_pick, preferred_element_type=jnp.float32
    )
    row_dots = jnp.sum(attention * grad_attention, axis=-1, keepdims=True)
    grad_scores = (attention * (grad_attention - row_dots)).astype(jnp.bfloat16)
    grad_query = (
        jnp.einsum("jhqk,jkhd->jqhd", grad_scores, key_pick, preferred_element_type=jnp.float32)
        * scale
    ).astype(jnp.bfloat16)
    grad_kpick = (
        jnp.einsum("jhqk,jqhd->jkhd", grad_scores, query_half, preferred_element_type=jnp.float32)
        * scale
    ).astype(jnp.bfloat16)
    grad_key = jnp.where(flipped, grad_kpick[::-1], grad_kpick)
    grad_value = jnp.where(flipped, grad_vpick[::-1], grad_vpick)
    return (
        grad_query.reshape(slot_len, -1),
        grad_key.reshape(slot_len, -1),
        grad_value.reshape(slot_len, -1),
    )


def per_device(
    hidden_in,
    qkv_weight,
    out_weight,
    up_weight,
    up_bias,
    down_weight,
    norm_params,
    cotangent,
    head_swap,
    slot_kind,
):
    tensor_count = lax.axis_size("tensor")
    tensor_rank = lax.axis_index("tensor")
    heads_here = head_swap.shape[0] // tensor_count
    local_swaps = lax.dynamic_slice_in_dim(head_swap, tensor_rank * heads_here, heads_here)
    qkv_low = qkv_weight.astype(jnp.bfloat16)
    out_low = out_weight.astype(jnp.bfloat16)
    norm_low = norm_params.astype(jnp.bfloat16)
    up_low = up_weight.astype(jnp.bfloat16)
    bias_low = up_bias.astype(jnp.bfloat16)
    down_low = down_weight.astype(jnp.bfloat16)
    qkv_full, out_full, norm_full = (
        lax.all_gather(qkv_low, "dp", axis=1, tiled=True),
        lax.all_gather(out_low, "dp", axis=1, tiled=True),
        lax.all_gather(norm_low, "dp", axis=1, tiled=True),
    )
    norm_gain = norm_full.astype(jnp.float32)
    full_in = lax.all_gather(hidden_in, "tensor", axis=0, tiled=True)
    group_rows = full_in.shape[0]
    local_width = qkv_full.shape[2]
    head_size = local_width // heads_here
    slot_count = group_rows // LONG_LEN

    def by_slot(rows):
        return rows.reshape(slot_count, LONG_LEN, heads_here, head_size)

    projected = jnp.einsum(
        "td,cde->cte", full_in, qkv_full, preferred_element_type=jnp.float32
    ).astype(jnp.bfloat16)
    context, log_totals = lax.map(
        partial(slot_forward, local_swaps=local_swaps),
        (by_slot(projected[0]), by_slot(projected[1]), by_slot(projected[2]), slot_kind),
    )
    context = context.reshape(group_rows, local_width)
    rows = context
    attn_share = lax.psum_scatter(
        jnp.dot(rows, out_full, preferred_element_type=jnp.float32).astype(jnp.bfloat16),
        "tensor",
        scatter_dimension=0,
        tiled=True,
    ).astype(jnp.float32)
    resid_one = hidden_in.astype(jnp.float32) + attn_share
    normed_one, norm_one_back = jax.vjp(norm_rows, resid_one, norm_gain[0], norm_gain[1])
    up_full, bias_full, down_full = (
        lax.all_gather(up_low, "dp", axis=0, tiled=True),
        lax.all_gather(bias_low, "dp", axis=1, tiled=True),
        lax.all_gather(down_low, "dp", axis=1, tiled=True),
    )
    ffn_in = lax.all_gather(normed_one.astype(jnp.bfloat16), "tensor", axis=0, tiled=True)
    pre = jnp.dot(ffn_in, up_full, preferred_element_type=jnp.float32) + bias_full.reshape(
        -1
    ).astype(jnp.float32)
    act_value, gate_back = jax.vjp(smooth_gate, pre)
    act = act_value.astype(jnp.bfloat16)
    rows = act
    ffn_share = lax.psum_scatter(
        jnp.dot(rows, down_full, preferred_element_type=jnp.float32).astype(jnp.bfloat16),
        "tensor",
        scatter_dimension=0,
        tiled=True,
    ).astype(jnp.float32)
    normed_two, norm_two_back = jax.vjp(
        norm_rows, normed_one + ffn_share, norm_gain[2], norm_gain[3]
    )
    mixed = normed_two.astype(jnp.bfloat16)
    grad_resid_two, grad_gain_two, grad_bias_two = norm_two_back(cotangent.astype(jnp.float32))
    grad_ffn = lax.all_gather(grad_resid_two.astype(jnp.bfloat16), "tensor", axis=0, tiled=True)
    grad_down = jnp.einsum("tf,td->fd", act, grad_ffn, preferred_element_type=jnp.float32)
    grad_act = jnp.einsum("td,fd->tf", grad_ffn, down_full, preferred_element_type=jnp.float32)
    grad_pre = gate_back(grad_act)[0].astype(jnp.bfloat16)
    grad_up = jnp.einsum("td,tf->df", ffn_in, grad_pre, preferred_element_type=jnp.float32)
    grad_bias = jnp.sum(grad_pre.astype(jnp.float32), axis=0).reshape(bias_full.shape)
    rows = grad_pre
    grad_normed_one = grad_resid_two + lax.psum_scatter(
        jnp.einsum("tf,df->td", rows, up_full, preferred_element_type=jnp.float32).astype(
            jnp.bfloat16
        ),
        "tensor",
        scatter_dimension=0,
        tiled=True,
    ).astype(jnp.float32)
    grad_resid_one, grad_gain_one, grad_bias_one = norm_one_back(grad_normed_one)
    grad_attn = lax.all_gather(grad_resid_one.astype(jnp.bfloat16), "tensor", axis=0, tiled=True)
    grad_out = jnp.einsum("tw,td->wd", context, grad_attn, preferred_element_type=jnp.float32)
    grad_context = jnp.einsum(
        "td,wd->tw", grad_attn, out_full, preferred_element_type=jnp.float32
    ).astype(jnp.bfloat16)
    grad_query, grad_key, grad_value = lax.map(
        partial(slot_backward, local_swaps=local_swaps),
        (
            by_slot(projected[0]),
            by_slot(projected[1]),
            by_slot(projected[2]),
            slot_kind,
            log_totals,
            grad_context.reshape(slot_count, LONG_LEN, local_width),
        ),
    )
    grad_proj = jnp.stack([grad_query, grad_key, grad_value]).reshape(3, group_rows, local_width)
    grad_qkv = jnp.einsum("td,cte->cde", full_in, grad_proj, preferred_element_type=jnp.float32)
    grad_in_part = jnp.einsum(
        "cte,cde->td", grad_proj, qkv_full, preferred_element_type=jnp.float32
    )
    norm_part = jnp.stack([grad_gain_one, grad_bias_one, grad_gain_two, grad_bias_two])
    grad_in_share, norm_row = (
        lax.psum_scatter(
            grad_in_part.astype(jnp.bfloat16), "tensor", scatter_dimension=0, tiled=True
        ).astype(jnp.float32),
        lax.psum_scatter(
            norm_part.astype(jnp.bfloat16), "tensor", scatter_dimension=0, tiled=True
        ).astype(jnp.float32),
    )
    input_grad = grad_resid_one + grad_in_share
    qkv_grad, out_grad, up_grad, up_bias_grad, down_grad, norm_grad = (
        lax.psum_scatter(grad_qkv, "dp", scatter_dimension=1, tiled=True),
        lax.psum_scatter(grad_out, "dp", scatter_dimension=1, tiled=True),
        lax.psum_scatter(grad_up, "dp", scatter_dimension=0, tiled=True),
        lax.psum_scatter(grad_bias, "dp", scatter_dimension=1, tiled=True),
        lax.psum_scatter(grad_down, "dp", scatter_dimension=1, tiled=True),
        lax.psum_scatter(norm_row, "dp", scatter_dimension=1, tiled=True),
    )
    return (mixed, input_grad, qkv_grad, out_grad, up_grad, up_bias_grad, down_grad, norm_grad)


def solution(mesh):
    placed = (
        P(("dp", "tensor"), None),
        P(None, "dp", "tensor"),
        P("tensor", "dp"),
        P("dp", "tensor"),
        P("tensor", "dp"),
        P("tensor", "dp"),
        P(None, "dp"),
        P(("dp", "tensor"), None),
        P(),
        P("dp"),
    )
    planned = mesh.shape["dp"] == 8 and mesh.shape["tensor"] == 4
    return jax.shard_map(
        whole_layer if planned else per_device,
        mesh=mesh,
        in_specs=placed,
        out_specs=(
            P(("dp", "tensor"), None),
            P(("dp", "tensor"), None),
            P(None, "dp", "tensor"),
            P("tensor", "dp"),
            P("dp", "tensor"),
            P("tensor", "dp"),
            P("tensor", "dp"),
            P("tensor", "dp"),
        ),
        check_vma=False,
    )
```

```python
from functools import partial
import math

import jax
import jax.numpy as jnp
from jax import lax
from jax.experimental import pallas as pl
from jax.experimental.pallas import tpu as pltpu
from jax.sharding import PartitionSpec as P

LONG_LEN = 1024
EPSILON = 1e-05
NEGATIVE = -1e30

BF = jnp.bfloat16
F32 = jnp.float32
NN = (((1,), (0,)), ((), ()))
NT = (((1,), (1,)), ((), ()))
TN = (((0,), (0,)), ((), ()))
PIECES = 6
SLOTS = 3
SIB_SLOT = (2, 0, 1, 0, 1, 2)
ROWS = 512
D = 768
HALF = 384


def dot(a, b, dims):
    return lax.dot_general(a, b, dims, preferred_element_type=F32)


def layer_kernel(
    hid_in, qkv_in, out_in, up_in, up_b, down_in, norm_p, cot_in, swap, kind,
    mixed_out, igrad_out, g_attn, g_up, g_down, g_misc,
    qkv_w, out_w, up_w, down_w, igrad, hid, cot, mixed, W, SH, AX, QKV, KVO, AT, CTX, XH, RS1, FI, ACT, GP, GF, DKVR,
    M, NB, V, VR,
    SQ, SR, PB, RA, RB, RA2, RB2, RO, RZ, RU, RD, R0,
    zs, zr, xs, xr, ys, yr, hs, hr, ds_, dr, ms, mr, es, er,
    qs, qr, as_, ar, bs, br, a2s, a2r, b2s, b2r, rzs, rzr, vs, vr, ls_, lr, lds, ldr, zls, zlr, z0s, z0r, io,
    c_sib, c_a, c_b, c_a2, c_b2,
):
    d = lax.axis_index("dp")
    t = lax.axis_index("tensor")
    z, y = d // 2, lax.rem(d, 2)
    x, c = t // 2, lax.rem(t, 2)
    ox, oy, oc = 1 - x, 1 - y, 1 - c

    def zk(k):
        hi, lo = z // 2, lax.rem(z, 2)
        kh, kl = k // 2, k % 2
        h2 = hi if kh == 0 else 1 - hi
        l2 = lo if kl == 0 else 1 - lo
        return 2 * h2 + l2

    zz = [zk(k) for k in range(4)]
    sib = (d, 2 * x + oc)
    xn = (d, 2 * ox + c)
    yn = (2 * z + oy, t)
    zn = [(2 * zz[k] + y, t) for k in range(4)]

    def rc(src, dst, s, r, dev):
        return pltpu.make_async_remote_copy(
            src_ref=src, dst_ref=dst, send_sem=s, recv_sem=r,
            device_id=dev, device_id_type=pl.DeviceIdType.MESH,
        )

    bar = pltpu.get_barrier_semaphore()
    for dev in (sib, xn, yn, zn[1], zn[2], zn[3]):
        pl.semaphore_signal(bar, inc=1, device_id=dev, device_id_type=pl.DeviceIdType.MESH)

    copy = pltpu.make_async_copy
    load_w = [
        copy(src, dst, io.at[3 + i])
        for i, (src, dst) in enumerate(((out_in, out_w), (qkv_in, qkv_w), (up_in, up_w), (down_in, down_w)))
    ]
    load_hid = copy(hid_in, hid, io.at[0])
    load_cot = copy(cot_in, cot, io.at[1])
    save_mixed = copy(mixed, mixed_out, io.at[2])
    save_igrad = copy(igrad, igrad_out, io.at[7])
    for cp in load_w:
        cp.start()
    load_hid.start()
    load_cot.start()

    def where(p, xx, core):
        if p < 2:
            return 2 * core + p, pl.multiple_of(xx * HALF, 128)
        if p < 4:
            return 4 + 2 * xx + core, (p - 2) * HALF
        return 8 + 2 * xx + core, (p - 4) * HALF

    def slab(p, xx, zi, yi, core=None):
        m, lane = where(p, xx, c if core is None else core)
        return W.at[m, zi, yi, :, :, pl.ds(lane, HALF)]

    def col(p, xx, yi, core=None):
        m, lane = where(p, xx, c if core is None else core)
        return W.at[m, :, yi, :, :, pl.ds(lane, HALF)]

    def hcol(p, xx, yi, half):
        m, lane = where(p, xx, c)
        return W.at[m, :, yi, half, :, pl.ds(lane, HALF)]

    def zcp(p, k, recv=False):
        s = slab(p, x, zz[k] if recv else z, y)
        return rc(s, s, zs.at[p, k - 1], zr.at[p, k - 1], zn[k])

    def xcp(p, k, recv=False):
        s = slab(p, ox if recv else x, zz[k], y)
        return rc(s, s, xs.at[p, k], xr.at[p, k], xn)

    def ycp(p, k, recv=False):
        s = slab(p, x, zz[k], oy if recv else y)
        return rc(s, s, ys.at[p, k], yr.at[p, k], yn)

    def acp(p, recv=False):
        s = hcol(p, ox, oy if recv else y, 0)
        return rc(s, s, hs.at[p, 0], hr.at[p, 0], yn)

    def bcp(p, recv=False):
        s = hcol(p, ox if recv else x, oy, 1)
        return rc(s, s, hs.at[p, 1], hr.at[p, 1], xn)

    groups = [(x, y), (ox, y), (x, oy), (ox, oy)]

    def dcp(p, g, recv=False):
        xx, yy = groups[g]
        s = col(p, xx, yy, oc if recv else c)
        return rc(s, s, ds_.at[p, g], dr.at[p, g], sib)

    last = PIECES - 1

    def lx(recv=False):
        s = slab(last, ox if recv else x, z, y)
        return rc(s, s, xs.at[last, 0], xr.at[last, 0], xn)

    def ly(recv=False):
        s = slab(last, x, z, oy if recv else y)
        return rc(s, s, ys.at[last, 0], yr.at[last, 0], yn)

    def lhalf(i, recv=False):
        if i == 0:
            xx, yy, dev = ox, oy if recv else y, yn
        else:
            xx, yy, dev = ox if recv else x, oy, xn
        m, lane = where(last, xx, c)
        s = W.at[m, z, yy, i, :, pl.ds(lane, HALF)]
        return rc(s, s, hs.at[last, i], hr.at[last, i], dev)

    def lcol(core, xx, zi):
        m, lane = where(last, xx, core)
        return W.at[m, zi, :, :, :, pl.ds(lane, HALF)]

    up_dev, down_dev = (d + 2, t), (d - 2, t)

    def line(way, j, xx, recv=False):
        zi = z - j if way == 0 else z + j
        s = lcol(c, xx, zi)
        i = j if recv else j + 1
        dev = up_dev if way == 0 else down_dev
        return rc(s, s, ls_.at[way, i - 1, xx], lr.at[way, i - 1, xx], dev)

    def ldc(way, j, xx, recv=False):
        zi = z - j if way == 0 else z + j
        s = lcol(oc if recv else c, xx, zi)
        i = 6 if j == 0 else way * 3 + j - 1
        return rc(s, s, lds.at[i, xx], ldr.at[i, xx], sib)

    def lsend(way, j):
        if way == 0:
            return (z < 3) & (z >= j)
        return (z > 0) & (z + j <= 3)

    def lgot(way, j):
        return z >= j if way == 0 else z + j <= 3

    def last_xy():
        lx(True).wait_recv()
        lhalf(0).start()
        ly(True).wait_recv()
        lhalf(1).start()

    def last_start():
        lhalf(0, True).wait_recv()
        lhalf(1, True).wait_recv()
        for xx in range(2):
            for way in range(2):
                pl.when(lsend(way, 0))(lambda: line(way, 0, xx).start())
        for xx in range(2):
            ldc(0, 0, xx).start()

    def last_step(j):
        for xx in range(2):
            for way in range(2):
                @pl.when(lgot(way, j))
                def _():
                    line(way, j, xx, True).wait_recv()
                    if j < 3:
                        pl.when(lsend(way, j))(lambda: line(way, j, xx).start())
                    ldc(way, j, xx).start()

    def last_ready():
        for xx in range(2):
            ldc(0, 0, xx, True).wait_recv()
            for way in range(2):
                for j in (1, 2, 3):
                    pl.when(lgot(way, j))(lambda: ldc(way, j, xx, True).wait_recv())

    def last_drain():
        lx().wait_send()
        ly().wait_send()
        lhalf(0).wait_send()
        lhalf(1).wait_send()
        for xx in range(2):
            ldc(0, 0, xx).wait_send()
            for way in range(2):
                for j in range(3):
                    pl.when(lsend(way, j))(lambda: line(way, j, xx).wait_send())
                for j in (1, 2, 3):
                    pl.when(lgot(way, j))(lambda: ldc(way, j, xx).wait_send())

    def own_xy(p):
        if p == last:
            lx().start()
            ly().start()
            return
        xcp(p, 0).start()
        ycp(p, 0).start()

    def own_z(p):
        for k in (1, 2, 3):
            zcp(p, k).start()

    def zf(p):
        for k in (1, 2, 3):
            zcp(p, k, True).wait_recv()
            xcp(p, k).start()
            ycp(p, k).start()
        dcp(p, 0).start()

    def xf(p):
        for k in range(4):
            xcp(p, k, True).wait_recv()
        acp(p).start()
        dcp(p, 1).start()
        for k in range(4):
            ycp(p, k, True).wait_recv()
        bcp(p).start()
        dcp(p, 2).start()

    def fin(p):
        acp(p, True).wait_recv()
        bcp(p, True).wait_recv()
        dcp(p, 3).start()

    def ready(p):
        for g in range(4):
            dcp(p, g, True).wait_recv()

    def drain(p):
        for k in (1, 2, 3):
            zcp(p, k).wait_send()
        for k in range(4):
            xcp(p, k).wait_send()
            ycp(p, k).wait_send()
        acp(p).wait_send()
        bcp(p).wait_send()
        for g in range(4):
            dcp(p, g).wait_send()

    load_w[0].wait()
    SH[3, :, 0:192] = out_w[...].astype(BF).T
    load_w[1].wait()
    for m, i in enumerate((1, 0, 2)):
        SH[m, :, 0:192] = qkv_w[i].astype(BF)
    load_w[2].wait()
    W[4 + t, z, y] = up_w[...].astype(BF).reshape(2, 48, D)
    load_w[3].wait()
    W[8 + t, z, y] = down_w[...].astype(BF).reshape(2, 48, D)
    M[c, x, y, z, 0, 0:4, 0:96] = norm_p[...].astype(BF).astype(F32)
    M[c, x, y, z, 1, 0:6, 0:16] = up_b[...].astype(BF).astype(F32)
    pl.semaphore_wait(bar, 6)
    axc = rc(SH.at[pl.ds(2 * oc, 2)], AX, es.at[0], er.at[0], sib)
    axc.start()
    own_xy(5)
    own_xy(2)
    mz = [rc(M.at[c, x, y, z], M.at[c, x, y, z], ms.at[k - 1], mr.at[k - 1], zn[k]) for k in (1, 2, 3)]
    for cp in mz:
        cp.start()
    axc.wait_recv()
    own_lane = pl.ds(pl.multiple_of(x * HALF, 128), HALF)
    first = jnp.full((96, 192), c, jnp.int32) == 0
    for i in range(2):
        mine, theirs = SH[2 * c + i, :, 0:192], AX[i, :, 0:192]
        both = jnp.concatenate([jnp.where(first, mine, theirs), jnp.where(first, theirs, mine)], axis=1)
        W[2 * c + i, z, y, :, :, own_lane] = both.reshape(2, 48, HALF)
        own_z(i)
        own_xy(i)

    for cp in mz:
        cp.wait_recv()
    mx = rc(M.at[c, x, y], M.at[c, x, y], ms.at[3], mr.at[3], xn)
    mx.start()
    own_xy(3)
    last_xy()
    zf(0)
    own_z(2)
    zf(1)
    xf(0)
    mx.wait_recv()
    my = rc(M.at[c, :, y], M.at[c, :, y], ms.at[4], mr.at[4], yn)
    own_z(3)
    xf(1)
    own_z(4)
    own_xy(4)
    fin(0)
    my.start()
    ready(0)

    fin(1)
    def mat(m):
        return W[m].reshape(D, D)

    load_hid.wait()
    QKV[1] = dot(hid[...], mat(0), NN).astype(BF)
    last_start()
    zf(2)
    QKV[2] = dot(hid[...], mat(2), NN).astype(BF)
    kvc = rc(QKV.at[pl.ds(1, 2)], KVO, es.at[1], er.at[1], sib)
    kvc.start()
    my.wait_recv()
    md = rc(M.at[c], M.at[c], ms.at[5], mr.at[5], sib)
    md.start()
    ready(1)
    QKV[0] = dot(hid[...], mat(1), NN).astype(BF)
    kvc.wait_recv()

    kd = kind[x]
    zf(3)

    lane = lax.broadcasted_iota(jnp.int32, (1, 128), 1)
    keylane = lax.broadcasted_iota(jnp.int32, (1, ROWS), 1)
    low_lane = lane < 64

    def flips(hp):
        fa = kd * swap[2 * hp]
        fb = kd * swap[2 * hp + 1]
        return jnp.where(low_lane, jnp.full((1, 128), fa, jnp.int32), jnp.full((1, 128), fb, jnp.int32)) == 1

    def pair_lanes(hp):
        return pl.ds(pl.multiple_of(hp * 128, 128), 128)

    def attn_fwd(hp):
        ls = pair_lanes(hp)
        fl = flips(hp)
        kk = jnp.where(fl, KVO[0, :, ls], QKV[1, :, ls])
        vv = jnp.where(fl, KVO[1, :, ls], QKV[2, :, ls])
        for rb in range(2):
            rows = slice(rb * 256, rb * 256 + 256)
            q = QKV[0, rows, ls] * jnp.asarray(0.125, BF)
            for e in range(2):
                sw = swap[2 * hp + e]
                qe = jnp.where(low_lane if e == 0 else ~low_lane, q, jnp.zeros_like(q))
                s = dot(qe, kk, NT)
                kb = jnp.where(keylane >= 256, 1, 0)
                same = jnp.where(kb == rb, 0, 1)
                seen = (same == jnp.full((1, ROWS), sw, jnp.int32)) | (jnp.full((1, ROWS), kd, jnp.int32) == 1)
                s = s + jnp.where(seen, 0.0, NEGATIVE)
                top = jnp.max(s, axis=1, keepdims=True)
                pw = jnp.exp(s - top)
                tot = jnp.sum(pw, axis=1, keepdims=True)
                a = (pw * (1.0 / tot)).astype(BF)
                AT[2 * hp + e, rows, :] = a
        outs = [dot(AT[2 * hp + e], vv, NN) for e in range(2)]
        CTX[:, ls] = jnp.where(low_lane, outs[0], outs[1]).astype(BF)

    @pl.loop(0, 6)
    def forward_pairs(hp):
        attn_fwd(hp)
        pl.when(hp == 1)(lambda: xf(2))
        pl.when(hp == 3)(lambda: last_step(1))
        pl.when(hp == 3)(lambda: xf(3))

        pl.when(hp == 5)(lambda: zf(4))
        pl.when(hp == 5)(lambda: fin(2))

    md.wait_recv()
    def picks(width, step, count):
        si = lax.broadcasted_iota(jnp.int32, (128, width), 0)
        sj = lax.broadcasted_iota(jnp.int32, (128, width), 1)
        return lambda dd: jnp.where((si < count) & (sj == si + dd * step), 1.0, 0.0).astype(BF)

    norm_pick, bias_pick = picks(D, 96, 96), picks(128, 16, 16)
    norm_acc = jnp.zeros((16, D), F32)
    bias_acc = jnp.zeros((32, 128), F32)
    for zi in range(4):
        for yi in range(2):
            dd = 2 * zi + yi
            norm_acc = norm_acc + dot(M[c, x, yi, zi].reshape(16, 128).astype(BF), norm_pick(dd), NN)
            bias_acc = bias_acc + dot(M[:, :, yi, zi, 1].reshape(32, 128).astype(BF), bias_pick(dd), NN)
    NB[0] = norm_acc[0:8]
    for tt in range(4):
        row = (tt % 2 * 2 + tt // 2) * 8
        for r in range(6):
            NB[1, tt : tt + 1, r * 128 : r * 128 + 128] = bias_acc[row + r : row + r + 1]

    igrad[...] = dot(CTX[...], mat(3), NT)
    last_step(2)

    def ln_rows(i):
        return pl.ds(pl.multiple_of(i * 128, 128), 128)

    g1, b1 = NB[0, 0:1, :], NB[0, 1:2, :]
    g2, b2 = NB[0, 2:3, :], NB[0, 3:4, :]

    @pl.loop(0, 4)
    def _(i):
        rs = ln_rows(i)
        r = hid[rs, :].astype(F32) + igrad[rs, :]
        cen = r - jnp.mean(r, axis=1, keepdims=True)
        rstd = lax.rsqrt(jnp.mean(cen * cen, axis=1, keepdims=True) + EPSILON)
        xh = cen * rstd
        XH[rs, :] = xh
        RS1[rs, :] = rstd
        FI[rs, :] = (xh * g1 + b1).astype(BF)

    ready(2)
    fin(3)
    ready(3)
    xf(4)
    for tt in range(4):
        if tt == 3:
            fin(4)
        pre = dot(FI[...], mat(4 + tt), NN) + NB[1, tt : tt + 1, :]
        cdf = 0.5 * (1.0 + lax.erf(pre * math.sqrt(0.5)))
        ACT[tt] = (pre * cdf).astype(BF)
        GP[tt] = (cdf + pre * (jnp.exp(-0.5 * pre * pre) * (1.0 / math.sqrt(2.0 * math.pi)))).astype(BF)

    last_step(3)
    ready(4)

    def half_mat(m, h):
        return W[m, :, :, :, :, h * HALF : h * HALF + HALF].reshape(D, HALF)

    acc = dot(ACT[0, :, 0:HALF], half_mat(8, 0), NT)
    for tt in range(1, 4):
        acc = acc + dot(ACT[tt, :, 0:HALF], half_mat(8 + tt, 0), NT)
    igrad[...] = acc
    last_ready()
    acc = dot(ACT[0, :, HALF:D], half_mat(8, 1), NT)
    for tt in range(1, 4):
        acc = acc + dot(ACT[tt, :, HALF:D], half_mat(8 + tt, 1), NT)
    igrad[...] += acc

    V[...] = jnp.zeros_like(V)
    load_cot.wait()

    @pl.loop(0, 4)
    def _(i):
        rs = ln_rows(i)
        r = XH[rs, :] * g1 + b1 + igrad[rs, :]
        cen = r - jnp.mean(r, axis=1, keepdims=True)
        rstd = lax.rsqrt(jnp.mean(cen * cen, axis=1, keepdims=True) + EPSILON)
        n2 = cen * rstd
        mixed[rs, :] = (n2 * g2 + b2).astype(BF)
        co = cot[rs, :].astype(F32)
        e = co * g2
        gr = rstd * (e - jnp.mean(e, axis=1, keepdims=True) - n2 * jnp.mean(e * n2, axis=1, keepdims=True))
        igrad[rs, :] = gr
        GF[rs, :] = gr.astype(BF)
        V[2:3, :] += jnp.sum(co * n2, axis=0, keepdims=True)
        V[3:4, :] += jnp.sum(co, axis=0, keepdims=True)

    save_mixed.start()

    def sq(r, xx):
        if r < 2:
            return SQ.at[r, xx]
        return W.at[8 + 2 * (r // 2 - 1) + xx, :, :, :, :, pl.ds((r % 2) * HALF, HALF)]

    def pb(r, xx, *rest):
        if r < 4:
            return PB.at[(r, xx) + rest]
        rest = rest + (slice(None),) * (4 - len(rest))
        return W.at[(4 + xx,) + rest + (pl.ds((r % 2) * HALF, HALF),)]

    def pb_all(r, *rest):
        if r < 4:
            return PB.at[(r, slice(None)) + rest]
        rest = rest + (slice(None),) * (4 - len(rest))
        return W.at[(pl.ds(4, 2),) + rest + (pl.ds((r % 2) * HALF, HALF),)]

    def b_sib(r, xx):
        return rc(sq(r, xx), SR.at[SIB_SLOT[r], xx], qs.at[r, xx], qr.at[r, xx], sib)

    ALL = slice(None)

    def b_a(r):
        return rc(pb(r, ox, ALL, ALL, 0), RA.at[r % SLOTS], as_.at[r], ar.at[r], xn)

    def b_b(r):
        return rc(pb_all(r, ALL, oy, 1), RB.at[r % SLOTS], bs.at[r], br.at[r], yn)

    def b_a2(r, k):
        dst = RO.at[r, 0] if k == 0 else RA2.at[r % SLOTS, k - 1]
        return rc(pb(r, x, zz[k], oy, 0), dst, a2s.at[r, k], a2r.at[r, k], yn)

    def b_b2(r, k):
        dst = RO.at[r, 1] if k == 0 else RB2.at[r % SLOTS, k - 1]
        return rc(pb(r, ox, zz[k], y, 1), dst, b2s.at[r, k], b2r.at[r, k], xn)

    def b_z(r, k):
        return rc(pb(r, x, zz[k], y), RZ.at[r, k - 1], rzs.at[r, k - 1], rzr.at[r, k - 1], zn[k])

    def zl(way, tgt, xx, recv=False):
        dst = (RU if way == 0 else RD).at[tgt, xx]
        dev = up_dev if way == 0 else down_dev
        return rc(PB.at[0, xx, tgt], dst, zls.at[way, tgt, xx], zlr.at[way, tgt, xx], dev)

    def zl_sends(way, tgt):
        return z < tgt if way == 0 else z > tgt

    def zl_got(way, tgt):
        return (z > 0) & (z <= tgt) if way == 0 else (z < 3) & (z >= tgt)

    def zl_first():
        for tgt in range(3):
            for xx in range(2):
                pl.when(z == 0)(lambda: zl(0, 3 - tgt, xx).start())
                pl.when(z == 3)(lambda: zl(1, tgt, xx).start())

    def zl_pass(way, at, tgt):
        for xx in range(2):
            @pl.when(z == at)
            def _():
                zl(way, tgt, xx).wait_recv()
                add(PB.at[0, xx, tgt], (RU if way == 0 else RD).at[tgt, xx])
                zl(way, tgt, xx).start()

    def zl_last():
        for way in range(2):
            for tgt in range(4):
                @pl.when((z == tgt) & ((z > 0) if way == 0 else (z < 3)))
                def _():
                    for xx in range(2):
                        zl(way, tgt, xx).wait_recv()
                        add(PB.at[0, xx, tgt], (RU if way == 0 else RD).at[tgt, xx])

    def b0(i):
        src, dst, dev = (
            (PB.at[0, ox, z, :, 0], R0.at[0], xn),
            (PB.at[0, :, z, oy, 1], R0.at[1], yn),
            (PB.at[0, x, z, oy, 0], R0.at[2, 0], yn),
            (PB.at[0, ox, z, y, 1], R0.at[2, 1], xn),
        )[i]
        return rc(src, dst, z0s.at[i], z0r.at[i], dev)

    def xy0_first():
        b0(0).start()
        b0(1).start()

    def xy0_second():
        b0(0).wait_recv()
        add(PB.at[0, x, z, :, 0], R0.at[0])
        b0(2).start()
        b0(1).wait_recv()
        add(PB.at[0, :, z, y, 1], R0.at[1])
        b0(3).start()

    def xy0_last():
        b0(2).wait_recv()
        b0(3).wait_recv()
        tot = PB[0, x, z, y].astype(F32) + R0[2].astype(F32)
        g_down[:, 0:HALF] = tot.reshape(96, HALF)

    def rs0_drain():
        for xx in range(2):
            b_sib(0, xx).wait_send()
        for i in range(4):
            b0(i).wait_send()
        for way in range(2):
            for tgt in range(4):
                for xx in range(2):
                    pl.when(zl_sends(way, tgt))(lambda: zl(way, tgt, xx).wait_send())

    def credit(sem, dev, r):
        if r + SLOTS < PIECES:
            pl.semaphore_signal(sem, inc=1, device_id=dev, device_id_type=pl.DeviceIdType.MESH)

    def need(sem, r):
        if r >= SLOTS + (sem is not c_sib):
            pl.semaphore_wait(sem, 1)

    def part(r, xx, core):
        if r < 4:
            src = ACT if r < 2 else GP
            lhs = GF if r < 2 else FI
            h = r % 2
            return dot(lhs[...], src[2 * xx + core, :, h * HALF : h * HALF + HALF], TN)
        raise ValueError

    def part_attn(m, xx):
        if m < 3:
            return dot(hid[...], ACT[(1, 0, 2)[m], :, xx * HALF : xx * HALF + HALF], TN)
        return dot(GF[...], CTX[:, xx * HALF : xx * HALF + HALF], TN)

    def gen_sib(r):
        need(c_sib, r)
        for xx in range(2):
            if r < 4:
                sq(r, xx)[...] = part(r, xx, oc).astype(BF).reshape(4, 2, 2, 48, HALF)
            else:
                for core in range(2):
                    @pl.when(oc == core)
                    def _():
                        sq(r, xx)[...] = part_attn(2 * core + 5 - r, xx).astype(BF).reshape(4, 2, 2, 48, HALF)
            b_sib(r, xx).start()

    def own_part(r, xx, grad):
        v = grad.reshape(4, 2, 2, 48, HALF) + SR[SIB_SLOT[r], xx].astype(F32)
        pb(r, xx)[...] = v.astype(BF)

    def gen_own(r):
        for xx in range(2):
            b_sib(r, xx).wait_recv()
            if r < 4:
                own_part(r, xx, part(r, xx, c))
            else:
                for core in range(2):
                    @pl.when(c == core)
                    def _():
                        own_part(r, xx, part_attn(2 * core + 5 - r, xx))
        credit(c_sib, sib, r)
        if r == 0:
            zl_first()
            return
        need(c_a, r)
        b_a(r).start()
        need(c_b, r)
        b_b(r).start()

    def add(dst, src):
        dst[...] = (dst[...].astype(F32) + src[...].astype(F32)).astype(BF)

    def st1(r):
        q = r % SLOTS
        b_a(r).wait_recv()
        add(pb(r, x, ALL, ALL, 0), RA.at[q])
        credit(c_a, xn, r)
        need(c_a2, r)
        for k in (2, 3, 1):
            b_a2(r, k).start()
        b_b(r).wait_recv()
        add(pb_all(r, ALL, y, 1), RB.at[q])
        credit(c_b, yn, r)
        need(c_b2, r)
        for k in (2, 3, 1):
            b_b2(r, k).start()

    def st2o(r):
        b_a2(r, 0).start()
        b_b2(r, 0).start()

    def st2(r):
        q = r % SLOTS
        for k in (2, 3, 1):
            b_a2(r, k).wait_recv()
            add(pb(r, x, zz[k], y, 0), RA2.at[q, k - 1])
            b_b2(r, k).wait_recv()
            add(pb(r, x, zz[k], y, 1), RB2.at[q, k - 1])
            b_z(r, k).start()
        credit(c_a2, yn, r)
        credit(c_b2, xn, r)

    def fx(r):
        m = g_attn.at[2 * c + 5 - r]
        return rc(m, m, es.at[r - 1], er.at[r - 1], sib)

    def st3(r):
        tot = pb(r, x, z, y)[...].astype(F32)
        for k in (2, 3, 1):
            b_z(r, k).wait_recv()
            tot = tot + RZ[r, k - 1].astype(F32)
        b_a2(r, 0).wait_recv()
        b_b2(r, 0).wait_recv()
        tot = (tot + RO[r].astype(F32)).reshape(96, HALF)
        h = r % 2
        if r < 2:
            g_down[:, h * HALF : h * HALF + HALF] = tot
        elif r < 4:
            g_up[:, h * HALF : h * HALF + HALF] = tot
        else:
            g_attn[2 * c + 5 - r] = tot
            fx(r).start()

    def rs_drain(r):
        for xx in range(2):
            b_sib(r, xx).wait_send()
        b_a(r).wait_send()
        b_b(r).wait_send()
        for k in range(4):
            b_a2(r, k).wait_send()
            b_b2(r, k).wait_send()
        for k in (1, 2, 3):
            b_z(r, k).wait_send()

    def gact(h):
        ls = slice(h * HALF, h * HALF + HALF)
        for tt in range(4):
            ga = dot(GF[...], half_mat(8 + tt, h), NN)
            gp = (ga * GP[tt, :, ls].astype(F32)).astype(BF)
            GP[tt, :, ls] = gp
            V[4 + tt : 5 + tt, ls] = jnp.sum(gp.astype(F32), axis=0, keepdims=True)

    gen_sib(1)
    gen_sib(0)
    for p in range(PIECES - 1):
        drain(p)
    last_drain()
    gen_own(1)
    gen_own(0)
    gact(0)
    gen_sib(2)
    gact(1)
    zl_pass(1, 2, 0)
    gen_own(2)
    gen_sib(3)
    acc = dot(GP[0], mat(4), NT)
    zl_pass(0, 1, 3)
    for tt in range(1, 4):
        acc = acc + dot(GP[tt], mat(4 + tt), NT)
    st1(1)

    igrad[...] += acc
    gen_own(3)

    zl_pass(1, 1, 0)

    zl_pass(1, 2, 1)
    @pl.loop(0, 4)
    def _(i):
        rs = ln_rows(i)
        gn = igrad[rs, :]
        xh = XH[rs, :]
        e = gn * g1
        gr = RS1[rs, :] * (e - jnp.mean(e, axis=1, keepdims=True) - xh * jnp.mean(e * xh, axis=1, keepdims=True))
        igrad[rs, :] = gr
        GF[rs, :] = gr.astype(BF)
        V[0:1, :] += jnp.sum(gn * xh, axis=0, keepdims=True)
        V[1:2, :] += jnp.sum(gn, axis=0, keepdims=True)

    vc = [
        rc(V, VR.at[0], vs.at[0], vr.at[0], sib),
        rc(V, VR.at[1], vs.at[1], vr.at[1], xn),
        rc(V, VR.at[2], vs.at[2], vr.at[2], yn),
    ] + [rc(V, VR.at[2 + k], vs.at[2 + k], vr.at[2 + k], zn[k]) for k in (1, 2, 3)]

    def v_step(i):
        vc[i].wait()
        V[...] += VR[i]

    vc[0].start()
    FI[...] = dot(GF[...], mat(3), NN).astype(BF)
    v_step(0)
    vc[1].start()

    zl_pass(0, 1, 2)
    def attn_bwd(hp):
        ls = pair_lanes(hp)
        fl = flips(hp)
        kk = jnp.where(fl, KVO[0, :, ls], QKV[1, :, ls])
        vv = jnp.where(fl, KVO[1, :, ls], QKV[2, :, ls])
        q = QKV[0, :, ls]
        do = FI[:, ls]
        dvs, dqs, dks = [], [], []
        for e in range(2):
            dvs.append(dot(AT[2 * hp + e], do, TN))
            for rb in range(2):
                rows = slice(rb * 256, rb * 256 + 256)
                dr = do[rows]
                dp = dot(jnp.where(low_lane if e == 0 else ~low_lane, dr, jnp.zeros_like(dr)), vv, NT)
                af = AT[2 * hp + e, rows, :].astype(F32)
                w = af * dp
                GP[2 + e, rows, 0:ROWS] = (w - af * jnp.sum(w, axis=1, keepdims=True)).astype(BF)
            gs = GP[2 + e, :, 0:ROWS]
            dqs.append(dot(gs, kk, NN))
            dks.append(dot(gs, q, TN))
        ACT[0, :, ls] = (jnp.where(low_lane, dqs[0], dqs[1]) * 0.125).astype(BF)
        GP[0, :, ls] = (jnp.where(low_lane, dks[0], dks[1]) * 0.125).astype(BF)
        GP[1, :, ls] = jnp.where(low_lane, dvs[0], dvs[1]).astype(BF)

    zl_pass(0, 2, 3)
    def dkv(i):
        ls = pl.ds(i * HALF, HALF)
        return rc(GP.at[pl.ds(0, 2), :, ls], DKVR.at[:, :, ls], es.at[2 + 3 * i], er.at[2 + 3 * i], sib)

    @pl.loop(0, 6)
    def backward_pairs(hp):
        attn_bwd(hp)

        pl.when(hp == 0)(lambda: st1(2))
        pl.when(hp == 2)(lambda: st2(1))
        pl.when(hp == 2)(lambda: dkv(0).start())
        pl.when(hp == 5)(lambda: st1(3))
        pl.when(hp == 0)(lambda: st2o(1))
        pl.when(hp == 2)(lambda: st2o(2))
        pl.when(hp == 5)(lambda: st2o(3))

    gen_sib(4)
    dkv(1).start()
    v_step(1)
    st2(2)
    zl_last()
    vc[2].start()
    gen_own(4)
    dkv(0).wait()
    dkv(1).wait()

    def pick(hp):
        ls = pair_lanes(hp)
        fl = flips(hp)
        ACT[1, :, ls] = jnp.where(fl, DKVR[0, :, ls], GP[0, :, ls])
        ACT[2, :, ls] = jnp.where(fl, DKVR[1, :, ls], GP[1, :, ls])

    st2(3)
    pl.loop(0, 6)(pick)

    gen_sib(5)
    v_step(2)
    xy0_first()
    for k in (1, 2, 3):
        vc[2 + k].start()
    acc = dot(ACT[0], mat(1), NT)
    for m in (1, 2):
        acc = acc + dot(ACT[m], mat((1, 0, 2)[m]), NT)
    st1(4)
    igrad[...] += acc
    save_igrad.start()
    gen_own(5)
    st2(4)
    st1(5)
    st3(1)
    st3(3)
    st3(2)
    st2o(5)
    xy0_second()
    st2(5)
    st2o(4)
    st3(4)
    xy0_last()
    st3(5)
    for k in (1, 2, 3):
        vc[2 + k].wait()
    g_misc[...] = V[...] + VR[3] + VR[4] + VR[5]
    save_mixed.wait()
    save_igrad.wait()
    rs0_drain()
    for r in range(1, PIECES):
        rs_drain(r)
    for cp in mz:
        cp.wait_send()
    mx.wait_send()
    my.wait_send()
    md.wait_send()
    axc.wait_send()
    kvc.wait_send()
    fx(4).wait()
    fx(5).wait()


def finish_kernel(
    mixed, igrad, ga, gu, gd, gm, o_mixed, o_igrad, o_qkv, o_out, o_up, o_bias, o_down, o_norm,
    v_igrad, v_mixed, v_up, v_down, v_ga, v_gm, w_qkv, w_out, w_bias, w_norm, tmp, sem,
):
    copy = pltpu.make_async_copy
    load_small = [copy(gm, v_gm, sem.at[0, 8]), copy(ga, v_ga, sem.at[0, 9])]
    parts = [(igrad, v_igrad, o_igrad, i * 128, 128) for i in range(4)]
    parts += [(mixed, v_mixed, o_mixed, i * 256, 256) for i in range(2)]
    parts += [(gu, v_up, o_up, 0, 96), (gd, v_down, o_down, 0, 96)]
    loads, stores = [], []
    for i, (src, mid, dst, at, n) in enumerate(parts):
        rows = pl.ds(at, n)
        loads.append(copy(src.at[rows], mid.at[rows], sem.at[0, i]))
        stores.append(copy(mid.at[rows], dst.at[rows], sem.at[1, i]))
    for cp in load_small + loads:
        cp.start()
    dd = lax.axis_index("dp")
    t = lax.axis_index("tensor")
    exact = dict(preferred_element_type=F32, precision=lax.Precision.HIGHEST)
    si = lax.broadcasted_iota(jnp.int32, (D, 128), 0)
    sj = lax.broadcasted_iota(jnp.int32, (D, 128), 1)
    norm_pick = jnp.where(si == sj + dd * 96, 1.0, 0.0).astype(F32)
    bias_pick = jnp.where(si[0:128] == sj[0:128] + dd * 16, 1.0, 0.0).astype(F32)
    sub = lax.broadcasted_iota(jnp.int32, (8, D), 0)
    load_small[0].wait()
    norm = lax.dot_general(v_gm[...], norm_pick, NN, **exact)
    w_norm[...] = jnp.sum(jnp.where(sub[:, 0:128] == t, norm, 0.0), axis=0, keepdims=True)[:, 0:96]
    row = jnp.sum(jnp.where(sub == 4 + t, v_gm[...], 0.0), axis=0, keepdims=True)
    for r in range(6):
        tmp[r : r + 1] = row[:, r * 128 : r * 128 + 128]
    w_bias[...] = lax.dot_general(tmp[...], bias_pick, NN, **exact)[0:6, 0:16]
    load_small[1].wait()
    first = jnp.full((96, 192), lax.rem(t, 2), jnp.int32) == 0
    for m in range(4):
        v = jnp.where(first, v_ga[m, :, 0:192], v_ga[m, :, 192:HALF])
        if m < 3:
            w_qkv[(1, 0, 2)[m]] = v
        else:
            w_out[...] = v.T
    small = ((w_norm, o_norm), (w_bias, o_bias), (w_qkv, o_qkv), (w_out, o_out))
    for i, (src, dst) in enumerate(small):
        stores.append(copy(src, dst, sem.at[1, 8 + i]))
        stores[-1].start()
    for load, store in zip(loads, stores):
        load.wait()
        store.start()
    for cp in stores:
        cp.wait()


def scratch():
    vm = pltpu.VMEM
    dma = lambda *s: pltpu.SemaphoreType.DMA(s)
    n = PIECES
    return [
        vm((3, 96, 192), F32), vm((192, 96), F32), vm((96, D), F32), vm((96, D), F32), vm((ROWS, D), F32),
        vm((ROWS, D), BF), vm((ROWS, D), BF), vm((ROWS, D), BF), vm((12, 4, 2, 2, 48, D), BF), vm((4, 96, 256), BF), vm((2, 96, 256), BF), vm((3, ROWS, D), BF), vm((2, ROWS, D), BF),
        vm((12, ROWS, ROWS), BF), vm((ROWS, D), BF), vm((ROWS, D), F32), vm((ROWS, 1), F32), vm((ROWS, D), BF),
        vm((4, ROWS, D), BF), vm((4, ROWS, D), BF), vm((ROWS, D), BF), vm((2, ROWS, D), BF),
        vm((2, 2, 2, 4, 2, 8, 128), F32), vm((2, 8, D), F32), vm((8, D), F32), vm((6, 8, D), F32),
        vm((2, 2, 4, 2, 2, 48, HALF), BF), vm((SLOTS, 2, 4, 2, 2, 48, HALF), BF), vm((4, 2, 4, 2, 2, 48, HALF), BF),
        vm((SLOTS, 4, 2, 48, HALF), BF), vm((SLOTS, 2, 4, 48, HALF), BF), vm((SLOTS, 3, 48, HALF), BF),
        vm((SLOTS, 3, 48, HALF), BF), vm((n, 2, 48, HALF), BF), vm((n, 3, 2, 48, HALF), BF),
        vm((4, 2, 2, 2, 48, HALF), BF), vm((4, 2, 2, 2, 48, HALF), BF), vm((3, 2, 48, HALF), BF),
        dma(n, 3), dma(n, 3), dma(n, 4), dma(n, 4), dma(n, 4), dma(n, 4), dma(n, 2), dma(n, 2), dma(n, 4), dma(n, 4),
        dma(6), dma(6), dma(6), dma(6),
        dma(n, 2), dma(n, 2), dma(n), dma(n), dma(n), dma(n), dma(n, 4), dma(n, 4), dma(n, 4), dma(n, 4), dma(n, 3), dma(n, 3), dma(6), dma(6),
        dma(2, 3, 2), dma(2, 3, 2), dma(7, 2), dma(7, 2), dma(2, 4, 2), dma(2, 4, 2), dma(4), dma(4), dma(8),
        pltpu.SemaphoreType.REGULAR, pltpu.SemaphoreType.REGULAR, pltpu.SemaphoreType.REGULAR,
        pltpu.SemaphoreType.REGULAR, pltpu.SemaphoreType.REGULAR,
    ]


def whole_layer(
    hidden_in, qkv_weight, out_weight, up_weight, up_bias, down_weight, norm_params, cotangent, head_swap, slot_kind
):
    any_ = pl.BlockSpec(memory_space=pl.ANY)
    vmem = pl.BlockSpec(memory_space=pltpu.VMEM)
    smem = pl.BlockSpec(memory_space=pltpu.SMEM)
    sds = jax.ShapeDtypeStruct
    mixed, igrad, ga, gu, gd, gm = pl.pallas_call(
        layer_kernel,
        out_shape=(
            sds((ROWS, D), BF), sds((ROWS, D), F32), sds((4, 96, HALF), F32),
            sds((96, D), F32), sds((96, D), F32), sds((8, D), F32),
        ),
        in_specs=[any_] * 4 + [vmem, any_, vmem, any_] + [smem] * 2,
        out_specs=(any_,) * 2 + (vmem,) * 4,
        scratch_shapes=scratch(),
        compiler_params=pltpu.CompilerParams(
            collective_id=0, has_side_effects=True, vmem_limit_bytes=63 * 2**20
        ),
        name="layer",
    )(
        hidden_in, qkv_weight, out_weight, up_weight, up_bias, down_weight.T, norm_params, cotangent, head_swap, slot_kind
    )
    *outs, bias_grad, down_grad, norm_grad = pl.pallas_call(
        finish_kernel,
        out_shape=(
            sds((ROWS, D), BF), sds((ROWS, D), F32), sds((3, 96, 192), F32), sds((192, 96), F32),
            sds((96, D), F32), sds((6, 16), F32), sds((96, D), F32), sds((1, 96), F32),
        ),
        in_specs=[any_] * 6,
        out_specs=(any_,) * 8,
        scratch_shapes=[
            pltpu.VMEM((ROWS, D), F32), pltpu.VMEM((ROWS, D), BF), pltpu.VMEM((96, D), F32), pltpu.VMEM((96, D), F32),
            pltpu.VMEM((4, 96, HALF), F32), pltpu.VMEM((8, D), F32), pltpu.VMEM((3, 96, 192), F32),
            pltpu.VMEM((192, 96), F32), pltpu.VMEM((6, 16), F32), pltpu.VMEM((1, 96), F32), pltpu.VMEM((8, 128), F32),
            pltpu.SemaphoreType.DMA((2, 12)),
        ],
        compiler_params=pltpu.CompilerParams(vmem_limit_bytes=63 * 2**20),
        name="finish",
    )(mixed, igrad, ga, gu, gd, gm)
    return (*outs, bias_grad, down_grad.T, norm_grad)


def norm_rows(residual, scales, offset):
    center = residual - jnp.mean(residual, axis=-1, keepdims=True)
    spread = jnp.mean(center * center, axis=-1, keepdims=True)
    return center * lax.rsqrt(spread + EPSILON) * scales + offset


def smooth_gate(values):
    return jax.nn.gelu(values, approximate=False)


def arrange(queries, keys_in, values_in, slot_type, local_swaps):
    slot_len, head_count, head_size = queries.shape
    half_len = slot_len // 2
    quarter = half_len // 2
    shape_four = (2, half_len, head_count, head_size)
    query_half = queries.reshape(shape_four)
    key_half = keys_in.reshape(shape_four)
    value_half = values_in.reshape(shape_four)
    flipped = (local_swaps * slot_type == 1)[None, None, :, None]
    key_pick = jnp.where(flipped, key_half[::-1], key_half)
    value_pick = jnp.where(flipped, value_half[::-1], value_half)
    blocks = jnp.arange(half_len, dtype=jnp.int32) // quarter
    matching = (
        jnp.bitwise_xor(blocks[None, :, None], local_swaps[:, None, None]) == blocks[None, None, :]
    )
    allowed = jnp.logical_or(slot_type == 1, matching)
    return (query_half, key_pick, value_pick, allowed, flipped)


def masked_scores(query_half, key_pick, allowed):
    scale = 1.0 / math.sqrt(query_half.shape[-1])
    scores = (
        jnp.einsum("jqhd,jkhd->jhqk", query_half, key_pick, preferred_element_type=jnp.float32)
        * scale
    )
    return jnp.where(allowed[None], scores, NEGATIVE)


def slot_forward(inputs, local_swaps):
    queries, keys_in, values_in, slot_type = inputs
    query_half, key_pick, value_pick, allowed, flipped = arrange(
        queries, keys_in, values_in, slot_type, local_swaps
    )
    scores = masked_scores(query_half, key_pick, allowed)
    largest = jnp.max(scores, axis=-1, keepdims=True)
    powers = jnp.exp(scores - largest)
    totals = jnp.sum(powers, axis=-1, keepdims=True)
    attention = (powers / totals).astype(jnp.bfloat16)
    context = jnp.einsum(
        "jhqk,jkhd->jqhd", attention, value_pick, preferred_element_type=jnp.float32
    )
    return (context.astype(jnp.bfloat16).reshape(queries.shape[0], -1), largest + jnp.log(totals))


def slot_backward(inputs, local_swaps):
    queries, keys_in, values_in, slot_type, log_totals, grad_out = inputs
    slot_len, head_count, head_size = queries.shape
    scale = 1.0 / math.sqrt(head_size)
    query_half, key_pick, value_pick, allowed, flipped = arrange(
        queries, keys_in, values_in, slot_type, local_swaps
    )
    attention = jnp.exp(masked_scores(query_half, key_pick, allowed) - log_totals)
    grad_half = grad_out.reshape(query_half.shape)
    grad_vpick = jnp.einsum(
        "jhqk,jqhd->jkhd",
        attention.astype(jnp.bfloat16),
        grad_half,
        preferred_element_type=jnp.float32,
    ).astype(jnp.bfloat16)
    grad_attention = jnp.einsum(
        "jqhd,jkhd->jhqk", grad_half, value_pick, preferred_element_type=jnp.float32
    )
    row_dots = jnp.sum(attention * grad_attention, axis=-1, keepdims=True)
    grad_scores = (attention * (grad_attention - row_dots)).astype(jnp.bfloat16)
    grad_query = (
        jnp.einsum("jhqk,jkhd->jqhd", grad_scores, key_pick, preferred_element_type=jnp.float32)
        * scale
    ).astype(jnp.bfloat16)
    grad_kpick = (
        jnp.einsum("jhqk,jqhd->jkhd", grad_scores, query_half, preferred_element_type=jnp.float32)
        * scale
    ).astype(jnp.bfloat16)
    grad_key = jnp.where(flipped, grad_kpick[::-1], grad_kpick)
    grad_value = jnp.where(flipped, grad_vpick[::-1], grad_vpick)
    return (
        grad_query.reshape(slot_len, -1),
        grad_key.reshape(slot_len, -1),
        grad_value.reshape(slot_len, -1),
    )


def per_device(
    hidden_in,
    qkv_weight,
    out_weight,
    up_weight,
    up_bias,
    down_weight,
    norm_params,
    cotangent,
    head_swap,
    slot_kind,
):
    tensor_count = lax.axis_size("tensor")
    tensor_rank = lax.axis_index("tensor")
    heads_here = head_swap.shape[0] // tensor_count
    local_swaps = lax.dynamic_slice_in_dim(head_swap, tensor_rank * heads_here, heads_here)
    qkv_low = qkv_weight.astype(jnp.bfloat16)
    out_low = out_weight.astype(jnp.bfloat16)
    norm_low = norm_params.astype(jnp.bfloat16)
    up_low = up_weight.astype(jnp.bfloat16)
    bias_low = up_bias.astype(jnp.bfloat16)
    down_low = down_weight.astype(jnp.bfloat16)
    qkv_full, out_full, norm_full = (
        lax.all_gather(qkv_low, "dp", axis=1, tiled=True),
        lax.all_gather(out_low, "dp", axis=1, tiled=True),
        lax.all_gather(norm_low, "dp", axis=1, tiled=True),
    )
    norm_gain = norm_full.astype(jnp.float32)
    full_in = lax.all_gather(hidden_in, "tensor", axis=0, tiled=True)
    group_rows = full_in.shape[0]
    local_width = qkv_full.shape[2]
    head_size = local_width // heads_here
    slot_count = group_rows // LONG_LEN

    def by_slot(rows):
        return rows.reshape(slot_count, LONG_LEN, heads_here, head_size)

    projected = jnp.einsum(
        "td,cde->cte", full_in, qkv_full, preferred_element_type=jnp.float32
    ).astype(jnp.bfloat16)
    context, log_totals = lax.map(
        partial(slot_forward, local_swaps=local_swaps),
        (by_slot(projected[0]), by_slot(projected[1]), by_slot(projected[2]), slot_kind),
    )
    context = context.reshape(group_rows, local_width)
    rows = context
    attn_share = lax.psum_scatter(
        jnp.dot(rows, out_full, preferred_element_type=jnp.float32).astype(jnp.bfloat16),
        "tensor",
        scatter_dimension=0,
        tiled=True,
    ).astype(jnp.float32)
    resid_one = hidden_in.astype(jnp.float32) + attn_share
    normed_one, norm_one_back = jax.vjp(norm_rows, resid_one, norm_gain[0], norm_gain[1])
    up_full, bias_full, down_full = (
        lax.all_gather(up_low, "dp", axis=0, tiled=True),
        lax.all_gather(bias_low, "dp", axis=1, tiled=True),
        lax.all_gather(down_low, "dp", axis=1, tiled=True),
    )
    ffn_in = lax.all_gather(normed_one.astype(jnp.bfloat16), "tensor", axis=0, tiled=True)
    pre = jnp.dot(ffn_in, up_full, preferred_element_type=jnp.float32) + bias_full.reshape(
        -1
    ).astype(jnp.float32)
    act_value, gate_back = jax.vjp(smooth_gate, pre)
    act = act_value.astype(jnp.bfloat16)
    rows = act
    ffn_share = lax.psum_scatter(
        jnp.dot(rows, down_full, preferred_element_type=jnp.float32).astype(jnp.bfloat16),
        "tensor",
        scatter_dimension=0,
        tiled=True,
    ).astype(jnp.float32)
    normed_two, norm_two_back = jax.vjp(
        norm_rows, normed_one + ffn_share, norm_gain[2], norm_gain[3]
    )
    mixed = normed_two.astype(jnp.bfloat16)
    grad_resid_two, grad_gain_two, grad_bias_two = norm_two_back(cotangent.astype(jnp.float32))
    grad_ffn = lax.all_gather(grad_resid_two.astype(jnp.bfloat16), "tensor", axis=0, tiled=True)
    grad_down = jnp.einsum("tf,td->fd", act, grad_ffn, preferred_element_type=jnp.float32)
    grad_act = jnp.einsum("td,fd->tf", grad_ffn, down_full, preferred_element_type=jnp.float32)
    grad_pre = gate_back(grad_act)[0].astype(jnp.bfloat16)
    grad_up = jnp.einsum("td,tf->df", ffn_in, grad_pre, preferred_element_type=jnp.float32)
    grad_bias = jnp.sum(grad_pre.astype(jnp.float32), axis=0).reshape(bias_full.shape)
    rows = grad_pre
    grad_normed_one = grad_resid_two + lax.psum_scatter(
        jnp.einsum("tf,df->td", rows, up_full, preferred_element_type=jnp.float32).astype(
            jnp.bfloat16
        ),
        "tensor",
        scatter_dimension=0,
        tiled=True,
    ).astype(jnp.float32)
    grad_resid_one, grad_gain_one, grad_bias_one = norm_one_back(grad_normed_one)
    grad_attn = lax.all_gather(grad_resid_one.astype(jnp.bfloat16), "tensor", axis=0, tiled=True)
    grad_out = jnp.einsum("tw,td->wd", context, grad_attn, preferred_element_type=jnp.float32)
    grad_context = jnp.einsum(
        "td,wd->tw", grad_attn, out_full, preferred_element_type=jnp.float32
    ).astype(jnp.bfloat16)
    grad_query, grad_key, grad_value = lax.map(
        partial(slot_backward, local_swaps=local_swaps),
        (
            by_slot(projected[0]),
            by_slot(projected[1]),
            by_slot(projected[2]),
            slot_kind,
            log_totals,
            grad_context.reshape(slot_count, LONG_LEN, local_width),
        ),
    )
    grad_proj = jnp.stack([grad_query, grad_key, grad_value]).reshape(3, group_rows, local_width)
    grad_qkv = jnp.einsum("td,cte->cde", full_in, grad_proj, preferred_element_type=jnp.float32)
    grad_in_part = jnp.einsum(
        "cte,cde->td", grad_proj, qkv_full, preferred_element_type=jnp.float32
    )
    norm_part = jnp.stack([grad_gain_one, grad_bias_one, grad_gain_two, grad_bias_two])
    grad_in_share, norm_row = (
        lax.psum_scatter(
            grad_in_part.astype(jnp.bfloat16), "tensor", scatter_dimension=0, tiled=True
        ).astype(jnp.float32),
        lax.psum_scatter(
            norm_part.astype(jnp.bfloat16), "tensor", scatter_dimension=0, tiled=True
        ).astype(jnp.float32),
    )
    input_grad = grad_resid_one + grad_in_share
    qkv_grad, out_grad, up_grad, up_bias_grad, down_grad, norm_grad = (
        lax.psum_scatter(grad_qkv, "dp", scatter_dimension=1, tiled=True),
        lax.psum_scatter(grad_out, "dp", scatter_dimension=1, tiled=True),
        lax.psum_scatter(grad_up, "dp", scatter_dimension=0, tiled=True),
        lax.psum_scatter(grad_bias, "dp", scatter_dimension=1, tiled=True),
        lax.psum_scatter(grad_down, "dp", scatter_dimension=1, tiled=True),
        lax.psum_scatter(norm_row, "dp", scatter_dimension=1, tiled=True),
    )
    return (mixed, input_grad, qkv_grad, out_grad, up_grad, up_bias_grad, down_grad, norm_grad)


def solution(mesh):
    placed = (
        P(("dp", "tensor"), None),
        P(None, "dp", "tensor"),
        P("tensor", "dp"),
        P("dp", "tensor"),
        P("tensor", "dp"),
        P("tensor", "dp"),
        P(None, "dp"),
        P(("dp", "tensor"), None),
        P(),
        P("dp"),
    )
    planned = mesh.shape["dp"] == 8 and mesh.shape["tensor"] == 4
    return jax.shard_map(
        whole_layer if planned else per_device,
        mesh=mesh,
        in_specs=placed,
        out_specs=(
            P(("dp", "tensor"), None),
            P(("dp", "tensor"), None),
            P(None, "dp", "tensor"),
            P("tensor", "dp"),
            P("dp", "tensor"),
            P("tensor", "dp"),
            P("tensor", "dp"),
            P("tensor", "dp"),
        ),
        check_vma=False,
    )
```

```python
from functools import partial
import math

import jax
import jax.numpy as jnp
from jax import lax
from jax.experimental import pallas as pl
from jax.experimental.pallas import tpu as pltpu
from jax.sharding import PartitionSpec as P

LONG_LEN = 1024
EPSILON = 1e-05
NEGATIVE = -1e30

BF = jnp.bfloat16
F32 = jnp.float32
NN = (((1,), (0,)), ((), ()))
NT = (((1,), (1,)), ((), ()))
TN = (((0,), (0,)), ((), ()))
PIECES = 6
SLOTS = 3
SIB_SLOT = (2, 0, 1, 0, 1, 2)
ROWS = 512
D = 768
HALF = 384


def dot(a, b, dims):
    return lax.dot_general(a, b, dims, preferred_element_type=F32)


def layer_kernel(
    hid_in, qkv_in, out_in, up_in, up_b, down_in, norm_p, cot_in, swap, kind,
    mixed_out, igrad_out, g_attn, g_up, g_down, g_misc,
    qkv_w, out_w, up_w, down_w, igrad, hid, cot, mixed, W, SH, AX, QKV, KVO, AT, CTX, XH, RS1, FI, ACT, GP, GF, DKVR,
    M, NB, V, VR,
    SQ, SR, PB, RA, RB, RA2, RB2, RO, RZ, RU, RD, R0,
    zs, zr, xs, xr, ys, yr, hs, hr, ds_, dr, ms, mr, es, er,
    qs, qr, as_, ar, bs, br, a2s, a2r, b2s, b2r, rzs, rzr, vs, vr, ls_, lr, lds, ldr, zls, zlr, z0s, z0r, io,
    c_sib, c_a, c_b, c_a2, c_b2,
):
    d = lax.axis_index("dp")
    t = lax.axis_index("tensor")
    z, y = d // 2, lax.rem(d, 2)
    x, c = t // 2, lax.rem(t, 2)
    ox, oy, oc = 1 - x, 1 - y, 1 - c

    def zk(k):
        hi, lo = z // 2, lax.rem(z, 2)
        kh, kl = k // 2, k % 2
        h2 = hi if kh == 0 else 1 - hi
        l2 = lo if kl == 0 else 1 - lo
        return 2 * h2 + l2

    zz = [zk(k) for k in range(4)]
    sib = (d, 2 * x + oc)
    xn = (d, 2 * ox + c)
    yn = (2 * z + oy, t)
    zn = [(2 * zz[k] + y, t) for k in range(4)]

    def rc(src, dst, s, r, dev):
        return pltpu.make_async_remote_copy(
            src_ref=src, dst_ref=dst, send_sem=s, recv_sem=r,
            device_id=dev, device_id_type=pl.DeviceIdType.MESH,
        )

    bar = pltpu.get_barrier_semaphore()
    for dev in (sib, xn, yn, zn[1], zn[2], zn[3]):
        pl.semaphore_signal(bar, inc=1, device_id=dev, device_id_type=pl.DeviceIdType.MESH)

    copy = pltpu.make_async_copy
    load_w = [
        copy(src, dst, io.at[3 + i])
        for i, (src, dst) in enumerate(((out_in, out_w), (qkv_in, qkv_w), (up_in, up_w), (down_in, down_w)))
    ]
    load_hid = copy(hid_in, hid, io.at[0])
    load_cot = copy(cot_in, cot, io.at[1])
    save_mixed = copy(mixed, mixed_out, io.at[2])
    save_igrad = copy(igrad, igrad_out, io.at[7])
    for cp in load_w:
        cp.start()
    load_hid.start()
    load_cot.start()

    def where(p, xx, core):
        if p < 2:
            return 2 * core + p, pl.multiple_of(xx * HALF, 128)
        if p < 4:
            return 4 + 2 * xx + core, (p - 2) * HALF
        return 8 + 2 * xx + core, (p - 4) * HALF

    def slab(p, xx, zi, yi, core=None):
        m, lane = where(p, xx, c if core is None else core)
        return W.at[m, zi, yi, :, :, pl.ds(lane, HALF)]

    def col(p, xx, yi, core=None):
        m, lane = where(p, xx, c if core is None else core)
        return W.at[m, :, yi, :, :, pl.ds(lane, HALF)]

    def hcol(p, xx, yi, half):
        m, lane = where(p, xx, c)
        return W.at[m, :, yi, half, :, pl.ds(lane, HALF)]

    def zcp(p, k, recv=False):
        s = slab(p, x, zz[k] if recv else z, y)
        return rc(s, s, zs.at[p, k - 1], zr.at[p, k - 1], zn[k])

    def xcp(p, k, recv=False):
        s = slab(p, ox if recv else x, zz[k], y)
        return rc(s, s, xs.at[p, k], xr.at[p, k], xn)

    def ycp(p, k, recv=False):
        s = slab(p, x, zz[k], oy if recv else y)
        return rc(s, s, ys.at[p, k], yr.at[p, k], yn)

    def acp(p, recv=False):
        s = hcol(p, ox, oy if recv else y, 0)
        return rc(s, s, hs.at[p, 0], hr.at[p, 0], yn)

    def bcp(p, recv=False):
        s = hcol(p, ox if recv else x, oy, 1)
        return rc(s, s, hs.at[p, 1], hr.at[p, 1], xn)

    groups = [(x, y), (ox, y), (x, oy), (ox, oy)]

    def dcp(p, g, recv=False):
        xx, yy = groups[g]
        s = col(p, xx, yy, oc if recv else c)
        return rc(s, s, ds_.at[p, g], dr.at[p, g], sib)

    last = PIECES - 1

    def lx(recv=False):
        s = slab(last, ox if recv else x, z, y)
        return rc(s, s, xs.at[last, 0], xr.at[last, 0], xn)

    def ly(recv=False):
        s = slab(last, x, z, oy if recv else y)
        return rc(s, s, ys.at[last, 0], yr.at[last, 0], yn)

    def lhalf(i, recv=False):
        if i == 0:
            xx, yy, dev = ox, oy if recv else y, yn
        else:
            xx, yy, dev = ox if recv else x, oy, xn
        m, lane = where(last, xx, c)
        s = W.at[m, z, yy, i, :, pl.ds(lane, HALF)]
        return rc(s, s, hs.at[last, i], hr.at[last, i], dev)

    def lcol(core, xx, zi):
        m, lane = where(last, xx, core)
        return W.at[m, zi, :, :, :, pl.ds(lane, HALF)]

    up_dev, down_dev = (d + 2, t), (d - 2, t)

    def line(way, j, xx, recv=False):
        zi = z - j if way == 0 else z + j
        s = lcol(c, xx, zi)
        i = j if recv else j + 1
        dev = up_dev if way == 0 else down_dev
        return rc(s, s, ls_.at[way, i - 1, xx], lr.at[way, i - 1, xx], dev)

    def ldc(way, j, xx, recv=False):
        zi = z - j if way == 0 else z + j
        s = lcol(oc if recv else c, xx, zi)
        i = 6 if j == 0 else way * 3 + j - 1
        return rc(s, s, lds.at[i, xx], ldr.at[i, xx], sib)

    def lsend(way, j):
        if way == 0:
            return (z < 3) & (z >= j)
        return (z > 0) & (z + j <= 3)

    def lgot(way, j):
        return z >= j if way == 0 else z + j <= 3

    def last_xy():
        lx(True).wait_recv()
        lhalf(0).start()
        ly(True).wait_recv()
        lhalf(1).start()

    def last_start():
        lhalf(0, True).wait_recv()
        lhalf(1, True).wait_recv()
        for xx in range(2):
            for way in range(2):
                pl.when(lsend(way, 0))(lambda: line(way, 0, xx).start())
        for xx in range(2):
            ldc(0, 0, xx).start()

    def last_step(j):
        for xx in range(2):
            for way in range(2):
                @pl.when(lgot(way, j))
                def _():
                    line(way, j, xx, True).wait_recv()
                    if j < 3:
                        pl.when(lsend(way, j))(lambda: line(way, j, xx).start())
                    ldc(way, j, xx).start()

    def last_ready():
        for xx in range(2):
            ldc(0, 0, xx, True).wait_recv()
            for way in range(2):
                for j in (1, 2, 3):
                    pl.when(lgot(way, j))(lambda: ldc(way, j, xx, True).wait_recv())

    def last_drain():
        lx().wait_send()
        ly().wait_send()
        lhalf(0).wait_send()
        lhalf(1).wait_send()
        for xx in range(2):
            ldc(0, 0, xx).wait_send()
            for way in range(2):
                for j in range(3):
                    pl.when(lsend(way, j))(lambda: line(way, j, xx).wait_send())
                for j in (1, 2, 3):
                    pl.when(lgot(way, j))(lambda: ldc(way, j, xx).wait_send())

    def own_xy(p):
        if p == last:
            lx().start()
            ly().start()
            return
        xcp(p, 0).start()
        ycp(p, 0).start()

    def own_z(p):
        for k in (1, 2, 3):
            zcp(p, k).start()

    def zf(p):
        for k in (1, 2, 3):
            zcp(p, k, True).wait_recv()
            xcp(p, k).start()
            ycp(p, k).start()
        dcp(p, 0).start()

    def xf(p):
        for k in range(4):
            xcp(p, k, True).wait_recv()
        acp(p).start()
        dcp(p, 1).start()
        for k in range(4):
            ycp(p, k, True).wait_recv()
        bcp(p).start()
        dcp(p, 2).start()

    def fin(p):
        acp(p, True).wait_recv()
        bcp(p, True).wait_recv()
        dcp(p, 3).start()

    def ready(p):
        for g in range(4):
            dcp(p, g, True).wait_recv()

    def drain(p):
        for k in (1, 2, 3):
            zcp(p, k).wait_send()
        for k in range(4):
            xcp(p, k).wait_send()
            ycp(p, k).wait_send()
        acp(p).wait_send()
        bcp(p).wait_send()
        for g in range(4):
            dcp(p, g).wait_send()

    load_w[0].wait()
    SH[3, :, 0:192] = out_w[...].astype(BF).T
    load_w[1].wait()
    for m, i in enumerate((1, 0, 2)):
        SH[m, :, 0:192] = qkv_w[i].astype(BF)
    pl.semaphore_wait(bar, 6)
    axc = rc(SH.at[pl.ds(2 * oc, 2)], AX, es.at[0], er.at[0], sib)
    axc.start()
    load_w[2].wait()
    W[4 + t, z, y] = up_w[...].astype(BF).reshape(2, 48, D)
    load_w[3].wait()
    W[8 + t, z, y] = down_w[...].astype(BF).reshape(2, 48, D)
    M[c, x, y, z, 0, 0:4, 0:96] = norm_p[...].astype(BF).astype(F32)
    M[c, x, y, z, 1, 0:6, 0:16] = up_b[...].astype(BF).astype(F32)
    own_xy(5)
    own_xy(2)
    mz = [rc(M.at[c, x, y, z], M.at[c, x, y, z], ms.at[k - 1], mr.at[k - 1], zn[k]) for k in (1, 2, 3)]
    for cp in mz:
        cp.start()
    axc.wait_recv()
    own_lane = pl.ds(pl.multiple_of(x * HALF, 128), HALF)
    first = jnp.full((96, 192), c, jnp.int32) == 0
    for i in range(2):
        mine, theirs = SH[2 * c + i, :, 0:192], AX[i, :, 0:192]
        both = jnp.concatenate([jnp.where(first, mine, theirs), jnp.where(first, theirs, mine)], axis=1)
        W[2 * c + i, z, y, :, :, own_lane] = both.reshape(2, 48, HALF)
        own_z(i)
        own_xy(i)

    for cp in mz:
        cp.wait_recv()
    mx = rc(M.at[c, x, y], M.at[c, x, y], ms.at[3], mr.at[3], xn)
    mx.start()
    own_xy(3)
    last_xy()
    zf(0)
    own_z(2)
    zf(1)
    xf(0)
    mx.wait_recv()
    my = rc(M.at[c, :, y], M.at[c, :, y], ms.at[4], mr.at[4], yn)
    own_z(3)
    xf(1)
    own_z(4)
    own_xy(4)
    fin(0)
    my.start()
    ready(0)

    fin(1)
    def mat(m):
        return W[m].reshape(D, D)

    load_hid.wait()
    QKV[1] = dot(hid[...], mat(0), NN).astype(BF)
    last_start()
    zf(2)
    QKV[2] = dot(hid[...], mat(2), NN).astype(BF)
    kvc = rc(QKV.at[pl.ds(1, 2)], KVO, es.at[1], er.at[1], sib)
    kvc.start()
    my.wait_recv()
    md = rc(M.at[c], M.at[c], ms.at[5], mr.at[5], sib)
    md.start()
    ready(1)
    QKV[0] = dot(hid[...], mat(1), NN).astype(BF)
    kvc.wait_recv()

    kd = kind[x]
    zf(3)

    lane = lax.broadcasted_iota(jnp.int32, (1, 128), 1)
    keylane = lax.broadcasted_iota(jnp.int32, (1, ROWS), 1)
    low_lane = lane < 64

    def flips(hp):
        fa = kd * swap[2 * hp]
        fb = kd * swap[2 * hp + 1]
        return jnp.where(low_lane, jnp.full((1, 128), fa, jnp.int32), jnp.full((1, 128), fb, jnp.int32)) == 1

    def pair_lanes(hp):
        return pl.ds(pl.multiple_of(hp * 128, 128), 128)

    def attn_fwd(hp):
        ls = pair_lanes(hp)
        fl = flips(hp)
        kk = jnp.where(fl, KVO[0, :, ls], QKV[1, :, ls])
        vv = jnp.where(fl, KVO[1, :, ls], QKV[2, :, ls])
        for rb in range(2):
            rows = slice(rb * 256, rb * 256 + 256)
            q = QKV[0, rows, ls] * jnp.asarray(0.125, BF)
            for e in range(2):
                sw = swap[2 * hp + e]
                qe = jnp.where(low_lane if e == 0 else ~low_lane, q, jnp.zeros_like(q))
                s = dot(qe, kk, NT)
                kb = jnp.where(keylane >= 256, 1, 0)
                same = jnp.where(kb == rb, 0, 1)
                seen = (same == jnp.full((1, ROWS), sw, jnp.int32)) | (jnp.full((1, ROWS), kd, jnp.int32) == 1)
                s = s + jnp.where(seen, 0.0, NEGATIVE)
                top = jnp.max(s, axis=1, keepdims=True)
                pw = jnp.exp(s - top)
                tot = jnp.sum(pw, axis=1, keepdims=True)
                a = (pw * (1.0 / tot)).astype(BF)
                AT[2 * hp + e, rows, :] = a
        outs = [dot(AT[2 * hp + e], vv, NN) for e in range(2)]
        CTX[:, ls] = jnp.where(low_lane, outs[0], outs[1]).astype(BF)

    @pl.loop(0, 6)
    def forward_pairs(hp):
        attn_fwd(hp)
        pl.when(hp == 1)(lambda: xf(2))
        pl.when(hp == 3)(lambda: last_step(1))
        pl.when(hp == 3)(lambda: xf(3))

        pl.when(hp == 5)(lambda: zf(4))
        pl.when(hp == 5)(lambda: fin(2))

    md.wait_recv()
    def picks(width, step, count):
        si = lax.broadcasted_iota(jnp.int32, (128, width), 0)
        sj = lax.broadcasted_iota(jnp.int32, (128, width), 1)
        return lambda dd: jnp.where((si < count) & (sj == si + dd * step), 1.0, 0.0).astype(BF)

    norm_pick, bias_pick = picks(D, 96, 96), picks(128, 16, 16)
    norm_acc = jnp.zeros((16, D), F32)
    bias_acc = jnp.zeros((32, 128), F32)
    for zi in range(4):
        for yi in range(2):
            dd = 2 * zi + yi
            norm_acc = norm_acc + dot(M[c, x, yi, zi].reshape(16, 128).astype(BF), norm_pick(dd), NN)
            bias_acc = bias_acc + dot(M[:, :, yi, zi, 1].reshape(32, 128).astype(BF), bias_pick(dd), NN)
    NB[0] = norm_acc[0:8]
    for tt in range(4):
        row = (tt % 2 * 2 + tt // 2) * 8
        for r in range(6):
            NB[1, tt : tt + 1, r * 128 : r * 128 + 128] = bias_acc[row + r : row + r + 1]

    igrad[...] = dot(CTX[...], mat(3), NT)
    last_step(2)

    def ln_rows(i):
        return pl.ds(pl.multiple_of(i * 128, 128), 128)

    g1, b1 = NB[0, 0:1, :], NB[0, 1:2, :]
    g2, b2 = NB[0, 2:3, :], NB[0, 3:4, :]

    @pl.loop(0, 4)
    def _(i):
        rs = ln_rows(i)
        r = hid[rs, :].astype(F32) + igrad[rs, :]
        cen = r - jnp.mean(r, axis=1, keepdims=True)
        rstd = lax.rsqrt(jnp.mean(cen * cen, axis=1, keepdims=True) + EPSILON)
        xh = cen * rstd
        XH[rs, :] = xh
        RS1[rs, :] = rstd
        FI[rs, :] = (xh * g1 + b1).astype(BF)

    ready(2)
    fin(3)
    ready(3)
    for p in (0, 1, 2):
        drain(p)
    for cp in mz:
        cp.wait_send()
    mx.wait_send()
    my.wait_send()
    axc.wait_send()
    kvc.wait_send()
    xf(4)
    for tt in range(4):
        if tt == 3:
            fin(4)
        pre = dot(FI[...], mat(4 + tt), NN) + NB[1, tt : tt + 1, :]
        cdf = 0.5 * (1.0 + lax.erf(pre * math.sqrt(0.5)))
        ACT[tt] = (pre * cdf).astype(BF)
        GP[tt] = (cdf + pre * (jnp.exp(-0.5 * pre * pre) * (1.0 / math.sqrt(2.0 * math.pi)))).astype(BF)

    last_step(3)
    drain(3)
    md.wait_send()
    ready(4)

    def half_mat(m, h):
        return W[m, :, :, :, :, h * HALF : h * HALF + HALF].reshape(D, HALF)

    acc = dot(ACT[0, :, 0:HALF], half_mat(8, 0), NT)
    for tt in range(1, 4):
        acc = acc + dot(ACT[tt, :, 0:HALF], half_mat(8 + tt, 0), NT)
    igrad[...] = acc
    last_ready()
    acc = dot(ACT[0, :, HALF:D], half_mat(8, 1), NT)
    for tt in range(1, 4):
        acc = acc + dot(ACT[tt, :, HALF:D], half_mat(8 + tt, 1), NT)
    igrad[...] += acc

    V[...] = jnp.zeros_like(V)
    load_cot.wait()

    @pl.loop(0, 4)
    def _(i):
        rs = ln_rows(i)
        r = XH[rs, :] * g1 + b1 + igrad[rs, :]
        cen = r - jnp.mean(r, axis=1, keepdims=True)
        rstd = lax.rsqrt(jnp.mean(cen * cen, axis=1, keepdims=True) + EPSILON)
        n2 = cen * rstd
        mixed[rs, :] = (n2 * g2 + b2).astype(BF)
        co = cot[rs, :].astype(F32)
        e = co * g2
        gr = rstd * (e - jnp.mean(e, axis=1, keepdims=True) - n2 * jnp.mean(e * n2, axis=1, keepdims=True))
        igrad[rs, :] = gr
        GF[rs, :] = gr.astype(BF)
        V[2:3, :] += jnp.sum(co * n2, axis=0, keepdims=True)
        V[3:4, :] += jnp.sum(co, axis=0, keepdims=True)

    save_mixed.start()

    def sq(r, xx):
        if r < 2:
            return SQ.at[r, xx]
        return W.at[8 + 2 * (r // 2 - 1) + xx, :, :, :, :, pl.ds((r % 2) * HALF, HALF)]

    def pb(r, xx, *rest):
        if r < 4:
            return PB.at[(r, xx) + rest]
        rest = rest + (slice(None),) * (4 - len(rest))
        return W.at[(4 + xx,) + rest + (pl.ds((r % 2) * HALF, HALF),)]

    def pb_all(r, *rest):
        if r < 4:
            return PB.at[(r, slice(None)) + rest]
        rest = rest + (slice(None),) * (4 - len(rest))
        return W.at[(pl.ds(4, 2),) + rest + (pl.ds((r % 2) * HALF, HALF),)]

    def b_sib(r, xx):
        return rc(sq(r, xx), SR.at[SIB_SLOT[r], xx], qs.at[r, xx], qr.at[r, xx], sib)

    ALL = slice(None)

    def b_a(r):
        return rc(pb(r, ox, ALL, ALL, 0), RA.at[r % SLOTS], as_.at[r], ar.at[r], xn)

    def b_b(r):
        return rc(pb_all(r, ALL, oy, 1), RB.at[r % SLOTS], bs.at[r], br.at[r], yn)

    def b_a2(r, k):
        dst = RO.at[r, 0] if k == 0 else RA2.at[r % SLOTS, k - 1]
        return rc(pb(r, x, zz[k], oy, 0), dst, a2s.at[r, k], a2r.at[r, k], yn)

    def b_b2(r, k):
        dst = RO.at[r, 1] if k == 0 else RB2.at[r % SLOTS, k - 1]
        return rc(pb(r, ox, zz[k], y, 1), dst, b2s.at[r, k], b2r.at[r, k], xn)

    def b_z(r, k):
        return rc(pb(r, x, zz[k], y), RZ.at[r, k - 1], rzs.at[r, k - 1], rzr.at[r, k - 1], zn[k])

    def zl(way, tgt, xx, recv=False):
        dst = (RU if way == 0 else RD).at[tgt, xx]
        dev = up_dev if way == 0 else down_dev
        return rc(PB.at[0, xx, tgt], dst, zls.at[way, tgt, xx], zlr.at[way, tgt, xx], dev)

    def zl_sends(way, tgt):
        return z < tgt if way == 0 else z > tgt

    def zl_got(way, tgt):
        return (z > 0) & (z <= tgt) if way == 0 else (z < 3) & (z >= tgt)

    def zl_first():
        for tgt in range(3):
            for xx in range(2):
                pl.when(z == 0)(lambda: zl(0, 3 - tgt, xx).start())
                pl.when(z == 3)(lambda: zl(1, tgt, xx).start())

    def zl_pass(way, at, tgt):
        for xx in range(2):
            @pl.when(z == at)
            def _():
                zl(way, tgt, xx).wait_recv()
                add(PB.at[0, xx, tgt], (RU if way == 0 else RD).at[tgt, xx])
                zl(way, tgt, xx).start()

    def zl_last():
        for way in range(2):
            for tgt in range(4):
                @pl.when((z == tgt) & ((z > 0) if way == 0 else (z < 3)))
                def _():
                    for xx in range(2):
                        zl(way, tgt, xx).wait_recv()
                        add(PB.at[0, xx, tgt], (RU if way == 0 else RD).at[tgt, xx])

    def b0(i):
        src, dst, dev = (
            (PB.at[0, ox, z, :, 0], R0.at[0], xn),
            (PB.at[0, :, z, oy, 1], R0.at[1], yn),
            (PB.at[0, x, z, oy, 0], R0.at[2, 0], yn),
            (PB.at[0, ox, z, y, 1], R0.at[2, 1], xn),
        )[i]
        return rc(src, dst, z0s.at[i], z0r.at[i], dev)

    def xy0_first():
        b0(0).start()
        b0(1).start()

    def xy0_second():
        b0(0).wait_recv()
        add(PB.at[0, x, z, :, 0], R0.at[0])
        b0(2).start()
        b0(1).wait_recv()
        add(PB.at[0, :, z, y, 1], R0.at[1])
        b0(3).start()

    def xy0_last():
        b0(2).wait_recv()
        b0(3).wait_recv()
        tot = PB[0, x, z, y].astype(F32) + R0[2].astype(F32)
        g_down[:, 0:HALF] = tot.reshape(96, HALF)

    def rs0_drain():
        for xx in range(2):
            b_sib(0, xx).wait_send()
        for i in range(4):
            b0(i).wait_send()
        for way in range(2):
            for tgt in range(4):
                for xx in range(2):
                    pl.when(zl_sends(way, tgt))(lambda: zl(way, tgt, xx).wait_send())

    def credit(sem, dev, r):
        if r + SLOTS < PIECES:
            pl.semaphore_signal(sem, inc=1, device_id=dev, device_id_type=pl.DeviceIdType.MESH)

    def need(sem, r):
        if r >= SLOTS + (sem is not c_sib):
            pl.semaphore_wait(sem, 1)

    def part(r, xx, core):
        if r < 4:
            src = ACT if r < 2 else GP
            lhs = GF if r < 2 else FI
            h = r % 2
            return dot(lhs[...], src[2 * xx + core, :, h * HALF : h * HALF + HALF], TN)
        raise ValueError

    def part_attn(m, xx):
        if m < 3:
            return dot(hid[...], ACT[(1, 0, 2)[m], :, xx * HALF : xx * HALF + HALF], TN)
        return dot(GF[...], CTX[:, xx * HALF : xx * HALF + HALF], TN)

    def gen_sib(r):
        need(c_sib, r)
        for xx in range(2):
            if r < 4:
                sq(r, xx)[...] = part(r, xx, oc).astype(BF).reshape(4, 2, 2, 48, HALF)
            else:
                for core in range(2):
                    @pl.when(oc == core)
                    def _():
                        sq(r, xx)[...] = part_attn(2 * core + 5 - r, xx).astype(BF).reshape(4, 2, 2, 48, HALF)
            b_sib(r, xx).start()

    def own_part(r, xx, grad):
        v = grad.reshape(4, 2, 2, 48, HALF) + SR[SIB_SLOT[r], xx].astype(F32)
        pb(r, xx)[...] = v.astype(BF)

    def gen_own(r):
        for xx in range(2):
            b_sib(r, xx).wait_recv()
            if r < 4:
                own_part(r, xx, part(r, xx, c))
            else:
                for core in range(2):
                    @pl.when(c == core)
                    def _():
                        own_part(r, xx, part_attn(2 * core + 5 - r, xx))
        credit(c_sib, sib, r)
        if r == 0:
            zl_first()
            return
        need(c_a, r)
        b_a(r).start()
        need(c_b, r)
        b_b(r).start()

    def add(dst, src):
        dst[...] = (dst[...].astype(F32) + src[...].astype(F32)).astype(BF)

    def st1(r):
        q = r % SLOTS
        b_a(r).wait_recv()
        add(pb(r, x, ALL, ALL, 0), RA.at[q])
        credit(c_a, xn, r)
        need(c_a2, r)
        for k in (2, 3, 1):
            b_a2(r, k).start()
        b_b(r).wait_recv()
        add(pb_all(r, ALL, y, 1), RB.at[q])
        credit(c_b, yn, r)
        need(c_b2, r)
        for k in (2, 3, 1):
            b_b2(r, k).start()

    def st2o(r):
        b_a2(r, 0).start()
        b_b2(r, 0).start()

    def st2(r):
        q = r % SLOTS
        for k in (2, 3, 1):
            b_a2(r, k).wait_recv()
            add(pb(r, x, zz[k], y, 0), RA2.at[q, k - 1])
            b_b2(r, k).wait_recv()
            add(pb(r, x, zz[k], y, 1), RB2.at[q, k - 1])
            b_z(r, k).start()
        credit(c_a2, yn, r)
        credit(c_b2, xn, r)

    def fx(r):
        m = g_attn.at[2 * c + 5 - r]
        return rc(m, m, es.at[r - 1], er.at[r - 1], sib)

    def st3(r):
        tot = pb(r, x, z, y)[...].astype(F32)
        for k in (2, 3, 1):
            b_z(r, k).wait_recv()
            tot = tot + RZ[r, k - 1].astype(F32)
        b_a2(r, 0).wait_recv()
        b_b2(r, 0).wait_recv()
        tot = (tot + RO[r].astype(F32)).reshape(96, HALF)
        h = r % 2
        if r < 2:
            g_down[:, h * HALF : h * HALF + HALF] = tot
        elif r < 4:
            g_up[:, h * HALF : h * HALF + HALF] = tot
        else:
            g_attn[2 * c + 5 - r] = tot
            fx(r).start()

    def rs_drain(r):
        for xx in range(2):
            b_sib(r, xx).wait_send()
        b_a(r).wait_send()
        b_b(r).wait_send()
        for k in range(4):
            b_a2(r, k).wait_send()
            b_b2(r, k).wait_send()
        for k in (1, 2, 3):
            b_z(r, k).wait_send()

    def gact(h):
        ls = slice(h * HALF, h * HALF + HALF)
        for tt in range(4):
            ga = dot(GF[...], half_mat(8 + tt, h), NN)
            gp = (ga * GP[tt, :, ls].astype(F32)).astype(BF)
            GP[tt, :, ls] = gp
            V[4 + tt : 5 + tt, ls] = jnp.sum(gp.astype(F32), axis=0, keepdims=True)

    gen_sib(1)
    gen_sib(0)
    gen_own(1)
    gen_own(0)
    drain(4)
    last_drain()
    gact(0)
    gen_sib(2)
    gact(1)
    zl_pass(1, 2, 0)
    gen_own(2)
    gen_sib(3)
    acc = dot(GP[0], mat(4), NT)
    zl_pass(0, 1, 3)
    for tt in range(1, 4):
        acc = acc + dot(GP[tt], mat(4 + tt), NT)
    st1(1)

    igrad[...] += acc
    gen_own(3)

    zl_pass(1, 1, 0)

    zl_pass(1, 2, 1)
    @pl.loop(0, 4)
    def _(i):
        rs = ln_rows(i)
        gn = igrad[rs, :]
        xh = XH[rs, :]
        e = gn * g1
        gr = RS1[rs, :] * (e - jnp.mean(e, axis=1, keepdims=True) - xh * jnp.mean(e * xh, axis=1, keepdims=True))
        igrad[rs, :] = gr
        GF[rs, :] = gr.astype(BF)
        V[0:1, :] += jnp.sum(gn * xh, axis=0, keepdims=True)
        V[1:2, :] += jnp.sum(gn, axis=0, keepdims=True)

    vc = [
        rc(V, VR.at[0], vs.at[0], vr.at[0], sib),
        rc(V, VR.at[1], vs.at[1], vr.at[1], xn),
        rc(V, VR.at[2], vs.at[2], vr.at[2], yn),
    ] + [rc(V, VR.at[2 + k], vs.at[2 + k], vr.at[2 + k], zn[k]) for k in (1, 2, 3)]

    def v_step(i):
        vc[i].wait()
        V[...] += VR[i]

    vc[0].start()
    FI[...] = dot(GF[...], mat(3), NN).astype(BF)
    v_step(0)
    vc[1].start()

    zl_pass(0, 1, 2)
    def attn_bwd(hp):
        ls = pair_lanes(hp)
        fl = flips(hp)
        kk = jnp.where(fl, KVO[0, :, ls], QKV[1, :, ls])
        vv = jnp.where(fl, KVO[1, :, ls], QKV[2, :, ls])
        q = QKV[0, :, ls]
        do = FI[:, ls]
        dvs, dqs, dks = [], [], []
        for e in range(2):
            dvs.append(dot(AT[2 * hp + e], do, TN))
            for rb in range(2):
                rows = slice(rb * 256, rb * 256 + 256)
                dr = do[rows]
                dp = dot(jnp.where(low_lane if e == 0 else ~low_lane, dr, jnp.zeros_like(dr)), vv, NT)
                af = AT[2 * hp + e, rows, :].astype(F32)
                w = af * dp
                GP[2 + e, rows, 0:ROWS] = (w - af * jnp.sum(w, axis=1, keepdims=True)).astype(BF)
            gs = GP[2 + e, :, 0:ROWS]
            dqs.append(dot(gs, kk, NN))
            dks.append(dot(gs, q, TN))
        ACT[0, :, ls] = (jnp.where(low_lane, dqs[0], dqs[1]) * 0.125).astype(BF)
        GP[0, :, ls] = (jnp.where(low_lane, dks[0], dks[1]) * 0.125).astype(BF)
        GP[1, :, ls] = jnp.where(low_lane, dvs[0], dvs[1]).astype(BF)

    zl_pass(0, 2, 3)
    def dkv(i):
        ls = pl.ds(i * HALF, HALF)
        return rc(GP.at[pl.ds(0, 2), :, ls], DKVR.at[:, :, ls], es.at[2 + 3 * i], er.at[2 + 3 * i], sib)

    @pl.loop(0, 6)
    def backward_pairs(hp):
        attn_bwd(hp)

        pl.when(hp == 0)(lambda: st1(2))
        pl.when(hp == 2)(lambda: st2(1))
        pl.when(hp == 2)(lambda: dkv(0).start())
        pl.when(hp == 5)(lambda: st1(3))
        pl.when(hp == 0)(lambda: st2o(1))
        pl.when(hp == 2)(lambda: st2o(2))
        pl.when(hp == 5)(lambda: st2o(3))

    gen_sib(4)
    dkv(1).start()
    v_step(1)
    st2(2)
    zl_last()
    vc[2].start()
    gen_own(4)
    dkv(0).wait()
    dkv(1).wait()

    def pick(hp):
        ls = pair_lanes(hp)
        fl = flips(hp)
        ACT[1, :, ls] = jnp.where(fl, DKVR[0, :, ls], GP[0, :, ls])
        ACT[2, :, ls] = jnp.where(fl, DKVR[1, :, ls], GP[1, :, ls])

    st2(3)
    pl.loop(0, 6)(pick)

    gen_sib(5)
    v_step(2)
    xy0_first()
    for k in (1, 2, 3):
        vc[2 + k].start()
    acc = dot(ACT[0], mat(1), NT)
    for m in (1, 2):
        acc = acc + dot(ACT[m], mat((1, 0, 2)[m]), NT)
    st1(4)
    igrad[...] += acc
    save_igrad.start()
    gen_own(5)
    st2(4)
    st1(5)
    st3(1)
    st3(3)
    st3(2)
    st2o(5)
    xy0_second()
    st2(5)
    st2o(4)
    st3(4)
    xy0_last()
    save_mixed.wait()
    save_igrad.wait()
    rs0_drain()
    for r in range(1, PIECES):
        rs_drain(r)
    st3(5)
    for k in (1, 2, 3):
        vc[2 + k].wait()
    g_misc[...] = V[...] + VR[3] + VR[4] + VR[5]
    fx(4).wait()
    fx(5).wait()


def finish_kernel(
    mixed, igrad, ga, gu, gd, gm, o_mixed, o_igrad, o_qkv, o_out, o_up, o_bias, o_down, o_norm,
    v_igrad, v_mixed, v_up, v_down, v_ga, v_gm, w_qkv, w_out, w_bias, w_norm, tmp, sem,
):
    copy = pltpu.make_async_copy
    load_small = [copy(gm, v_gm, sem.at[0, 8]), copy(ga, v_ga, sem.at[0, 9])]
    parts = [(igrad, v_igrad, o_igrad, i * 128, 128) for i in range(4)]
    parts += [(mixed, v_mixed, o_mixed, i * 256, 256) for i in range(2)]
    parts += [(gu, v_up, o_up, 0, 96), (gd, v_down, o_down, 0, 96)]
    loads, stores = [], []
    for i, (src, mid, dst, at, n) in enumerate(parts):
        rows = pl.ds(at, n)
        loads.append(copy(src.at[rows], mid.at[rows], sem.at[0, i]))
        stores.append(copy(mid.at[rows], dst.at[rows], sem.at[1, i]))
    for cp in load_small + loads:
        cp.start()
    dd = lax.axis_index("dp")
    t = lax.axis_index("tensor")
    exact = dict(preferred_element_type=F32, precision=lax.Precision.HIGHEST)
    si = lax.broadcasted_iota(jnp.int32, (D, 128), 0)
    sj = lax.broadcasted_iota(jnp.int32, (D, 128), 1)
    norm_pick = jnp.where(si == sj + dd * 96, 1.0, 0.0).astype(F32)
    bias_pick = jnp.where(si[0:128] == sj[0:128] + dd * 16, 1.0, 0.0).astype(F32)
    sub = lax.broadcasted_iota(jnp.int32, (8, D), 0)
    load_small[0].wait()
    norm = lax.dot_general(v_gm[...], norm_pick, NN, **exact)
    w_norm[...] = jnp.sum(jnp.where(sub[:, 0:128] == t, norm, 0.0), axis=0, keepdims=True)[:, 0:96]
    row = jnp.sum(jnp.where(sub == 4 + t, v_gm[...], 0.0), axis=0, keepdims=True)
    for r in range(6):
        tmp[r : r + 1] = row[:, r * 128 : r * 128 + 128]
    w_bias[...] = lax.dot_general(tmp[...], bias_pick, NN, **exact)[0:6, 0:16]
    load_small[1].wait()
    first = jnp.full((96, 192), lax.rem(t, 2), jnp.int32) == 0
    for m in range(4):
        v = jnp.where(first, v_ga[m, :, 0:192], v_ga[m, :, 192:HALF])
        if m < 3:
            w_qkv[(1, 0, 2)[m]] = v
        else:
            w_out[...] = v.T
    small = ((w_norm, o_norm), (w_bias, o_bias), (w_qkv, o_qkv), (w_out, o_out))
    for i, (src, dst) in enumerate(small):
        stores.append(copy(src, dst, sem.at[1, 8 + i]))
        stores[-1].start()
    for load, store in zip(loads, stores):
        load.wait()
        store.start()
    for cp in stores:
        cp.wait()


def scratch():
    vm = pltpu.VMEM
    dma = lambda *s: pltpu.SemaphoreType.DMA(s)
    n = PIECES
    return [
        vm((3, 96, 192), F32), vm((192, 96), F32), vm((96, D), F32), vm((96, D), F32), vm((ROWS, D), F32),
        vm((ROWS, D), BF), vm((ROWS, D), BF), vm((ROWS, D), BF), vm((12, 4, 2, 2, 48, D), BF), vm((4, 96, 256), BF), vm((2, 96, 256), BF), vm((3, ROWS, D), BF), vm((2, ROWS, D), BF),
        vm((12, ROWS, ROWS), BF), vm((ROWS, D), BF), vm((ROWS, D), F32), vm((ROWS, 1), F32), vm((ROWS, D), BF),
        vm((4, ROWS, D), BF), vm((4, ROWS, D), BF), vm((ROWS, D), BF), vm((2, ROWS, D), BF),
        vm((2, 2, 2, 4, 2, 8, 128), F32), vm((2, 8, D), F32), vm((8, D), F32), vm((6, 8, D), F32),
        vm((2, 2, 4, 2, 2, 48, HALF), BF), vm((SLOTS, 2, 4, 2, 2, 48, HALF), BF), vm((4, 2, 4, 2, 2, 48, HALF), BF),
        vm((SLOTS, 4, 2, 48, HALF), BF), vm((SLOTS, 2, 4, 48, HALF), BF), vm((SLOTS, 3, 48, HALF), BF),
        vm((SLOTS, 3, 48, HALF), BF), vm((n, 2, 48, HALF), BF), vm((n, 3, 2, 48, HALF), BF),
        vm((4, 2, 2, 2, 48, HALF), BF), vm((4, 2, 2, 2, 48, HALF), BF), vm((3, 2, 48, HALF), BF),
        dma(n, 3), dma(n, 3), dma(n, 4), dma(n, 4), dma(n, 4), dma(n, 4), dma(n, 2), dma(n, 2), dma(n, 4), dma(n, 4),
        dma(6), dma(6), dma(6), dma(6),
        dma(n, 2), dma(n, 2), dma(n), dma(n), dma(n), dma(n), dma(n, 4), dma(n, 4), dma(n, 4), dma(n, 4), dma(n, 3), dma(n, 3), dma(6), dma(6),
        dma(2, 3, 2), dma(2, 3, 2), dma(7, 2), dma(7, 2), dma(2, 4, 2), dma(2, 4, 2), dma(4), dma(4), dma(8),
        pltpu.SemaphoreType.REGULAR, pltpu.SemaphoreType.REGULAR, pltpu.SemaphoreType.REGULAR,
        pltpu.SemaphoreType.REGULAR, pltpu.SemaphoreType.REGULAR,
    ]


def whole_layer(
    hidden_in, qkv_weight, out_weight, up_weight, up_bias, down_weight, norm_params, cotangent, head_swap, slot_kind
):
    any_ = pl.BlockSpec(memory_space=pl.ANY)
    vmem = pl.BlockSpec(memory_space=pltpu.VMEM)
    smem = pl.BlockSpec(memory_space=pltpu.SMEM)
    sds = jax.ShapeDtypeStruct
    mixed, igrad, ga, gu, gd, gm = pl.pallas_call(
        layer_kernel,
        out_shape=(
            sds((ROWS, D), BF), sds((ROWS, D), F32), sds((4, 96, HALF), F32),
            sds((96, D), F32), sds((96, D), F32), sds((8, D), F32),
        ),
        in_specs=[any_] * 4 + [vmem, any_, vmem, any_] + [smem] * 2,
        out_specs=(any_,) * 2 + (vmem,) * 4,
        scratch_shapes=scratch(),
        compiler_params=pltpu.CompilerParams(
            collective_id=0, has_side_effects=True, vmem_limit_bytes=63 * 2**20
        ),
        name="layer",
    )(
        hidden_in, qkv_weight, out_weight, up_weight, up_bias, down_weight.T, norm_params, cotangent, head_swap, slot_kind
    )
    *outs, bias_grad, down_grad, norm_grad = pl.pallas_call(
        finish_kernel,
        out_shape=(
            sds((ROWS, D), BF), sds((ROWS, D), F32), sds((3, 96, 192), F32), sds((192, 96), F32),
            sds((96, D), F32), sds((6, 16), F32), sds((96, D), F32), sds((1, 96), F32),
        ),
        in_specs=[any_] * 6,
        out_specs=(any_,) * 8,
        scratch_shapes=[
            pltpu.VMEM((ROWS, D), F32), pltpu.VMEM((ROWS, D), BF), pltpu.VMEM((96, D), F32), pltpu.VMEM((96, D), F32),
            pltpu.VMEM((4, 96, HALF), F32), pltpu.VMEM((8, D), F32), pltpu.VMEM((3, 96, 192), F32),
            pltpu.VMEM((192, 96), F32), pltpu.VMEM((6, 16), F32), pltpu.VMEM((1, 96), F32), pltpu.VMEM((8, 128), F32),
            pltpu.SemaphoreType.DMA((2, 12)),
        ],
        compiler_params=pltpu.CompilerParams(vmem_limit_bytes=63 * 2**20),
        name="finish",
    )(mixed, igrad, ga, gu, gd, gm)
    return (*outs, bias_grad, down_grad.T, norm_grad)


def norm_rows(residual, scales, offset):
    center = residual - jnp.mean(residual, axis=-1, keepdims=True)
    spread = jnp.mean(center * center, axis=-1, keepdims=True)
    return center * lax.rsqrt(spread + EPSILON) * scales + offset


def smooth_gate(values):
    return jax.nn.gelu(values, approximate=False)


def arrange(queries, keys_in, values_in, slot_type, local_swaps):
    slot_len, head_count, head_size = queries.shape
    half_len = slot_len // 2
    quarter = half_len // 2
    shape_four = (2, half_len, head_count, head_size)
    query_half = queries.reshape(shape_four)
    key_half = keys_in.reshape(shape_four)
    value_half = values_in.reshape(shape_four)
    flipped = (local_swaps * slot_type == 1)[None, None, :, None]
    key_pick = jnp.where(flipped, key_half[::-1], key_half)
    value_pick = jnp.where(flipped, value_half[::-1], value_half)
    blocks = jnp.arange(half_len, dtype=jnp.int32) // quarter
    matching = (
        jnp.bitwise_xor(blocks[None, :, None], local_swaps[:, None, None]) == blocks[None, None, :]
    )
    allowed = jnp.logical_or(slot_type == 1, matching)
    return (query_half, key_pick, value_pick, allowed, flipped)


def masked_scores(query_half, key_pick, allowed):
    scale = 1.0 / math.sqrt(query_half.shape[-1])
    scores = (
        jnp.einsum("jqhd,jkhd->jhqk", query_half, key_pick, preferred_element_type=jnp.float32)
        * scale
    )
    return jnp.where(allowed[None], scores, NEGATIVE)


def slot_forward(inputs, local_swaps):
    queries, keys_in, values_in, slot_type = inputs
    query_half, key_pick, value_pick, allowed, flipped = arrange(
        queries, keys_in, values_in, slot_type, local_swaps
    )
    scores = masked_scores(query_half, key_pick, allowed)
    largest = jnp.max(scores, axis=-1, keepdims=True)
    powers = jnp.exp(scores - largest)
    totals = jnp.sum(powers, axis=-1, keepdims=True)
    attention = (powers / totals).astype(jnp.bfloat16)
    context = jnp.einsum(
        "jhqk,jkhd->jqhd", attention, value_pick, preferred_element_type=jnp.float32
    )
    return (context.astype(jnp.bfloat16).reshape(queries.shape[0], -1), largest + jnp.log(totals))


def slot_backward(inputs, local_swaps):
    queries, keys_in, values_in, slot_type, log_totals, grad_out = inputs
    slot_len, head_count, head_size = queries.shape
    scale = 1.0 / math.sqrt(head_size)
    query_half, key_pick, value_pick, allowed, flipped = arrange(
        queries, keys_in, values_in, slot_type, local_swaps
    )
    attention = jnp.exp(masked_scores(query_half, key_pick, allowed) - log_totals)
    grad_half = grad_out.reshape(query_half.shape)
    grad_vpick = jnp.einsum(
        "jhqk,jqhd->jkhd",
        attention.astype(jnp.bfloat16),
        grad_half,
        preferred_element_type=jnp.float32,
    ).astype(jnp.bfloat16)
    grad_attention = jnp.einsum(
        "jqhd,jkhd->jhqk", grad_half, value_pick, preferred_element_type=jnp.float32
    )
    row_dots = jnp.sum(attention * grad_attention, axis=-1, keepdims=True)
    grad_scores = (attention * (grad_attention - row_dots)).astype(jnp.bfloat16)
    grad_query = (
        jnp.einsum("jhqk,jkhd->jqhd", grad_scores, key_pick, preferred_element_type=jnp.float32)
        * scale
    ).astype(jnp.bfloat16)
    grad_kpick = (
        jnp.einsum("jhqk,jqhd->jkhd", grad_scores, query_half, preferred_element_type=jnp.float32)
        * scale
    ).astype(jnp.bfloat16)
    grad_key = jnp.where(flipped, grad_kpick[::-1], grad_kpick)
    grad_value = jnp.where(flipped, grad_vpick[::-1], grad_vpick)
    return (
        grad_query.reshape(slot_len, -1),
        grad_key.reshape(slot_len, -1),
        grad_value.reshape(slot_len, -1),
    )


def per_device(
    hidden_in,
    qkv_weight,
    out_weight,
    up_weight,
    up_bias,
    down_weight,
    norm_params,
    cotangent,
    head_swap,
    slot_kind,
):
    tensor_count = lax.axis_size("tensor")
    tensor_rank = lax.axis_index("tensor")
    heads_here = head_swap.shape[0] // tensor_count
    local_swaps = lax.dynamic_slice_in_dim(head_swap, tensor_rank * heads_here, heads_here)
    qkv_low = qkv_weight.astype(jnp.bfloat16)
    out_low = out_weight.astype(jnp.bfloat16)
    norm_low = norm_params.astype(jnp.bfloat16)
    up_low = up_weight.astype(jnp.bfloat16)
    bias_low = up_bias.astype(jnp.bfloat16)
    down_low = down_weight.astype(jnp.bfloat16)
    qkv_full, out_full, norm_full = (
        lax.all_gather(qkv_low, "dp", axis=1, tiled=True),
        lax.all_gather(out_low, "dp", axis=1, tiled=True),
        lax.all_gather(norm_low, "dp", axis=1, tiled=True),
    )
    norm_gain = norm_full.astype(jnp.float32)
    full_in = lax.all_gather(hidden_in, "tensor", axis=0, tiled=True)
    group_rows = full_in.shape[0]
    local_width = qkv_full.shape[2]
    head_size = local_width // heads_here
    slot_count = group_rows // LONG_LEN

    def by_slot(rows):
        return rows.reshape(slot_count, LONG_LEN, heads_here, head_size)

    projected = jnp.einsum(
        "td,cde->cte", full_in, qkv_full, preferred_element_type=jnp.float32
    ).astype(jnp.bfloat16)
    context, log_totals = lax.map(
        partial(slot_forward, local_swaps=local_swaps),
        (by_slot(projected[0]), by_slot(projected[1]), by_slot(projected[2]), slot_kind),
    )
    context = context.reshape(group_rows, local_width)
    rows = context
    attn_share = lax.psum_scatter(
        jnp.dot(rows, out_full, preferred_element_type=jnp.float32).astype(jnp.bfloat16),
        "tensor",
        scatter_dimension=0,
        tiled=True,
    ).astype(jnp.float32)
    resid_one = hidden_in.astype(jnp.float32) + attn_share
    normed_one, norm_one_back = jax.vjp(norm_rows, resid_one, norm_gain[0], norm_gain[1])
    up_full, bias_full, down_full = (
        lax.all_gather(up_low, "dp", axis=0, tiled=True),
        lax.all_gather(bias_low, "dp", axis=1, tiled=True),
        lax.all_gather(down_low, "dp", axis=1, tiled=True),
    )
    ffn_in = lax.all_gather(normed_one.astype(jnp.bfloat16), "tensor", axis=0, tiled=True)
    pre = jnp.dot(ffn_in, up_full, preferred_element_type=jnp.float32) + bias_full.reshape(
        -1
    ).astype(jnp.float32)
    act_value, gate_back = jax.vjp(smooth_gate, pre)
    act = act_value.astype(jnp.bfloat16)
    rows = act
    ffn_share = lax.psum_scatter(
        jnp.dot(rows, down_full, preferred_element_type=jnp.float32).astype(jnp.bfloat16),
        "tensor",
        scatter_dimension=0,
        tiled=True,
    ).astype(jnp.float32)
    normed_two, norm_two_back = jax.vjp(
        norm_rows, normed_one + ffn_share, norm_gain[2], norm_gain[3]
    )
    mixed = normed_two.astype(jnp.bfloat16)
    grad_resid_two, grad_gain_two, grad_bias_two = norm_two_back(cotangent.astype(jnp.float32))
    grad_ffn = lax.all_gather(grad_resid_two.astype(jnp.bfloat16), "tensor", axis=0, tiled=True)
    grad_down = jnp.einsum("tf,td->fd", act, grad_ffn, preferred_element_type=jnp.float32)
    grad_act = jnp.einsum("td,fd->tf", grad_ffn, down_full, preferred_element_type=jnp.float32)
    grad_pre = gate_back(grad_act)[0].astype(jnp.bfloat16)
    grad_up = jnp.einsum("td,tf->df", ffn_in, grad_pre, preferred_element_type=jnp.float32)
    grad_bias = jnp.sum(grad_pre.astype(jnp.float32), axis=0).reshape(bias_full.shape)
    rows = grad_pre
    grad_normed_one = grad_resid_two + lax.psum_scatter(
        jnp.einsum("tf,df->td", rows, up_full, preferred_element_type=jnp.float32).astype(
            jnp.bfloat16
        ),
        "tensor",
        scatter_dimension=0,
        tiled=True,
    ).astype(jnp.float32)
    grad_resid_one, grad_gain_one, grad_bias_one = norm_one_back(grad_normed_one)
    grad_attn = lax.all_gather(grad_resid_one.astype(jnp.bfloat16), "tensor", axis=0, tiled=True)
    grad_out = jnp.einsum("tw,td->wd", context, grad_attn, preferred_element_type=jnp.float32)
    grad_context = jnp.einsum(
        "td,wd->tw", grad_attn, out_full, preferred_element_type=jnp.float32
    ).astype(jnp.bfloat16)
    grad_query, grad_key, grad_value = lax.map(
        partial(slot_backward, local_swaps=local_swaps),
        (
            by_slot(projected[0]),
            by_slot(projected[1]),
            by_slot(projected[2]),
            slot_kind,
            log_totals,
            grad_context.reshape(slot_count, LONG_LEN, local_width),
        ),
    )
    grad_proj = jnp.stack([grad_query, grad_key, grad_value]).reshape(3, group_rows, local_width)
    grad_qkv = jnp.einsum("td,cte->cde", full_in, grad_proj, preferred_element_type=jnp.float32)
    grad_in_part = jnp.einsum(
        "cte,cde->td", grad_proj, qkv_full, preferred_element_type=jnp.float32
    )
    norm_part = jnp.stack([grad_gain_one, grad_bias_one, grad_gain_two, grad_bias_two])
    grad_in_share, norm_row = (
        lax.psum_scatter(
            grad_in_part.astype(jnp.bfloat16), "tensor", scatter_dimension=0, tiled=True
        ).astype(jnp.float32),
        lax.psum_scatter(
            norm_part.astype(jnp.bfloat16), "tensor", scatter_dimension=0, tiled=True
        ).astype(jnp.float32),
    )
    input_grad = grad_resid_one + grad_in_share
    qkv_grad, out_grad, up_grad, up_bias_grad, down_grad, norm_grad = (
        lax.psum_scatter(grad_qkv, "dp", scatter_dimension=1, tiled=True),
        lax.psum_scatter(grad_out, "dp", scatter_dimension=1, tiled=True),
        lax.psum_scatter(grad_up, "dp", scatter_dimension=0, tiled=True),
        lax.psum_scatter(grad_bias, "dp", scatter_dimension=1, tiled=True),
        lax.psum_scatter(grad_down, "dp", scatter_dimension=1, tiled=True),
        lax.psum_scatter(norm_row, "dp", scatter_dimension=1, tiled=True),
    )
    return (mixed, input_grad, qkv_grad, out_grad, up_grad, up_bias_grad, down_grad, norm_grad)


def solution(mesh):
    placed = (
        P(("dp", "tensor"), None),
        P(None, "dp", "tensor"),
        P("tensor", "dp"),
        P("dp", "tensor"),
        P("tensor", "dp"),
        P("tensor", "dp"),
        P(None, "dp"),
        P(("dp", "tensor"), None),
        P(),
        P("dp"),
    )
    planned = mesh.shape["dp"] == 8 and mesh.shape["tensor"] == 4
    return jax.shard_map(
        whole_layer if planned else per_device,
        mesh=mesh,
        in_specs=placed,
        out_specs=(
            P(("dp", "tensor"), None),
            P(("dp", "tensor"), None),
            P(None, "dp", "tensor"),
            P("tensor", "dp"),
            P("dp", "tensor"),
            P("tensor", "dp"),
            P("tensor", "dp"),
            P("tensor", "dp"),
        ),
        check_vma=False,
    )
```
